128 devices in a mesh: seq: 32 (over x, z, core), rows: 4 (over y).
Axes of the slice: x: 4, y: 4, z: 4, core: 2. Of those that a mesh axis runs over, the one named last changes fastest.
Arguments:
- tokens: bfloat16 [8, 2048, 2048], P('rows', 'seq'), may hold values from -6 to 6
- seg_starts: int32 [8, 4], P('rows'), may hold values from 0 to 2048, as said below
- gain_one: bfloat16 [2048], P(('seq', 'rows')), may hold values from 0.5 to 1.5
- gain_two: bfloat16 [2048], P(('seq', 'rows')), may hold values from 0.5 to 1.5
- conv_weight: bfloat16 [4, 2560], P(None, ('seq', 'rows')), may hold values from -3 to 3
- conv_bias: bfloat16 [2560], P(('seq', 'rows')), may hold values from -3 to 3
- rate_weight: bfloat16 [2560, 160], P(('seq', 'rows')), may hold values from -0.5 to 0.5
- input_weight: bfloat16 [2560, 160], P(('seq', 'rows')), may hold values from -0.5 to 0.5
- rate_bias: bfloat16 [2560], P(('seq', 'rows')), may hold values from -4 to 4
- input_bias: bfloat16 [2560], P(('seq', 'rows')), may hold values from -4 to 4
- decay_param: bfloat16 [2560], P(('seq', 'rows')), may hold values from 4 to 12
- proj_out: bfloat16 [2048, 2560], P(('seq', 'rows')), may hold values from -0.125 to 0.125
- proj_x: bfloat16 [2048, 2560], P(('seq', 'rows')), may hold values from -0.125 to 0.125
- proj_y: bfloat16 [2048, 2560], P(('seq', 'rows')), may hold values from -0.125 to 0.125
- ffn_gate: bfloat16 [2048, 6144], P(('seq', 'rows')), may hold values from -0.125 to 0.125
- ffn_up: bfloat16 [2048, 6144], P(('seq', 'rows')), may hold values from -0.125 to 0.125
- ffn_down: bfloat16 [2048, 6144], P(('seq', 'rows')), may hold values from -0.078125 to 0.078125
- cotangent: bfloat16 [8, 2048, 2048], P('rows', 'seq'), may hold values from -6 to 6
Outputs:
- output: bfloat16 [8, 2048, 2048], P('rows', 'seq')
- grad_tokens: bfloat16 [8, 2048, 2048], P('rows', 'seq')
- grad_gain_one: float32 [2048], P(('seq', 'rows'))
- grad_gain_two: float32 [2048], P(('seq', 'rows'))
- grad_conv_weight: float32 [4, 2560], P(None, ('seq', 'rows'))
- grad_conv_bias: float32 [2560], P(('seq', 'rows'))
- grad_rate_weight: float32 [2560, 160], P(('seq', 'rows'))
- grad_input_weight: float32 [2560, 160], P(('seq', 'rows'))
- grad_rate_bias: float32 [2560], P(('seq', 'rows'))
- grad_input_bias: float32 [2560], P(('seq', 'rows'))
- grad_decay_param: float32 [2560], P(('seq', 'rows'))
- grad_proj_out: float32 [2048, 2560], P(('seq', 'rows'))
- grad_proj_x: float32 [2048, 2560], P(('seq', 'rows'))
- grad_proj_y: float32 [2048, 2560], P(('seq', 'rows'))
- grad_ffn_gate: float32 [2048, 6144], P(('seq', 'rows'))
- grad_ffn_up: float32 [2048, 6144], P(('seq', 'rows'))
- grad_ffn_down: float32 [2048, 6144], P(('seq', 'rows'))
The draws below stay inside these ranges and needn't reach their ends.
Inputs may be any that keep to these rules, and one draw needn't show every extreme that they name: `seg_starts`: in each row the entries rise and the first is 0; an entry equal to 2048 marks no document. In every aligned group of 2 rows exactly one row holds a single document over the whole row; the other rows hold 4 documents.
All inputs are finite; a program needn't handle non-finite values.
Results may differ from the reference program's by a relative error of at most 0.017.
Values may be sent and summed in bfloat16 or wider, within the bound.
A program may use at most 256 MiB of HBM per device.

```python
import jax
import jax.numpy as jnp
from jax import lax

D = 2048
R = 2560
FF = 6144
H = 16
HS = 160
CW = 4
LEN = 2048
DOCS = 4
SLOT_DEV = 2
SLOTS = 8


def draw_seg_starts(key, part):
    key = jax.random.fold_in(key, 11)
    pick_key, jitter_key = jax.random.split(key)
    groups = SLOTS // SLOT_DEV
    chosen = jax.random.randint(pick_key, (groups,), 0, SLOT_DEV)
    slot_ids = jnp.arange(SLOTS, dtype=jnp.int32)
    single = slot_ids % SLOT_DEV == jnp.repeat(chosen, SLOT_DEV)
    spread = LEN // 16
    jitter = jax.random.randint(jitter_key, (SLOTS, DOCS), -spread, spread + 1)
    columns = jnp.arange(DOCS, dtype=jnp.int32)
    starts = columns[None, :] * (LEN // DOCS) + jitter
    starts = jnp.where(columns[None, :] == 0, 0, starts)
    starts = jnp.where(single[:, None] & (columns[None, :] > 0), LEN, starts)
    return starts.astype(jnp.int32)


def raised(entries, key, source, target, blocks, factor):
    owner, partner = [(jnp.arange(entries.shape[axis_at]) // (entries.shape[axis_at] // blocks)).reshape([-1 if axis == axis_at else 1 for axis in range(entries.ndim)]) for axis_at in (source, target)]
    chosen = jax.random.permutation(key, blocks)[partner]
    strong = (owner == chosen) | (owner == (partner + blocks // 2) % blocks)
    return jnp.where(strong, factor * entries, entries)


def block_scale(key, dims, cuts, least, high):
    level = 1.0
    for position, blocks in cuts:
        draws = jax.random.uniform(jax.random.fold_in(jax.random.fold_in(key, 6), position), (blocks,), jnp.float32, least / len(cuts), high / len(cuts))
        level = level * jnp.repeat(jnp.exp(draws), dims[position] // blocks).reshape((-1,) + (1,) * (len(dims) - 1 - position))
    return level


def bell_draw(own_key, extent, scale, most, shards=(), held_as=jnp.bfloat16):
    drawn = scale * jax.random.normal(own_key, extent, jnp.float32)
    if shards:
        drawn = drawn * block_scale(own_key, extent, shards, -0.22, 0.18)
    return jnp.clip(drawn, -most, most).astype(held_as)


def bell_draw_with(key, dims, width, limit, cuts, heavy, held_as=jnp.bfloat16):
    values = width * jax.random.normal(key, dims, jnp.float32)
    if cuts:
        values = values * block_scale(key, dims, cuts, -0.22, 0.18)
    return jnp.clip(raised(values, jax.random.fold_in(key, 3), *heavy), -limit, limit).astype(held_as)


def setup_inputs(seed: int = 0) -> dict:
    splits = jax.random.split(jax.random.key(seed), 19)
    tokens = bell_draw(splits[0], (SLOTS, LEN, D), 1.0, 6.0, ((0, 4), (1, 32)))
    seg_starts = draw_seg_starts(jax.random.fold_in(splits[18], 71), 0)
    gain_one = jnp.clip(1.0 + 0.1 * jax.random.normal(splits[2], (D,), jnp.float32), 0.5, 1.5).astype(jnp.bfloat16)
    gain_two = jnp.clip(1.0 + 0.1 * jax.random.normal(splits[3], (D,), jnp.float32), 0.5, 1.5).astype(jnp.bfloat16)
    conv_weight = bell_draw(splits[4], (CW, R), 0.5, 3.0, ((1, 128),))
    conv_bias = bell_draw(splits[5], (R,), 0.5, 3.0, ((0, 128),))
    rate_weight = bell_draw(splits[6], (R, HS), HS ** -0.5, 0.5, ((0, 128),))
    input_weight = bell_draw(splits[7], (R, HS), HS ** -0.5, 0.5, ((0, 128),))
    rate_bias = bell_draw(splits[8], (R,), 1.0, 4.0, ((0, 128),))
    input_bias = bell_draw(splits[9], (R,), 1.0, 4.0, ((0, 128),))
    decay_param = jnp.clip(4.0 + 8.0 * jax.random.uniform(splits[10], (R,), jnp.float32) ** block_scale(splits[10], (R,), ((0, 128),), -0.2, 0.2), 4.0, 12.0).astype(jnp.bfloat16)
    proj_out = bell_draw(splits[11], (D, R), R ** -0.5, 0.125, ((0, 128),))
    proj_x = bell_draw(splits[12], (D, R), D ** -0.5, 0.125, ((0, 128),))
    proj_y = bell_draw(splits[13], (D, R), D ** -0.5, 0.125, ((0, 128),))
    ffn_gate = bell_draw(splits[14], (D, FF), D ** -0.5, 0.125, ((0, 128),))
    ffn_up = bell_draw(splits[15], (D, FF), D ** -0.5, 0.125, ((0, 128),))
    ffn_down = bell_draw(splits[16], (D, FF), FF ** -0.5, 0.078125, ((0, 128),))
    cotangent = bell_draw_with(splits[17], (SLOTS, LEN, D), 1.0, 6.0, ((0, 4), (1, 32)), (1, 2, 32, 2.75))
    return dict(tokens=tokens, seg_starts=seg_starts, gain_one=gain_one, gain_two=gain_two, conv_weight=conv_weight, conv_bias=conv_bias, rate_weight=rate_weight, input_weight=input_weight, rate_bias=rate_bias, input_bias=input_bias, decay_param=decay_param, proj_out=proj_out, proj_x=proj_x, proj_y=proj_y, ffn_gate=ffn_gate, ffn_up=ffn_up, ffn_down=ffn_down, cotangent=cotangent)


EPSILON = 1e-06
FLOOR_VALUE = 0.001
PRECISION = lax.Precision.HIGHEST

@jax.custom_vjp
def low(v):
    return lax.optimization_barrier(v.astype(jnp.bfloat16)).astype(jnp.float32)

@jax.custom_vjp
def low_back(v):
    return v

def low_keep(v):
    return (low(v), None)

def low_pass(kept, grad):
    return (grad,)

def back_keep(v):
    return (v, None)

def back_low(kept, grad):
    return (low(grad),)
low.defvjp(low_keep, low_pass)
low_back.defvjp(back_keep, back_low)

def rms_norm(values):
    return values * lax.rsqrt(lax.optimization_barrier(jnp.mean(values * values, axis=-1, keepdims=True)) + EPSILON)

def gelu_tanh(values):
    return jax.nn.gelu(values, approximate=True)

def combine(earlier, latter):
    return (earlier[0] * latter[0], latter[0] * earlier[1] + latter[1])

def decay_terms(conv_out, rate_pre, input_pre, rate_bias, input_bias, decay_param, resets):
    rate_gate = jax.nn.sigmoid(rate_pre + rate_bias)
    input_gate = jax.nn.sigmoid(input_pre + input_bias)
    log_decay = -8.0 * rate_gate * jax.nn.softplus(-decay_param)
    keep_mask = 1.0 - resets
    factor = jnp.exp(log_decay) * keep_mask
    scale_term = jnp.where(resets > 0.5, 1.0, jnp.sqrt(jnp.maximum(-jnp.expm1(2.0 * log_decay), FLOOR_VALUE)))
    return (factor, scale_term * (input_gate * conv_out))

def matmul(left, right):
    return jnp.dot(left, right, precision=PRECISION)

def contract_last(left, right):
    return lax.dot_general(left, right, (((1,), (1,)), ((), ())), precision=PRECISION)

def slot_forward(weights, row_values, starts):
    gain_one, gain_two, conv_weight, conv_bias, rate_weight, input_weight, rate_bias, input_bias, decay_param, proj_out, proj_x, proj_y, ffn_gate, ffn_up, ffn_down = weights
    positions = jnp.arange(LEN, dtype=jnp.int32)
    current = lax.optimization_barrier(jnp.sum((starts[None, :] <= positions[:, None]).astype(jnp.int32), axis=1))
    resets = jnp.any(starts[None, :] == positions[:, None], axis=1).astype(jnp.float32)[:, None]
    scaled_one = low(rms_norm(row_values) * gain_one)
    conv_in = low(low_back(matmul(scaled_one, proj_x)))
    pre_y = low_back(matmul(scaled_one, proj_y))
    padded = jnp.concatenate([jnp.zeros((CW - 1, R), jnp.float32), conv_in], axis=0)
    conv_out = conv_bias
    for tap_index in range(CW):
        earlier_doc = jnp.concatenate([jnp.full((tap_index,), -1, jnp.int32), current[:LEN - tap_index]])
        validity = (earlier_doc == current).astype(jnp.float32)[:, None]
        offset = CW - 1 - tap_index
        conv_out = conv_out + conv_weight[tap_index] * validity * padded[offset:offset + LEN]
    conv_low = low(conv_out).reshape(LEN, H, HS)
    rate_pre = low_back(jnp.einsum('thi,hij->thj', conv_low, rate_weight.reshape(H, HS, HS), precision=PRECISION).reshape(LEN, R))
    input_pre = low_back(jnp.einsum('thi,hij->thj', conv_low, input_weight.reshape(H, HS, HS), precision=PRECISION).reshape(LEN, R))
    factor, drive_term = decay_terms(conv_out, rate_pre, input_pre, rate_bias, input_bias, decay_param, resets)
    states = lax.associative_scan(combine, (factor, drive_term), axis=0)[1]
    mixed_low = low(states * gelu_tanh(pre_y))
    residual = row_values + low_back(contract_last(mixed_low, proj_out))
    scaled_two = low(rms_norm(residual) * gain_two)
    gate_pre = low_back(matmul(scaled_two, ffn_gate))
    up_pre = low_back(matmul(scaled_two, ffn_up))
    hidden_low = low(gelu_tanh(gate_pre) * up_pre)
    return residual + low_back(contract_last(hidden_low, ffn_down))

def reference(tokens, seg_starts, gain_one, gain_two, conv_weight, conv_bias, rate_weight, input_weight, rate_bias, input_bias, decay_param, proj_out, proj_x, proj_y, ffn_gate, ffn_up, ffn_down, cotangent):
    weights = tuple((value.astype(jnp.float32) for value in (gain_one, gain_two, conv_weight, conv_bias, rate_weight, input_weight, rate_bias, input_bias, decay_param, proj_out, proj_x, proj_y, ffn_gate, ffn_up, ffn_down)))
    row_values = tokens.astype(jnp.float32)

    def run_slots(params, inputs):

        def slot_step(slot_pair):
            return slot_forward(params, slot_pair[0], slot_pair[1])
        return lax.map(jax.checkpoint(slot_step), (inputs, seg_starts))
    result, pullback = jax.vjp(run_slots, weights, row_values)
    gradients, grad_rows = pullback(cotangent.astype(jnp.float32))
    return (result.astype(jnp.bfloat16), grad_rows.astype(jnp.bfloat16), gradients[0], gradients[1], gradients[2], gradients[3], gradients[4], gradients[5], gradients[6], gradients[7], gradients[8], gradients[9], gradients[10], gradients[11], gradients[12], gradients[13], gradients[14])
```

```python
import jax
import jax.numpy as jnp
from jax import lax
from jax.experimental import pallas as pl
from jax.experimental.pallas import tpu as pltpu
from jax.sharding import PartitionSpec as P

BF, F32 = jnp.bfloat16, jnp.float32
MESH = pl.DeviceIdType.MESH
EPSILON = 1e-06
FLOOR_VALUE = 0.001
HID = 768
CH = 320
WIDE = 384
PK = 1024
FK = 2304
FG = 1536
TOK = 2176
SMALL = 32


def dot(left, right):
    return jnp.dot(left, right, preferred_element_type=F32)


def dot_last(left, right):
    return lax.dot_general(left, right, (((1,), (1,)), ((), ())), preferred_element_type=F32)


def dot_first(left, right):
    return lax.dot_general(left, right, (((0,), (0,)), ((), ())), preferred_element_type=F32)


def gelu(v):
    return 0.5 * v * (1.0 + jnp.tanh(0.7978845608028654 * (v + 0.044715 * (v * v * v))))


def gelu_and_slope(v):
    square = v * v
    t = jnp.tanh(0.7978845608028654 * v * (1.0 + 0.044715 * square))
    half = 0.5 * (1.0 + t)
    slope = half + 0.5 * v * (1.0 - t * t) * (0.7978845608028654 * (1.0 + 0.134145 * square))
    return v * half, slope


def turn(v, d):
    return lax.rem(v + (d % 4), 4)


class Place:
    def __init__(self):
        s, self.y = lax.axis_index("seq"), lax.axis_index("rows")
        self.x, self.z, self.c = lax.div(s, 8), lax.rem(lax.div(s, 2), 4), lax.rem(s, 2)
        self.plane = self.x * 4 + self.z
        self.part = self.y * 2 + self.c

    def at(self, x=None, z=None, c=None, y=None):
        x = self.x if x is None else x
        z = self.z if z is None else z
        c = self.c if c is None else c
        return (x * 8 + z * 2 + c, self.y if y is None else y)

    def sibling(self):
        return self.at(c=1 - self.c)

    def column(self, d):
        return turn(self.y, d // 2), (self.c + d % 2) % 2 if d % 2 == 0 else 1 - self.c

    def flat(self, d):
        p = lax.rem(self.plane + (d % 16), 16)
        return self.at(x=lax.div(p, 4), z=lax.rem(p, 4))


class Net:
    def __init__(self, send, recv, local):
        self.send, self.recv, self.near = send, recv, local
        self.names, self.sent, self.kept = {}, [], []

    def slot(self, name):
        assert len(self.names) < self.recv.shape[0] and len(self.sent) <= self.send.shape[0]
        return self.names.setdefault(name, len(self.names))

    def go(self, src, dst, to, name):
        copy = pltpu.make_async_remote_copy(
            src_ref=src,
            dst_ref=dst,
            send_sem=self.send.at[len(self.sent)],
            recv_sem=self.recv.at[self.slot(name)],
            device_id=to,
            device_id_type=MESH,
        )
        copy.start()
        self.sent.append(copy)
        return copy

    def many(self, copies, pieces):
        waits = []
        for src, dst, to, name in copies:
            waits.append(
                pltpu.make_async_remote_copy(
                    src_ref=src,
                    dst_ref=dst,
                    send_sem=self.send.at[len(self.sent)],
                    recv_sem=self.recv.at[self.slot(name)],
                    device_id=to,
                    device_id_type=MESH,
                )
            )
            self.sent.append(waits[-1])
        first = len(self.sent) - len(copies)
        for piece in range(pieces):
            for i, (src, dst, to, name) in enumerate(copies):
                rows = src.shape[-2] // pieces
                at = (slice(None),) * (len(src.shape) - 2) + (pl.ds(rows * piece, rows),)
                pltpu.make_async_remote_copy(
                    src_ref=src.at[at],
                    dst_ref=dst.at[at],
                    send_sem=self.send.at[first + i],
                    recv_sem=self.recv.at[self.slot(name)],
                    device_id=to,
                    device_id_type=MESH,
                ).start()
        return waits

    def take(self, dst, name, to):
        pltpu.make_async_remote_copy(
            src_ref=dst,
            dst_ref=dst,
            send_sem=self.send.at[0],
            recv_sem=self.recv.at[self.slot(name)],
            device_id=to,
            device_id_type=MESH,
        ).wait_recv()

    def local(self, src, dst):
        assert len(self.kept) < self.near.shape[0]
        copy = pltpu.make_async_copy(src, dst, self.near.at[len(self.kept)])
        copy.start()
        self.kept.append(copy)
        return copy

    def drain(self, but=()):
        for copy in self.sent:
            if all(copy is not other for other in but):
                copy.wait_send()


def greet(peers, extra=0):
    barrier = pltpu.get_barrier_semaphore()
    for peer in peers:
        pl.semaphore_signal(barrier, inc=1, device_id=peer, device_id_type=MESH)
    return barrier


def add_into(out, terms):
    rows = out.shape[-2]
    lead = [()]
    for extent in out.shape[:-2]:
        lead = [one + (i,) for one in lead for i in range(extent)]
    for one in lead:

        def step(i, _):
            at = pl.ds(pl.multiple_of(i * 16, 16), 16)
            if len(terms) == 2:
                total = terms[0][one + (at, slice(None))] + terms[1][one + (at, slice(None))]
            else:
                total = terms[0][one + (at, slice(None))].astype(F32)
                for term in terms[1:]:
                    total = total + term[one + (at, slice(None))].astype(F32)
            out[one + (at, slice(None))] = total.astype(out.dtype)
            return 0

        lax.fori_loop(0, rows // 16, step, 0, unroll=2)


class GatherColumn:
    def __init__(self, net, me, g, tag):
        self.net, self.me, self.g, self.tag = net, me, g, tag
        self.sent = []

    def go(self, *what):
        self.sent.append(self.net.go(*what))

    def block(self, dy, k, c):
        return self.g.at[2 * turn(self.me.y, dy) + k, c]

    def start(self, src):
        me, net, tag = self.me, self.net, self.tag
        copies = []
        for k in range(2):
            copies.append((src.at[k], self.block(0, k, me.c), me.at(y=turn(me.y, 1)), (tag, "ring", -1, k)))
            copies.append((src.at[1 - k], self.block(0, 1 - k, me.c), me.at(y=turn(me.y, -1)), (tag, "ring", 1, 1 - k)))
            copies.append((src.at[k], self.block(0, k, me.c), me.sibling(), (tag, "sib", 0, k)))
        for group in (copies[:3], copies[3:]):
            self.sent += net.many(group, 1)
        self.own = net.local(src, self.g.at[pl.ds(2 * me.y, 2), me.c])

    def relay(self, halves=(0, 1)):
        me, net, tag = self.me, self.net, self.tag
        for first in halves:
            copies = []
            for dy in (-1, 1):
                k = first if dy == -1 else 1 - first
                here = self.block(dy, k, me.c)
                net.take(here, (tag, "ring", dy, k), me.sibling())
                if first == 0:
                    copies.append((here, here, me.at(y=turn(me.y, -dy)), (tag, "far", k)))
                copies.append((here, here, me.sibling(), (tag, "sib", dy, k)))
            self.sent += net.many(copies, 1)

    def last(self):
        me, net, tag = self.me, self.net, self.tag
        for k in range(2):
            here = self.block(2, k, me.c)
            net.take(here, (tag, "far", k), me.sibling())
            self.go(here, here, me.sibling(), (tag, "sib", 2, k))

    def whole(self, dy):
        me, net, tag = self.me, self.net, self.tag
        if dy == 0:
            self.own.wait()
        for k in range(2):
            net.take(self.block(dy, k, 1 - me.c), (tag, "sib", dy, k), me.sibling())

    def finish(self):
        for dy in (0, -1, 1, 2):
            self.whole(dy)


class ReduceColumn:
    def __init__(self, net, me, part, pair, far, side, tag):
        self.net, self.me, self.tag = net, me, tag
        self.part, self.pair, self.far, self.side = part, pair, far, side
        self.sent = []

    def go(self, *what):
        self.sent.append(self.net.go(*what))

    def drain(self):
        for copy in self.sent:
            copy.wait_send()

    def mine(self, dy):
        return self.part.at[pl.ds(2 * turn(self.me.y, dy), 2), self.me.c]

    def one(self, dy, k):
        return self.part.at[2 * turn(self.me.y, dy) + k, self.me.c]

    def send_pair(self, dy):
        me = self.me
        src = self.part.at[pl.ds(2 * turn(me.y, dy), 2), 1 - me.c]
        self.go(src, self.pair.at[dy % 4], me.sibling(), (self.tag, "pair", dy % 4))

    def take_pair(self, dy):
        me, net, tag = self.me, self.net, self.tag
        net.take(self.pair.at[dy % 4], (tag, "pair", dy % 4), me.sibling())
        add_into(self.mine(dy), (self.mine(dy), self.pair.at[dy % 4]))
        above, below = me.at(y=turn(me.y, 1)), me.at(y=turn(me.y, -1))
        if dy == 2:
            self.go(self.one(2, 0), self.far.at[0], above, (tag, "far", 0))
            self.go(self.one(2, 1), self.far.at[1], below, (tag, "far", 1))
        elif dy == 1:
            self.go(self.one(1, 1), self.side.at[0, 1], above, (tag, "side", 0, 1))
        elif dy == -1:
            self.go(self.one(-1, 0), self.side.at[1, 0], below, (tag, "side", 1, 0))

    def relay(self):
        me, net, tag = self.me, self.net, self.tag
        above, below = me.at(y=turn(me.y, 1)), me.at(y=turn(me.y, -1))
        net.take(self.far.at[0], (tag, "far", 0), below)
        add_into(self.one(1, 0), (self.one(1, 0), self.far.at[0]))
        self.go(self.one(1, 0), self.side.at[0, 0], above, (tag, "side", 0, 0))
        net.take(self.far.at[1], (tag, "far", 1), above)
        add_into(self.one(-1, 1), (self.one(-1, 1), self.far.at[1]))
        self.go(self.one(-1, 1), self.side.at[1, 1], below, (tag, "side", 1, 1))

    def arrive(self):
        for way in range(2):
            for k in range(2):
                self.net.take(self.side.at[way, k], (self.tag, "side", way, k), self.me.sibling())

    def total(self, k, at):
        return (
            self.one(0, k)[at, :].astype(F32)
            + self.side[0, k, at, :].astype(F32)
            + self.side[1, k, at, :].astype(F32)
        )


class GatherPlane:
    def __init__(self, net, me, g, tag, pieces):
        self.net, self.me, self.g, self.tag, self.pieces = net, me, g, tag, pieces
        self.sent = []

    def block(self, h, da, db):
        me = self.me
        if h == 0:
            return self.g.at[turn(me.x, db), turn(me.z, da), 0]
        return self.g.at[turn(me.x, da), turn(me.z, db), 1]

    def peer(self, h, da, db):
        me = self.me
        if h == 0:
            return me.at(x=turn(me.x, db), z=turn(me.z, da))
        return me.at(x=turn(me.x, da), z=turn(me.z, db))

    def copy(self, h, da, db, step_a, step_b, rows=None):
        here = self.block(h, da, db)
        name = (self.tag, h, (da - step_a) % 4, (db - step_b) % 4)
        if rows is not None:
            here = here.at[pl.ds(32 * rows, 32)]
            name += (rows,)
        return (here, here, self.peer(h, step_a, step_b), name)

    def send(self, copies):
        self.sent += self.net.many([self.copy(*one) for one in copies], self.pieces)

    def take(self, h, da, db, rows=None):
        here = self.block(h, da, db)
        name = (self.tag, h, da % 4, db % 4)
        if rows is not None:
            here = here.at[pl.ds(32 * rows, 32)]
            name += (rows,)
        self.net.take(here, name, self.me.sibling())

    def start(self):
        self.send([(h, 0, 0, step, 0) for h in range(2) for step in (1, -1)])
        self.send([(h, 0, 0, 0, step) for h in range(2) for step in (1, -1)])

    def second(self):
        for h in range(2):
            self.take(h, -1, 0)
            self.take(h, 1, 0)
        self.send(
            [(h, -step, 0, step, 0, 0 if step == 1 else 1) for h in range(2) for step in (1, -1)]
        )
        for da in (-1, 1):
            self.send([(h, da, 0, 0, step) for h in range(2) for step in (1, -1)])

    def third(self):
        for h in range(2):
            self.take(h, 0, -1)
            self.take(h, 0, 1)
        self.send([(h, 0, -1, 0, 1) for h in range(2)])
        for h in range(2):
            self.take(h, 2, 0, rows=0)
            self.take(h, 2, 0, rows=1)
        self.send([(h, 2, 0, 0, step) for h in range(2) for step in (1, -1)])

    def fourth(self):
        for h in range(2):
            self.take(h, -1, -1)
            self.take(h, -1, 1)
            self.take(h, 1, -1)
            self.take(h, 1, 1)
        self.send([(h, da, 1, 0, -1) for da in (-1, 1) for h in range(2)])

    def fifth(self):
        for h in range(2):
            self.take(h, 2, -1)
            self.take(h, 2, 1)
        self.send([(h, 2, -1, 0, 1) for h in range(2)])

    def finish(self):
        for h in range(2):
            for da in (0, -1, 1, 2):
                self.take(h, da, 2)


class ReducePlane:
    def __init__(self, net, me, g, far, side, far2, side2, tag):
        self.net, self.me, self.g, self.tag = net, me, g, tag
        self.far, self.side, self.far2, self.side2 = far, side, far2, side2

    def super(self, h, db, lo, g=None):
        me = self.me
        g = self.g if g is None else g
        if h == 0:
            return g.at[turn(me.x, db), pl.ds(lo, 2), 0]
        return g.at[pl.ds(lo, 2), turn(me.z, db), 1]

    def whole(self, h, a):
        me = self.me
        return self.g.at[me.x, a, 0] if h == 0 else self.g.at[a, me.z, 1]

    def along(self, h, db):
        me = self.me
        return me.at(x=turn(me.x, db)) if h == 0 else me.at(z=turn(me.z, db))

    def across(self, h, da):
        me = self.me
        return me.at(z=turn(me.z, da)) if h == 0 else me.at(x=turn(me.x, da))

    def start(self, g=None):
        net, tag = self.net, self.tag
        far, side = [], []
        for h in range(2):
            far.append((self.super(h, 2, 0, g), self.far.at[h, 0], self.along(h, 1), (tag, h, "far", 0)))
            far.append((self.super(h, 2, 2, g), self.far.at[h, 1], self.along(h, -1), (tag, h, "far", 1)))
            to = self.side.at[h, 0, pl.ds(2, 2)]
            side.append((self.super(h, 1, 2, g), to, self.along(h, 1), (tag, h, "side", 0, 1)))
            to = self.side.at[h, 1, pl.ds(0, 2)]
            side.append((self.super(h, -1, 0, g), to, self.along(h, -1), (tag, h, "side", 1, 0)))
        net.many(far, 1)
        net.many(side, 1)

    def second(self):
        net, tag = self.net, self.tag
        for h in range(2):
            for way in range(2):
                here = self.far.at[h, way]
                net.take(here, (tag, h, "far", way), self.me.sibling())
                step = 1 if way == 0 else -1
                add_into(here, (here, self.super(h, step, 2 * way)))
                net.go(
                    here, self.side.at[h, way, pl.ds(2 * way, 2)], self.along(h, step), (tag, h, "side", way, way)
                )

    def third(self):
        net, tag = self.net, self.tag
        for h in range(2):
            for way in range(2):
                for lo in range(2):
                    here = self.side.at[h, way, pl.ds(2 * lo, 2)]
                    net.take(here, (tag, h, "side", way, lo), self.me.sibling())
        me = self.me
        for h in range(2):
            mine = me.z if h == 0 else me.x
            for da in (2, 1, -1, 0):
                a = turn(mine, da)
                here = self.side.at[h, 0, a]
                add_into(here, (here, self.side.at[h, 1, a], self.whole(h, a)))
                if da == 2:
                    for way in range(2):
                        net.go(
                            here.at[pl.ds(32 * way, 32)],
                            self.far2.at[h, way],
                            self.across(h, 1 if way == 0 else -1),
                            (tag, h, "far2", way),
                        )
                elif da != 0:
                    way = 0 if da == 1 else 1
                    rows = pl.ds(32 * (1 - way), 32)
                    net.go(
                        here.at[rows], self.side2.at[h, way, rows], self.across(h, da), (tag, h, "side2", way, 1 - way)
                    )

    def fourth(self):
        net, tag, me = self.net, self.tag, self.me
        for h in range(2):
            mine = me.z if h == 0 else me.x
            for way in range(2):
                here = self.far2.at[h, way]
                net.take(here, (tag, h, "far2", way), me.sibling())
                da = 1 if way == 0 else -1
                rows = pl.ds(32 * way, 32)
                add_into(here, (here, self.side.at[h, 0, turn(mine, da), rows]))
                net.go(here, self.side2.at[h, way, rows], self.across(h, da), (tag, h, "side2", way, way))

    def finish(self):
        net, tag, me = self.net, self.tag, self.me
        for h in range(2):
            mine = me.z if h == 0 else me.x
            for way in range(2):
                for part in range(2):
                    here = self.side2.at[h, way, pl.ds(32 * part, 32)]
                    net.take(here, (tag, h, "side2", way, part), me.sibling())
            here = self.side2.at[h, 0]
            add_into(here, (here, self.side2.at[h, 1], self.side.at[h, 0, mine]))


def column_peers(me):
    peers = []
    for d in range(1, 8):
        y, c = me.column(d)
        peers.append(me.at(y=y, c=c))
    return peers


def one_less_exp(t, plain):
    series = 1.0 - t * (1.0 / 8.0)
    for k in range(7, 1, -1):
        series = 1.0 - t * (1.0 / k) * series
    return jnp.where(t < 0.5, t * series, plain)


def decay_parts(rate, log_scale, resets):
    log_decay = rate * log_scale
    a = jnp.exp(log_decay)
    margin = one_less_exp(-2.0 * log_decay, 1.0 - a * a)
    scale = jnp.where(resets > 0.5, 1.0, jnp.sqrt(jnp.maximum(margin, FLOOR_VALUE)))
    return a, a * (1.0 - resets), scale, margin


def log_scale_row(vec):
    return -8.0 * jax.nn.softplus(-vec[7:8, :])


STEP = 32


def blocks(first, count, body):
    def one(i, _):
        row, j = first + lax.div(i, 128 // STEP), lax.rem(i, 128 // STEP)
        at = pl.ds(pl.multiple_of(j * STEP, STEP), STEP)
        body(row, j, at)
        return 0

    lax.fori_loop(0, count * (128 // STEP), one, 0, unroll=2)


def mask_block(masks, row, j):
    inner = 64 // STEP
    at = pl.ds(pl.multiple_of(lax.rem(j, inner) * STEP, STEP), STEP)
    return masks[row, lax.div(j, inner), at, :].astype(F32)


def lanes_below(shape, limit):
    return lax.broadcasted_iota(jnp.int32, shape, len(shape) - 1) < limit


def forward_kernel(
    px, py, po, wg, wu, wd, tokens_in, cot_in, seg, rate_in, input_in, odds_in,
    p_out, one_out, mask_out, gain_out, vec_out, riw_out, ce_out,
    pre_out, co_out, rt_out, ig_out, st_out, carry_out, mix_out, gf_out, gd_out, gb_out, pout_out, res_out, gres_out, gain2_out,
    pxl, pyl, pol, wp, rate_l, input_l, odds, sm, x1, gt, gpart,
    pbuf, wf, xg, sg, small, riw, vec, gains, ce, pre, co, rt, ig, fa, st, mix, car, carry, pair, far, side, res, two, xo,
    s2, ct, cot, hid, gu, pout, gb, gres, gain2, flip, far_d, side_d, far2_d, side2_d,
    send, recv, local, ssend, srecv,
):
    me = Place()
    net = Net(send, recv, local)
    loads = [
        net.local(a, b)
        for a, b in (
            (px, pxl), (py, pyl), (po, pol), (odds_in, odds), (rate_in, rate_l), (input_in, input_l), (tokens_in, xo), (cot_in, cot)
        )
    ]
    to_y, to_c, index = me.x, lax.div(me.z, 2), lax.rem(me.z, 2) * 8 + me.c * 4 + me.y
    mine = jnp.logical_and(to_y == me.y, to_c == me.c)

    def small_from(j):
        return me.at(x=me.y, z=2 * me.c + j // 8, c=(j // 4) % 2, y=j % 4)

    def small_to(p):
        return me.at(x=p // 4, z=p % 4, c=to_c, y=to_y)

    barrier = greet(column_peers(me) + [me.flat(d) for d in range(1, 16)])
    for i in range(16):

        @pl.when(jnp.logical_not(jnp.logical_and(mine, me.plane == i)))
        def _():
            pl.semaphore_signal(barrier, inc=1, device_id=small_to(i), device_id_type=MESH)

        @pl.when(jnp.logical_not(jnp.logical_and(mine, index == i)))
        def _():
            pl.semaphore_signal(barrier, inc=1, device_id=small_from(i), device_id_type=MESH)

    spot = lax.broadcasted_iota(jnp.int32, (64, 128), 0) + (me.plane * 2 + me.c) * 64
    lane = lax.broadcasted_iota(jnp.int32, (64, 128), 1)
    for k in range(2):
        reset, crossed = jnp.zeros((64, 128), F32), jnp.zeros((64, 128), F32)
        for j in range(4):
            start = seg[k, j]
            reset = jnp.where(spot == start, 1.0, reset)
            crossed = jnp.where(jnp.logical_and(start <= spot, start > spot - lane), 1.0, crossed)
        usable = jnp.where(jnp.logical_and(lane <= 3, spot >= lane), 1.0 - crossed, 0.0)
        x1[k, :, 2048:TOK] = jnp.where(lane == 0, reset, usable).astype(BF)

    for copy in loads[:6]:
        copy.wait()
    zeros = jnp.zeros((16, 256), F32)
    for t in range(8):
        low, shift = 128 * (CH * t // 128), CH * t % 128

        def window(ref):
            wide = ref[:, low : low + WIDE].astype(F32)
            wide = pltpu.roll(wide, WIDE - shift, 1) if shift else wide
            return jnp.where(lanes_below((16, WIDE), CH), wide, 0.0)

        both = jnp.concatenate([window(pxl), zeros], axis=1)
        both = both + pltpu.roll(jnp.concatenate([window(pyl), zeros], axis=1), CH, 1)
        wp[t, :, 0:640] = both.astype(BF)
        wp[t, :, 640:PK] = window(pol).astype(BF)
    small[0:32, :] = jnp.zeros((32, WIDE), F32)
    small[0:20, 0:160] = rate_l[...].astype(F32)
    left = small[0:32, :]
    small[0:20, 0:160] = input_l[...].astype(F32)
    left = left + pltpu.roll(small[0:32, :], 160, 1)
    small[0:32, :] = left
    small[24:32, 0:128] = odds[0:8, :]
    sm[...] = small[0:32, :].astype(BF)
    gt[...] = pltpu.roll(odds[8:16, :], me.c * 64 + me.y * 16, 1)
    pl.semaphore_wait(barrier, 22 + 32 - 2 * mine.astype(jnp.int32))

    def p_block(y, c):
        return pbuf.at[me.x, me.z, c, pl.ds(pl.multiple_of(16 * y, 16), 16)]

    def f_block(y, c, k):
        rows = pl.ds(pl.multiple_of(16 * y, 16), 16)
        return wf.at[me.x, me.z, c, rows, pl.ds(HID * k, HID)]

    def features(p):
        return pl.ds(pl.multiple_of(128 * p, 128), 128)

    for d in range(1, 8):
        y, c = me.column(d)
        net.go(gt, gpart.at[d], me.at(y=y, c=c), ("gain8", d))
    for d in range(1, 8):
        y, c = me.column(d)
        net.go(wp.at[2 * y + c], p_block(me.y, me.c), me.at(y=y, c=c), ("wp", d))
    own_p = net.local(wp.at[me.part], p_block(me.y, me.c))
    total = gt[...]
    for d in range(1, 8):
        net.take(gpart.at[d], ("gain8", d), me.sibling())
        total = total + gpart[d]
    gpart[0] = total
    gains[:, features(me.plane)] = total
    for d in range(1, 16):
        net.go(gpart.at[0], gains.at[:, features(me.plane)], me.flat(d), ("gain", d))

    def source(d):
        return turn(me.y, -(d // 2)), me.c if d % 2 == 0 else 1 - me.c

    for d in range(1, 8):
        net.take(p_block(*source(d)), ("wp", d), me.sibling())
    own_p.wait()
    proj = GatherPlane(net, me, pbuf, "p", 1)
    proj.start()
    loads[6].wait()
    for d in range(1, 16):
        net.take(gains.at[:, features(lax.rem(me.plane + 16 - d, 16))], ("gain", d), me.sibling())
    for k in range(2):

        def norm_step(i, _):
            at = pl.ds(pl.multiple_of(i * 16, 16), 16)
            x = xo[k, at, :].astype(F32)
            scale = lax.rsqrt(jnp.mean(x * x, axis=-1, keepdims=True) + EPSILON)
            x1[k, at, 0:2048] = (x * scale * gains[0:1, :]).astype(BF)
            return 0

        lax.fori_loop(0, 4, norm_step, 0, unroll=2)
    tokens = GatherColumn(net, me, xg, "x")
    tokens.start(x1)
    proj.second()

    def small_copy(i):
        return pltpu.make_async_remote_copy(
            src_ref=sm,
            dst_ref=sg.at[index],
            send_sem=ssend.at[i],
            recv_sem=srecv.at[index],
            device_id=small_to(i),
            device_id_type=MESH,
        )

    for i in range(16):
        own = jnp.logical_and(mine, me.plane == i)

        @pl.when(jnp.logical_not(own))
        def _():
            small_copy(i).start()

        @pl.when(own)
        def _():
            pltpu.make_async_copy(sm, sg.at[index], srecv.at[index]).start()

    tokens.relay((0,))
    proj.third()
    for d in range(1, 8):
        y, c = me.column(d)
        for k, w in enumerate((wg, wu, wd)):
            cols = pl.ds(pl.multiple_of(HID * (2 * y + c), HID), HID)
            net.go(w.at[:, cols], f_block(me.y, me.c, k), me.at(y=y, c=c), ("wf", d, k))
    own_f = []
    for k, w in enumerate((wg, wu, wd)):
        cols = pl.ds(pl.multiple_of(HID * me.part, HID), HID)
        own_f.append(net.local(w.at[:, cols], f_block(me.y, me.c, k)))
    proj.fourth()
    tokens.relay((1,))
    proj.fifth()
    tokens.last()

    small[...] = jnp.zeros_like(small)
    for j in range(16):

        @pl.when(jnp.logical_not(jnp.logical_and(mine, index == j)))
        def _():
            pltpu.make_async_remote_copy(
                src_ref=sm,
                dst_ref=sg.at[j],
                send_sem=ssend.at[0],
                recv_sem=srecv.at[j],
                device_id=me.sibling(),
                device_id_type=MESH,
            ).wait_recv()

        @pl.when(jnp.logical_and(mine, index == j))
        def _():
            pltpu.make_async_copy(sm, sg.at[j], srecv.at[j]).wait()

    vectors = jnp.zeros((8, WIDE), F32)
    inside = lanes_below((8, WIDE), 20)
    for j in range(16):
        block = sg[j].astype(F32)
        small[20 * j : 20 * j + 20, :] = block[0:20, :]
        vectors = vectors + pltpu.roll(jnp.where(inside, block[24:32, :], 0.0), 20 * j, 1)
    vec[...] = vectors
    rows = lax.broadcasted_iota(jnp.int32, (WIDE, WIDE), 0)
    lanes = lax.broadcasted_iota(jnp.int32, (WIDE, WIDE), 1)
    held = small[...]
    first = jnp.logical_and(rows < 160, lanes < 160)
    second = jnp.logical_and(jnp.logical_and(rows >= 160, rows < CH), jnp.logical_and(lanes >= 160, lanes < CH))
    riw[:, 0:WIDE] = (jnp.where(first, held, 0.0) + jnp.where(second, pltpu.roll(held, 160, 1), 0.0)).astype(BF)
    riw[:, WIDE:] = (
        jnp.where(first, pltpu.roll(held, WIDE - 160, 1), 0.0) + jnp.where(second, held, 0.0)
    ).astype(BF)
    for d in range(1, 8):
        for k in range(3):
            net.take(f_block(*source(d), k), ("wf", d, k), me.sibling())
    for copy in own_f:
        copy.wait()
    feed = GatherPlane(net, me, wf, "f", 1)
    feed.start()
    loads[7].wait()
    cots = GatherColumn(net, me, ct, "c")
    cots.start(cot)
    proj.finish()
    tokens.finish()
    masks = xg.at[:, :, :, pl.ds(2048, 128)]

    def project(i, _):
        at = pl.ds(2 * i, 2)
        left = xg[at, :, :, 0:2048].reshape(256, 2048)
        both = dot(left, pbuf[:, :, :, :, 0:640].reshape(2048, 640))
        low = jnp.where(lanes_below((256, WIDE), CH), both[:, 0:WIDE], 0.0).astype(BF)
        ce[at, 16:144, :] = low.reshape(2, 128, WIDE)
        right = jnp.where(lanes_below((256, WIDE), CH), pltpu.roll(both[:, 256:640], WIDE - 64, 1), 0.0)
        pre[at] = right.reshape(2, 128, WIDE)
        return 0

    lax.fori_loop(0, 4, project, 0)
    for copy in tokens.sent:
        copy.wait_send()
    wide = xg.at[:, :, :, pl.ds(0, 2048)]
    save_one = net.local(wide, one_out)
    net.go(ce.at[:, pl.ds(128, 16)], ce.at[:, pl.ds(0, 16)], me.flat(1), "halo")
    cots.relay()
    net.take(ce.at[:, pl.ds(0, 16)], "halo", me.sibling())

    def convolve(row, j, at):
        wide = ce[row, pl.ds(pl.multiple_of(j * STEP, STEP), STEP + 16), :].astype(F32)
        valid = mask_block(masks, row, j)
        total = jnp.broadcast_to(vec[4:5, :], (STEP, WIDE))
        for k in range(4):
            piece = wide[16 - k : 16 - k + STEP, :]
            if k > 0:
                piece = piece * valid[:, k : k + 1]
            total = total + vec[k : k + 1, :] * piece
        co[row, at, :] = total

    blocks(0, 8, convolve)
    feed.second()

    def gates(i, _):
        at = pl.ds(4 * i, 4)
        both = dot(co[at].reshape(512, WIDE).astype(BF), riw[...])
        rt[at] = both[:, 0:WIDE].reshape(4, 128, WIDE)
        ig[at] = both[:, WIDE:].reshape(4, 128, WIDE)
        return 0

    lax.fori_loop(0, 2, gates, 0)
    log_scale = log_scale_row(vec)

    def decays(row, j, at):
        rate = jax.nn.sigmoid(rt[row, at, :] + vec[5:6, :])
        gate = jax.nn.sigmoid(ig[row, at, :] + vec[6:7, :])
        _, factor, scale, _ = decay_parts(rate, log_scale, mask_block(masks, row, j)[:, 0:1])
        rt[row, at, :] = rate
        ig[row, at, :] = gate
        fa[row, at, :] = factor
        st[row, at, :] = scale * (gate * co[row, at, :])

    blocks(0, 8, decays)
    cots.last()
    feed.third()

    def scan(i, held):
        h, q = held
        at = pl.ds(pl.multiple_of(i * 8, 8), 8)
        f, d = jnp.swapaxes(fa[:, at, :], 0, 1), jnp.swapaxes(st[:, at, :], 0, 1)
        hs, qs = [], []
        for k in range(8):
            h, q = f[k] * h + d[k], q * f[k]
            hs.append(h)
            qs.append(q)
        st[:, at, :] = jnp.swapaxes(jnp.stack(hs), 0, 1)
        fa[:, at, :] = jnp.swapaxes(jnp.stack(qs), 0, 1)
        return h, q

    h, q = lax.fori_loop(0, 16, scan, (jnp.zeros((8, WIDE), F32), jnp.ones((8, WIDE), F32)), unroll=2)
    car[me.plane, 0] = q
    car[me.plane, 1] = h
    for d in range(1, 16):
        net.go(car.at[me.plane], car.at[me.plane], me.flat(d), ("carry", d))
    for d in range(1, 16):
        net.take(car.at[lax.rem(me.plane + 16 - d, 16)], ("carry", d), me.sibling())
    h = jnp.zeros((8, WIDE), F32)
    for k in range(15):
        h = jnp.where(k < me.plane, car[k, 0] * h + car[k, 1], h)
    carry[...] = h
    branch = ReduceColumn(net, me, wide, pair, far, side, "branch")
    save_one.wait()
    feed.fourth()

    def outward(dy):
        first = 2 * turn(me.y, dy)

        def mixing(row, j, at):
            states = st[row, at, :] + fa[row, at, :] * carry[pl.ds(row, 1), :]
            st[row, at, :] = states
            mix[row, at, :] = (states * gelu(pre[row, at, :])).astype(BF)

        blocks(first, 2, mixing)
        at = pl.ds(first, 2)

        def onto(n, _):
            low = dot_last(mix[at].reshape(256, WIDE), pbuf[n, :, :, :, 640:1024].reshape(512, WIDE)).astype(BF)
            xg[at, :, :, pl.ds(pl.multiple_of(512 * n, 512), 512)] = low.reshape(2, 2, 64, 512)
            return 0

        lax.fori_loop(0, 4, onto, 0)
        branch.send_pair(dy)

    outward(2)
    outward(1)
    branch.take_pair(2)
    outward(-1)
    branch.take_pair(1)
    outward(0)
    branch.take_pair(-1)
    feed.fifth()
    keep = [
        net.local(src, dst)
        for src, dst in (
            (rt, rt_out), (ig, ig_out), (co, co_out), (pbuf, p_out), (masks, mask_out), (gains, gain_out),
            (vec, vec_out), (riw, riw_out), (ce, ce_out), (pre, pre_out), (st, st_out), (carry, carry_out),
            (mix, mix_out),
        )
    ]
    branch.relay()
    branch.take_pair(0)
    branch.arrive()
    for k in range(2):

        def close_branch(i, _):
            at = pl.ds(pl.multiple_of(i * 16, 16), 16)
            value = xo[k, at, :].astype(F32) + branch.total(k, at)
            res[k, at, :] = value
            scale = lax.rsqrt(jnp.mean(value * value, axis=-1, keepdims=True) + EPSILON)
            two[k, at, :] = (value * scale * gains[1:2, :]).astype(BF)
            return 0

        lax.fori_loop(0, 4, close_branch, 0, unroll=2)
    branch.drain()
    scaled = GatherColumn(net, me, s2, "two")
    scaled.start(two)
    cots.finish()
    for copy in keep[:3]:
        copy.wait()
    feed.finish()

    def ahead(*dys):
        count = 2 * len(dys)
        first = [turn(me.y, dy) for dy in dys]
        for ref, source, k in ((rt, s2, 0), (ig, s2, 1), (co, ct, 2)):
            left = jnp.concatenate([source[pl.ds(2 * yy, 2)].reshape(256, 2048) for yy in first], axis=0)
            product = dot(left, wf[:, :, :, :, HID * k : HID * (k + 1)].reshape(2048, HID))
            ref[0:count] = product[:, 0:WIDE].reshape(count, 128, WIDE)
            ref[count : 2 * count] = product[:, WIDE:].reshape(count, 128, WIDE)
        for number, yy in enumerate(first):

            def bend(j, _):
                row = lax.div(j, 8)
                here = pl.ds(pl.multiple_of(16 * lax.rem(j, 8), 16), 16)
                rows = pl.ds(pl.multiple_of(256 * yy + 16 * j, 16), 16)
                for half in range(2):
                    lanes = slice(WIDE * half, WIDE * (half + 1))
                    at = count * half + 2 * number + row
                    up, grad = ig[at, here, :], co[at, here, :]
                    act, slant = gelu_and_slope(rt[at, here, :])
                    hid[rows, lanes] = (act * up).astype(BF)
                    gu[rows, lanes] = (grad * (up * slant)).astype(BF)
                    gu[rows, HID + WIDE * half : HID + WIDE * (half + 1)] = (grad * act).astype(BF)
                return 0

            lax.fori_loop(0, 16, bend, 0)

    scaled.whole(0)
    ahead(0)
    scaled.relay()
    scaled.whole(1)
    scaled.whole(-1)
    ahead(1, -1)
    scaled.last()
    scaled.whole(2)
    ahead(2)
    slope = ReduceColumn(net, me, wide, pair, far, side, "slope")

    def inner(*dys):
        first = [turn(me.y, dy) for dy in dys]

        def out(n, _):
            left = [gu[pl.ds(pl.multiple_of(256 * yy, 256), 256), :] for yy in first]
            low = dot_last(jnp.concatenate(left, axis=0), wf[n, :, :, :, 0:FG].reshape(512, FG)).astype(BF)
            at = pl.ds(pl.multiple_of(512 * n, 512), 512)
            for number, yy in enumerate(first):
                xg[pl.ds(2 * yy, 2), :, :, at] = low[256 * number : 256 * (number + 1)].reshape(2, 2, 64, 512)
            return 0

        lax.fori_loop(0, 4, out, 0)
        for dy in dys:
            slope.send_pair(dy)

    def down(n, _):
        low = dot_last(hid[...], wf[n, :, :, :, FG:].reshape(512, HID)).astype(BF)
        pout[:, :, :, pl.ds(pl.multiple_of(512 * n, 512), 512)] = low.reshape(8, 2, 64, 512)
        return 0

    inner(2, 1)
    slope.take_pair(2)
    slope.take_pair(1)
    inner(-1, 0)
    slope.take_pair(-1)
    slope.relay()
    slope.take_pair(0)
    lax.fori_loop(0, 4, down, 0)

    def store(i):
        lanes = pl.ds(0, FG)
        return pltpu.make_async_copy(wf.at[i, :, :, :, lanes], gf_out.at[i], ssend.at[i])

    def columns(i):
        return pl.ds(pl.multiple_of(512 * i, 512), 512)

    def weights_down(i, _):
        flip[...] = jnp.transpose(ct[:, :, :, columns(i)].reshape(1024, 512))
        wf[i, :, :, :, FG:] = dot(flip[...], hid[...]).astype(BF).reshape(4, 2, 64, HID)
        return 0

    def weights(i, _):
        flip[...] = jnp.transpose(s2[:, :, :, columns(i)].reshape(1024, 512))
        for k in range(2):
            lanes = slice(HID * k, HID * (k + 1))
            wf[i, :, :, :, lanes] = dot(flip[...], gu[:, lanes]).astype(BF).reshape(4, 2, 64, HID)
        store(i).start()
        return 0

    under = ReducePlane(net, me, wf.at[:, :, :, :, pl.ds(FG, HID)], far_d, side_d, far2_d, side2_d, "d")

    for i in range(16):

        @pl.when(jnp.logical_not(jnp.logical_and(mine, me.plane == i)))
        def _():
            small_copy(i).wait_send()

    gain2[...] = jnp.zeros_like(gain2)
    for copy in feed.sent:
        copy.wait_send()
    lax.fori_loop(0, 4, weights_down, 0)
    under.start()
    slope.arrive()
    for k in range(2):

        def close(i, _):
            at = pl.ds(pl.multiple_of(i * 16, 16), 16)
            value = res[k, at, :]
            scale = lax.rsqrt(jnp.mean(value * value, axis=-1, keepdims=True) + EPSILON)
            normed = value * scale
            got = slope.total(k, at)
            gain2[0:8, :] = gain2[0:8, :] + (got * normed).reshape(2, 8, 2048).sum(axis=0)
            v = got * gains[1:2, :]
            back = (v - normed * jnp.mean(v * normed, axis=-1, keepdims=True)) * scale
            total = cot[k, at, :].astype(F32) + back
            gres[k, at, :] = total
            gb[k, at, :] = total.astype(BF)
            return 0

        lax.fori_loop(0, 4, close, 0, unroll=2)
    back = GatherColumn(net, me, gb_out, "gb")
    back.start(gb)
    keep += [net.local(gres, gres_out), net.local(gain2, gain2_out), net.local(pout, pout_out), net.local(res, res_out)]
    under.second()
    lax.fori_loop(0, 2, weights, 0)
    back.relay((0,))
    under.third()
    lax.fori_loop(2, 3, weights, 0)
    back.relay((1,))
    lax.fori_loop(3, 4, weights, 0)
    back.last()
    under.fourth()
    under.finish()
    keep.append(net.local(side2_d.at[:, 0], gd_out))
    for i in range(4):
        store(i).wait()
    back.finish()
    for copy in keep[3:]:
        copy.wait()
    net.drain(tokens.sent + branch.sent + feed.sent)


def backward_kernel(
    gb_in, p_in, gf_in, one_in, mask_in, gain_in, vec_in, riw_in, ce_in, pre_in, co_in, rt_in, ig_in, st_in, mix_in,
    carry_in, gres_in, gain2_in, x_in, pout_in, res_in, gd_in,
    ff_out, fd_out, fo_out, fi_out, small_out, gains_out, gx_out, out_out,
    gb, w, gf, masks, gains, vec, riw, ce, pre, co, rt, ig, st, mix, carry, gres, gain2, xo,
    gm, fa, car, edge, z, sgr, srec, ssum, part, pair, far, side, pair2, far2, side2, res, out, gpi, far_f, side_f, far2_f, side2_f,
    far_o, side_o, far2_o, side2_o, far_i, side_i, far2_i, side2_i, ff, fd, fo, fi, grow, gsum, gtot, gall, gx, wacc, halo,
    send, recv, local, ssend, srecv,
):
    me = Place()
    net = Net(send, recv, local)
    loads = {
        name: net.local(a, b)
        for name, a, b in (
            ("gb", gb_in, gb), ("w", p_in, w), ("pre", pre_in, pre), ("st", st_in, st), ("part", pout_in, part), ("mix", mix_in, mix),
            ("rt", rt_in, rt), ("masks", mask_in, masks), ("vec", vec_in, vec), ("gf", gf_in, gf), ("co", co_in, co),
            ("ig", ig_in, ig), ("carry", carry_in, carry), ("riw", riw_in, riw), ("ce", ce_in, ce),
            ("gains", gain_in, gains), ("gres", gres_in, gres), ("gain2", gain2_in, gain2), ("x", x_in, xo), ("res", res_in, res),
        )
    }

    def need(*names):
        for name in names:
            loads[name].wait()

    to_y, to_c, index = me.x, lax.div(me.z, 2), lax.rem(me.z, 2) * 8 + me.c * 4 + me.y
    mine = jnp.logical_and(to_y == me.y, to_c == me.c)

    def small_to(j):
        return me.at(x=me.y, z=2 * me.c + j // 8, c=(j // 4) % 2, y=j % 4)

    def small_from(p):
        return me.at(x=p // 4, z=p % 4, c=to_c, y=to_y)

    barrier = greet(column_peers(me) + [me.flat(d) for d in range(1, 16)])
    for i in range(16):

        @pl.when(jnp.logical_not(jnp.logical_and(mine, me.plane == i)))
        def _():
            pl.semaphore_signal(barrier, inc=1, device_id=small_from(i), device_id_type=MESH)

        @pl.when(jnp.logical_not(jnp.logical_and(mine, index == i)))
        def _():
            pl.semaphore_signal(barrier, inc=1, device_id=small_to(i), device_id_type=MESH)

    pl.semaphore_wait(barrier, 22 + 32 - 2 * mine.astype(jnp.int32))
    feed = ReducePlane(net, me, gf, far_f, side_f, far2_f, side2_f, "f")
    result = ReduceColumn(net, me, part, pair2, far2, side2, "result")
    gpo = w.at[:, :, :, :, pl.ds(640, WIDE)]
    outer = ReducePlane(net, me, gpo, far_o, side_o, far2_o, side2_o, "o")
    inner = ReducePlane(net, me, gpi, far_i, side_i, far2_i, side2_i, "i")
    feed.start(gf_in)

    def share(source, dst, tag):
        for d in range(1, 8):
            y, c = me.column(d)
            src = source.at[c, pl.ds(pl.multiple_of(16 * y, 16), 16)]
            net.go(src, dst.at[me.part], me.at(y=y, c=c), (tag, d))
        src = source.at[me.c, pl.ds(pl.multiple_of(16 * me.y, 16), 16)]
        return net.local(src, dst.at[me.part])

    def collect(dst, tag):
        for d in range(1, 8):
            y = turn(me.y, -(d // 2))
            c = me.c if d % 2 == 0 else 1 - me.c
            net.take(dst.at[2 * y + c], (tag, d), me.sibling())

    own_d = share(gd_in, fd, "fd")
    need("gb", "w")

    def mix_back(i, _):
        at = pl.ds(4 * i, 4)
        grad = dot(gb[at].reshape(512, 2048), w[:, :, :, :, 640:1024].reshape(2048, WIDE))
        gm[at] = grad.reshape(4, 128, WIDE)
        return 0

    lax.fori_loop(0, 2, mix_back, 0)
    need("part")
    for dy in (2, 1, -1, 0):
        result.send_pair(dy)
    need("pre", "st", "rt", "masks", "vec")
    log_scale = log_scale_row(vec)

    def bend_back(row, j, at):
        act, slant = gelu_and_slope(pre[row, at, :])
        grad = jnp.where(lanes_below((STEP, WIDE), CH), gm[row, at, :], 0.0)
        low = grad * st[row, at, :] * slant
        z[row, at, 256:640] = pltpu.roll(low, 64, 1).astype(BF)
        gm[row, at, :] = grad * act
        _, factor, _, _ = decay_parts(rt[row, at, :], log_scale, mask_block(masks, row, j)[:, 0:1])
        fa[row, at, :] = factor

    blocks(0, 8, bend_back)

    def scan(step, held):
        g, m = held
        at = pl.ds(pl.multiple_of((15 - step) * 8, 8), 8)
        f, d = jnp.swapaxes(fa[:, at, :], 0, 1), jnp.swapaxes(gm[:, at, :], 0, 1)
        las, lps = [None] * 8, [None] * 8
        for k in range(7, -1, -1):
            la = d[k] + g
            las[k], lps[k] = la, m
            g, m = f[k] * la, f[k] * m
        gm[:, at, :] = jnp.swapaxes(jnp.stack(las), 0, 1)
        fa[:, at, :] = jnp.swapaxes(jnp.stack(lps), 0, 1)
        return g, m

    g, m = lax.fori_loop(0, 16, scan, (jnp.zeros((8, WIDE), F32), jnp.ones((8, WIDE), F32)), unroll=2)
    car[me.plane, 0] = m
    car[me.plane, 1] = g
    for d in range(1, 16):
        net.go(car.at[me.plane], car.at[me.plane], me.flat(d), ("carry", d))
    need("mix", "gf")

    def weight_out(i, _):
        left = gb[:, :, :, pl.ds(pl.multiple_of(512 * i, 512), 512)].reshape(1024, 512)
        w[i, :, :, :, 640:1024] = dot_first(left, mix[...].reshape(1024, WIDE)).astype(BF).reshape(4, 2, 64, WIDE)
        return 0

    lax.fori_loop(0, 4, weight_out, 0)
    load_one = net.local(one_in, gb)
    feed.second()
    outer.start()
    for dy in (2, 1, -1, 0):
        result.take_pair(dy)
    for d in range(1, 16):
        net.take(car.at[lax.rem(me.plane + 16 - d, 16)], ("carry", d), me.sibling())
    g = jnp.zeros((8, WIDE), F32)
    for k in range(15, 0, -1):
        g = jnp.where(k > me.plane, car[k, 1] + car[k, 0] * g, g)
    edge[...] = g
    wacc[...] = jnp.zeros_like(wacc)
    need("co", "ig", "carry", "riw", "ce")

    def fold(value):
        return value.reshape(STEP // 8, 8, WIDE).sum(axis=0)

    def gate_back(row, j, at):
        resets = mask_block(masks, row, j)[:, 0:1]
        adjoint = gm[row, at, :] + fa[row, at, :] * edge[pl.ds(row, 1), :]
        rate, gate, conv = rt[row, at, :], ig[row, at, :], co[row, at, :]
        a, factor, scale, margin = decay_parts(rate, log_scale, resets)
        before = st[row, pl.ds(pl.multiple_of(jnp.maximum(j * STEP - 8, 0), 8), 8), :]
        edge_row = jnp.where(j == 0, carry[pl.ds(row, 1), :], before[7:8, :])
        top = lax.broadcasted_iota(jnp.int32, (STEP, WIDE), 0) == 0
        previous = jnp.where(top, edge_row, pltpu.roll(st[row, at, :], 1, 0))
        grad_scale = adjoint * gate * conv
        free = jnp.logical_and(margin > FLOOR_VALUE, resets < 0.5)
        grad_log = adjoint * previous * factor - jnp.where(free, grad_scale * (a * a) / scale, 0.0)
        rate_pre = grad_log * log_scale * rate * (1.0 - rate)
        through = adjoint * scale
        gate_pre = through * conv * gate * (1.0 - gate)
        wacc[5] = wacc[5] + fold(rate_pre)
        wacc[6] = wacc[6] + fold(gate_pre)
        wacc[7] = wacc[7] + fold(grad_log * rate)
        gm[row, at, :] = through * gate
        rt[row, at, :] = rate_pre
        ig[row, at, :] = gate_pre

    blocks(0, 8, gate_back)
    result.relay()

    def through_gates(i, _):
        at = pl.ds(4 * i, 4)
        total = gm[at].reshape(512, WIDE)
        total = total + dot_last(rt[at].reshape(512, WIDE).astype(BF), riw[:, 0:WIDE])
        total = total + dot_last(ig[at].reshape(512, WIDE).astype(BF), riw[:, WIDE:])
        gm[at] = total.reshape(4, 128, WIDE)
        return 0

    lax.fori_loop(0, 2, through_gates, 0)

    def conv_back(row, j, at):
        wide = ce[row, pl.ds(pl.multiple_of(j * STEP, STEP), STEP + 16), :].astype(F32)
        valid = mask_block(masks, row, j)
        grad = gm[row, at, :]
        wacc[4] = wacc[4] + fold(grad)
        total = jnp.zeros((STEP + 8, WIDE), F32)
        for k in range(4):
            kept = grad if k == 0 else grad * valid[:, k : k + 1]
            wacc[k] = wacc[k] + fold(kept * wide[16 - k : 16 - k + STEP, :])
            scaled = kept * vec[k : k + 1, :]
            total = total + jnp.concatenate(
                [jnp.zeros((8 - k, WIDE), F32), scaled] + ([jnp.zeros((k, WIDE), F32)] if k else []), axis=0
            )
        fa[row, at, :] = total[8:, :]
        early = total[0:8, :]

        @pl.when(j == 0)
        def _():
            halo[0, row] = early

        @pl.when(j > 0)
        def _():
            last = pl.ds(pl.multiple_of(j * STEP - 8, 8), 8)
            fa[row, last, :] = fa[row, last, :] + early

    blocks(0, 8, conv_back)
    net.go(halo.at[0], halo.at[1], me.flat(-1), "halo")
    feed.third()
    outer.second()

    net.take(halo.at[1], "halo", me.sibling())

    def conv_in_back(row, j, at):
        grad = fa[row, at, :]
        tail = jnp.where(j == 128 // STEP - 1, halo[1, row], 0.0)
        grad = grad + jnp.concatenate([jnp.zeros((STEP - 8, WIDE), F32), tail], axis=0)
        z[row, at, 0:256] = grad[:, 0:256].astype(BF)
        late = jnp.where(lanes_below((STEP, 128), 64), grad[:, 256:384], z[row, at, 256:384].astype(F32))
        z[row, at, 256:384] = late.astype(BF)

    blocks(0, 8, conv_in_back)
    result.arrive()
    result.drain()
    need("res")
    for k in range(2):

        def close_result(i, _):
            at = pl.ds(pl.multiple_of(i * 16, 16), 16)
            out[k, at, :] = (res[k, at, :] + result.total(k, at)).astype(BF)
            return 0

        lax.fori_loop(0, 4, close_result, 0, unroll=2)
    save_out = net.local(out, out_out)
    entry = ReduceColumn(net, me, part, pair, far, side, "entry")

    def inward(dy):
        at = pl.ds(2 * turn(me.y, dy), 2)

        def out(n, _):
            low = dot_last(z[at].reshape(256, 640), w[n, :, :, :, 0:640].reshape(512, 640)).astype(BF)
            part[at, :, :, pl.ds(pl.multiple_of(512 * n, 512), 512)] = low.reshape(2, 2, 64, 512)
            return 0

        lax.fori_loop(0, 4, out, 0)
        entry.send_pair(dy)

    def weight_in(i, _):
        left = gb[:, :, :, pl.ds(pl.multiple_of(512 * i, 512), 512)].reshape(1024, 512)
        gpi[i] = dot_first(left, z[...].reshape(1024, 640)).astype(BF).reshape(4, 2, 64, 640)
        return 0

    load_one.wait()
    lax.fori_loop(0, 4, weight_in, 0)
    inner.start()
    inward(2)
    inward(1)
    entry.take_pair(2)
    inner.second()
    inward(-1)
    entry.take_pair(1)
    inward(0)
    entry.take_pair(-1)
    feed.fourth()
    inner.third()
    entry.relay()
    entry.take_pair(0)
    outer.third()
    feed.finish()
    own_f = share(side2_f.at[:, 0], ff, "ff")
    inner.fourth()
    outer.fourth()
    low = co[...].reshape(1024, WIDE).astype(BF)
    grad_rate = dot_first(low, rt[...].reshape(1024, WIDE).astype(BF))
    grad_gate = dot_first(low, ig[...].reshape(1024, WIDE).astype(BF))
    rows = lax.broadcasted_iota(jnp.int32, (WIDE, WIDE), 0)
    lanes = lax.broadcasted_iota(jnp.int32, (WIDE, WIDE), 1)
    upper = rows < 160
    held = jnp.where(
        lanes < 160,
        jnp.where(upper, grad_rate, pltpu.roll(grad_rate, WIDE - 160, 1)),
        jnp.where(upper, pltpu.roll(grad_gate, 160, 1), grad_gate),
    )
    vectors = jnp.concatenate([jnp.sum(wacc[k], axis=0, keepdims=True) for k in range(8)], axis=0)
    slope = -8.0 * -jax.nn.sigmoid(-vec[7:8, :])
    line = lax.broadcasted_iota(jnp.int32, (8, WIDE), 0)
    vectors = jnp.where(line == 7, vectors * slope, vectors)
    tall = jnp.transpose(jnp.concatenate([vectors, jnp.zeros((120, WIDE), F32)], axis=0))
    gm[0:3] = held.reshape(3, 128, WIDE)
    late = jnp.where(lanes_below((WIDE, 128), 64), held[:, 256:384], pltpu.roll(tall, 64, 1))
    gm[0:3, :, 256:384] = late.reshape(3, 128, 128)
    flat = gm[0:3].reshape(WIDE, WIDE)
    for j in range(16):
        piece = jnp.concatenate([flat[20 * j : 20 * j + 20, :], jnp.zeros((12, WIDE), F32)], axis=0)
        sgr[j] = piece.astype(BF)

    def small_copy(j):
        return pltpu.make_async_remote_copy(
            src_ref=sgr.at[j],
            dst_ref=srec.at[me.plane],
            send_sem=ssend.at[j],
            recv_sem=srecv.at[me.plane],
            device_id=small_to(j),
            device_id_type=MESH,
        )

    for j in range(16):
        own = jnp.logical_and(mine, index == j)

        @pl.when(jnp.logical_not(own))
        def _():
            small_copy(j).start()

        @pl.when(own)
        def _():
            pltpu.make_async_copy(sgr.at[j], srec.at[me.plane], srecv.at[me.plane]).start()

    need("gains", "gres", "gain2", "x")
    grow[...] = jnp.zeros_like(grow)
    entry.arrive()
    for k in range(2):

        def close(i, _):
            at = pl.ds(pl.multiple_of(i * 16, 16), 16)
            value = xo[k, at, :].astype(F32)
            scale = lax.rsqrt(jnp.mean(value * value, axis=-1, keepdims=True) + EPSILON)
            normed = value * scale
            got = entry.total(k, at)
            grow[...] = grow[...] + (got * normed).reshape(2, 8, 2048).sum(axis=0)
            v = got * gains[0:1, :]
            back = (v - normed * jnp.mean(v * normed, axis=-1, keepdims=True)) * scale
            gx[k, at, :] = (gres[k, at, :] + back).astype(BF)
            return 0

        lax.fori_loop(0, 4, close, 0, unroll=2)
    keep = [net.local(gx, gx_out), save_out]
    line = lax.broadcasted_iota(jnp.int32, (8, 2048), 0)
    one = jnp.broadcast_to(jnp.sum(grow[...], axis=0, keepdims=True), (8, 2048))
    two = jnp.broadcast_to(jnp.sum(gain2[...], axis=0, keepdims=True), (8, 2048))
    grow[...] = jnp.where(line == 0, one, jnp.where(line == 1, two, 0.0))

    def features(p):
        return pl.ds(pl.multiple_of(128 * p, 128), 128)

    for d in range(1, 16):
        p = lax.rem(me.plane + d, 16)
        net.go(grow.at[:, features(p)], gsum.at[me.plane], me.flat(d), ("gain", d))
    gsum[me.plane] = grow[:, features(me.plane)]

    inner.finish()
    own_i = share(side2_i.at[:, 0], fi, "fi")
    outer.finish()
    own_o = share(side2_o.at[:, 0], fo, "fo")
    for p in range(16):

        @pl.when(jnp.logical_not(jnp.logical_and(mine, me.plane == p)))
        def _():
            pltpu.make_async_remote_copy(
                src_ref=sgr.at[0],
                dst_ref=srec.at[p],
                send_sem=ssend.at[0],
                recv_sem=srecv.at[p],
                device_id=me.sibling(),
                device_id_type=MESH,
            ).wait_recv()

        @pl.when(jnp.logical_and(mine, me.plane == p))
        def _():
            pltpu.make_async_copy(sgr.at[0], srec.at[p], srecv.at[p]).wait()

    total = srec[0].astype(F32)
    for k in range(1, 16):
        total = total + srec[k].astype(F32)
    ssum[...] = total
    keep.append(net.local(ssum, small_out))
    for d in range(1, 16):
        net.take(gsum.at[lax.rem(me.plane + 16 - d, 16)], ("gain", d), me.sibling())
    total = gsum[0]
    for k in range(1, 16):
        total = total + gsum[k]
    gall[me.part] = total
    for d in range(1, 8):
        y, c = me.column(d)
        net.go(gall.at[me.part], gall.at[me.part], me.at(y=y, c=c), ("gain8", d))
    own_f.wait()
    collect(ff, "ff")
    keep.append(net.local(ff, ff_out))
    own_d.wait()
    collect(fd, "fd")
    keep.append(net.local(fd, fd_out))
    collect(gall, "gain8")
    total = gall[0]
    for k in range(1, 8):
        total = total + gall[k]
    gtot[...] = total
    keep.append(net.local(gtot, gains_out))
    own_o.wait()
    collect(fo, "fo")
    keep.append(net.local(fo, fo_out))
    own_i.wait()
    collect(fi, "fi")
    keep.append(net.local(fi, fi_out))
    for copy in keep:
        copy.wait()
    net.drain(result.sent)
    for j in range(16):

        @pl.when(jnp.logical_not(jnp.logical_and(mine, index == j)))
        def _():
            small_copy(j).wait_send()


def shaped(shape, kind):
    return jax.ShapeDtypeStruct(shape, kind)


def vmem(shape, kind):
    return pltpu.VMEM(shape, kind)


def call(kernel, args, outs, scratch, name, number, sends, recvs, extra=(), places={}):
    anywhere = pl.BlockSpec(memory_space=pl.ANY)
    return pl.pallas_call(
        kernel,
        out_shape=[shaped(*out) for out in outs],
        in_specs=[places.get(i, anywhere) for i in range(len(args))],
        out_specs=[anywhere] * len(outs),
        scratch_shapes=[vmem(*one) for one in scratch]
        + [pltpu.SemaphoreType.DMA((sends,)), pltpu.SemaphoreType.DMA((recvs,)), pltpu.SemaphoreType.DMA((48,))]
        + list(extra),
        compiler_params=pltpu.CompilerParams(
            collective_id=number, has_side_effects=True, vmem_limit_bytes=62 * 1024 * 1024
        ),
        name=name,
    )(*args)


ROWS = (8, 128, WIDE)
BLOCK = (2, 64, 2048)
ALL = (8, 2, 64, 2048)
SIXTEEN = (pltpu.SemaphoreType.DMA((16,)), pltpu.SemaphoreType.DMA((16,)))


def plane(width):
    return [((2, 2, 2, 64, width), BF), ((2, 2, 4, 64, width), BF), ((2, 2, 32, width), BF), ((2, 2, 64, width), BF)]


def forward(args):
    weights = (4, 4, 2, 64)
    flat = pl.BlockSpec(memory_space=pltpu.SMEM)
    sums = [((4,) + BLOCK, BF), (BLOCK, BF), ((2,) + BLOCK, BF)]
    return call(
        forward_kernel,
        args,
        [
            (weights + (PK,), BF), (ALL, BF), ((8, 2, 64, 128), BF), ((8, 2048), F32), ((8, WIDE), F32),
            ((WIDE, 2 * WIDE), BF), ((8, 144, WIDE), BF),
            (ROWS, F32), (ROWS, F32), (ROWS, F32), (ROWS, F32), (ROWS, F32), ((8, WIDE), F32), (ROWS, BF),
            (weights + (FG,), BF), ((2, 64, HID), BF), (ALL, BF), (ALL, BF), (BLOCK, F32), (BLOCK, F32),
            ((8, 2048), F32),
        ],
        [
            ((16, 2560), BF), ((16, 2560), BF), ((16, 2560), BF), ((8, 16, PK), BF), ((20, 160), BF), ((20, 160), BF),
            ((16, 128), F32), ((SMALL, WIDE), BF), ((2, 64, TOK), BF), ((8, 128), F32), ((8, 8, 128), F32),
            (weights + (PK,), BF), (weights + (FK,), BF), ((8, 2, 64, TOK), BF), ((16, SMALL, WIDE), BF),
            ((WIDE, WIDE), F32), ((WIDE, 2 * WIDE), BF), ((8, WIDE), F32), ((8, 2048), F32), ((8, 144, WIDE), BF),
            (ROWS, F32), (ROWS, F32), (ROWS, F32), (ROWS, F32), (ROWS, F32), (ROWS, F32), (ROWS, BF),
            ((16, 2, 8, WIDE), F32), ((8, WIDE), F32), *sums, (BLOCK, F32), (BLOCK, BF), (BLOCK, BF),
            (ALL, BF), (ALL, BF), (BLOCK, BF), ((1024, HID), BF), ((1024, FG), BF),
            (ALL, BF), (BLOCK, BF), (BLOCK, F32), ((8, 2048), F32), ((512, 1024), BF), *plane(HID),
        ],
        "forward", 1, 256, 256, SIXTEEN, {8: flat},
    )


def backward(args):
    return call(
        backward_kernel,
        args,
        [
            ((8, 16, FG), BF), ((8, 16, HID), BF), ((8, 16, WIDE), BF), ((8, 16, 640), BF), ((SMALL, WIDE), F32), ((8, 128), F32),
            (BLOCK, BF), (BLOCK, BF),
        ],
        [
            (ALL, BF), ((4, 4, 2, 64, PK), BF), ((4, 4, 2, 64, FG), BF), ((8, 2, 64, 128), BF), ((8, 2048), F32),
            ((8, WIDE), F32), ((WIDE, 2 * WIDE), BF), ((8, 144, WIDE), BF), (ROWS, F32), (ROWS, F32), (ROWS, F32),
            (ROWS, F32), (ROWS, F32), (ROWS, BF), ((8, WIDE), F32), (BLOCK, F32), ((8, 2048), F32), (BLOCK, BF),
            (ROWS, F32), (ROWS, F32), ((16, 2, 8, WIDE), F32), ((8, WIDE), F32), ((8, 128, 640), BF),
            ((16, SMALL, WIDE), BF), ((16, SMALL, WIDE), BF), ((SMALL, WIDE), F32),
            (ALL, BF), ((4,) + BLOCK, BF), (BLOCK, BF), ((2,) + BLOCK, BF),
            ((4,) + BLOCK, BF), (BLOCK, BF), ((2,) + BLOCK, BF), (BLOCK, F32), (BLOCK, BF), ((4, 4, 2, 64, 640), BF),
            *plane(FG), *plane(WIDE), *plane(640),
            ((8, 16, FG), BF), ((8, 16, HID), BF), ((8, 16, WIDE), BF), ((8, 16, 640), BF),
            ((8, 2048), F32), ((16, 8, 128), F32), ((8, 128), F32),
            ((8, 8, 128), F32), (BLOCK, BF), ((8, 8, WIDE), F32), ((2, 8, 8, WIDE), F32),
        ],
        "recurrent_backward", 3, 256, 256, SIXTEEN,
    )


def finish_kernel(
    ff_in, fd_in, fo_in, fi_in, small_in, sums_in, gx_in, result_in,
    output, grad_tokens, gain_a, gain_b, conv_w, conv_b, rate_w, input_w, rate_b, input_b, decay,
    out_w, x_w, y_w, gate_w, up_w, down_w,
    ff, fd, fo, fi, small, sums, sems,
):
    me = Place()
    moves = (
        (ff_in, ff), (fd_in, fd), (fo_in, fo), (fi_in, fi), (small_in, small), (sums_in, sums), (gx_in, grad_tokens),
        (result_in, output),
    )
    loads = [pltpu.make_async_copy(a, b, sems.at[i]) for i, (a, b) in enumerate(moves)]
    for copy in loads:
        copy.start()
    for copy in loads:
        copy.wait()
    own = pltpu.roll(sums[...], 128 - (me.c * 64 + me.y * 16), 1)
    gain_a[...] = own[0:1, 0:16]
    gain_b[...] = own[1:2, 0:16]
    rate_w[...] = small[0:20, 0:160]
    input_w[...] = pltpu.roll(small[0:20, :], WIDE - 160, 1)[:, 0:160]
    tall = jnp.concatenate([small[:, 256:384], jnp.zeros((128 - SMALL, 128), F32)], axis=0)
    vectors = jnp.transpose(tall)[64:72, 0:20]
    conv_w[...] = vectors[0:4, :]
    conv_b[...] = vectors[4:5, :]
    rate_b[...] = vectors[5:6, :]
    input_b[...] = vectors[6:7, :]
    decay[...] = vectors[7:8, :]
    for t in range(8):
        at = slice(HID * t, HID * (t + 1))
        gate_w[:, at] = ff[t, :, 0:HID].astype(F32)
        up_w[:, at] = ff[t, :, HID:].astype(F32)
        down_w[:, at] = fd[t].astype(F32)
    zeros = jnp.zeros((16, 256), F32)

    def pair(first, second):
        keep = lanes_below((16, WIDE), CH)
        left = jnp.concatenate([jnp.where(keep, first, 0.0), zeros], axis=1)
        right = jnp.concatenate([jnp.where(keep, second, 0.0), zeros], axis=1)
        return left + pltpu.roll(right, CH, 1)

    for t in range(0, 8, 2):
        at = slice(CH * t, CH * (t + 2))
        out_w[:, at] = pair(fo[t].astype(F32), fo[t + 1].astype(F32))
        x_w[:, at] = pair(fi[t, :, 0:WIDE].astype(F32), fi[t + 1, :, 0:WIDE].astype(F32))
        late = [pltpu.roll(fi[t + i, :, 256:640].astype(F32), WIDE - 64, 1) for i in range(2)]
        y_w[:, at] = pair(*late)


def finish(args):
    held = pl.BlockSpec(memory_space=pltpu.VMEM)
    outs = [
        (BLOCK, BF), (BLOCK, BF), ((1, 16), F32), ((1, 16), F32), ((4, 20), F32), ((1, 20), F32), ((20, 160), F32),
        ((20, 160), F32), ((1, 20), F32), ((1, 20), F32), ((1, 20), F32), ((16, 2560), F32), ((16, 2560), F32),
        ((16, 2560), F32), ((16, 6144), F32), ((16, 6144), F32), ((16, 6144), F32),
    ]
    return pl.pallas_call(
        finish_kernel,
        out_shape=[shaped(*out) for out in outs],
        in_specs=[pl.BlockSpec(memory_space=pl.ANY)] * len(args),
        out_specs=[held] * len(outs),
        scratch_shapes=[
            vmem((8, 16, FG), BF), vmem((8, 16, HID), BF), vmem((8, 16, WIDE), BF), vmem((8, 16, 640), BF),
            vmem((SMALL, WIDE), F32), vmem((8, 128), F32), pltpu.SemaphoreType.DMA((8,)),
        ],
        compiler_params=pltpu.CompilerParams(vmem_limit_bytes=62 * 1024 * 1024),
        name="results",
    )(*args)


def local(
    tokens,
    seg_starts,
    gain_one,
    gain_two,
    conv_weight,
    conv_bias,
    rate_weight,
    input_weight,
    rate_bias,
    input_bias,
    decay_param,
    proj_out,
    proj_x,
    proj_y,
    ffn_gate,
    ffn_up,
    ffn_down,
    cotangent,
):
    vectors = jnp.concatenate([conv_weight, jnp.stack([conv_bias, rate_bias, input_bias, decay_param])], axis=0)
    odds = jnp.concatenate(
        [
            jnp.pad(vectors, ((0, 0), (0, 108))),
            jnp.pad(jnp.stack([gain_one, gain_two]), ((0, 6), (0, 112))),
        ],
        axis=0,
    ).astype(F32)
    (
        p_all, one, mask_all, gains, vec, riw, ce, pre, co, rt, ig, st, carry, mix, gf, gd, gb, pout, res, gres, gain2
    ) = forward((
        proj_x, proj_y, proj_out, ffn_gate, ffn_up, ffn_down, tokens, cotangent, seg_starts, rate_weight, input_weight,
        odds,
    ))
    ff, fd, fo, fi, small, gain_sums, grad_tokens, output = backward((
        gb, p_all, gf, one, mask_all, gains, vec, riw, ce, pre, co, rt, ig, st, mix, carry, gres, gain2, tokens, pout, res,
        gd,
    ))
    results = finish((ff, fd, fo, fi, small, gain_sums, grad_tokens, output))
    return tuple(one.reshape(one.shape[1:]) if i in (2, 3, 5, 8, 9, 10) else one for i, one in enumerate(results))


def solution(mesh):
    both = ("seq", "rows")
    wide, flat = P(both, None), P(both)
    rows = P("rows", "seq", None)
    return jax.shard_map(
        local,
        mesh=mesh,
        in_specs=(
            rows, P("rows", None), flat, flat, P(None, both), flat, wide, wide, flat, flat, flat,
            wide, wide, wide, wide, wide, wide, rows,
        ),
        out_specs=(
            rows, rows, flat, flat, P(None, both), flat, wide, wide, flat, flat, flat,
            wide, wide, wide, wide, wide, wide,
        ),
        check_vma=False,
    )
```

```python
import jax
import jax.numpy as jnp
from jax import lax
from jax.experimental import pallas as pl
from jax.experimental.pallas import tpu as pltpu
from jax.sharding import PartitionSpec as P

BF, F32 = jnp.bfloat16, jnp.float32
MESH = pl.DeviceIdType.MESH
EPSILON = 1e-06
FLOOR_VALUE = 0.001
HID = 768
CH = 320
WIDE = 384
PK = 1024
FK = 2304
FG = 1536
TOK = 2176
SMALL = 32


def dot(left, right):
    return jnp.dot(left, right, preferred_element_type=F32)


def dot_last(left, right):
    return lax.dot_general(left, right, (((1,), (1,)), ((), ())), preferred_element_type=F32)


def dot_first(left, right):
    return lax.dot_general(left, right, (((0,), (0,)), ((), ())), preferred_element_type=F32)


def gelu(v):
    return 0.5 * v * (1.0 + jnp.tanh(0.7978845608028654 * (v + 0.044715 * (v * v * v))))


def gelu_and_slope(v):
    square = v * v
    t = jnp.tanh(0.7978845608028654 * v * (1.0 + 0.044715 * square))
    half = 0.5 * (1.0 + t)
    slope = half + 0.5 * v * (1.0 - t * t) * (0.7978845608028654 * (1.0 + 0.134145 * square))
    return v * half, slope


def turn(v, d):
    return lax.rem(v + (d % 4), 4)


class Place:
    def __init__(self):
        s, self.y = lax.axis_index("seq"), lax.axis_index("rows")
        self.x, self.z, self.c = lax.div(s, 8), lax.rem(lax.div(s, 2), 4), lax.rem(s, 2)
        self.plane = self.x * 4 + self.z
        self.part = self.y * 2 + self.c

    def at(self, x=None, z=None, c=None, y=None):
        x = self.x if x is None else x
        z = self.z if z is None else z
        c = self.c if c is None else c
        return (x * 8 + z * 2 + c, self.y if y is None else y)

    def sibling(self):
        return self.at(c=1 - self.c)

    def column(self, d):
        return turn(self.y, d // 2), (self.c + d % 2) % 2 if d % 2 == 0 else 1 - self.c

    def flat(self, d):
        p = lax.rem(self.plane + (d % 16), 16)
        return self.at(x=lax.div(p, 4), z=lax.rem(p, 4))


class Net:
    def __init__(self, send, recv, local):
        self.send, self.recv, self.near = send, recv, local
        self.names, self.sent, self.kept = {}, [], []

    def slot(self, name):
        assert len(self.names) < self.recv.shape[0] and len(self.sent) <= self.send.shape[0]
        return self.names.setdefault(name, len(self.names))

    def go(self, src, dst, to, name):
        copy = pltpu.make_async_remote_copy(
            src_ref=src,
            dst_ref=dst,
            send_sem=self.send.at[len(self.sent)],
            recv_sem=self.recv.at[self.slot(name)],
            device_id=to,
            device_id_type=MESH,
        )
        copy.start()
        self.sent.append(copy)
        return copy

    def many(self, copies, pieces):
        waits = []
        for src, dst, to, name in copies:
            waits.append(
                pltpu.make_async_remote_copy(
                    src_ref=src,
                    dst_ref=dst,
                    send_sem=self.send.at[len(self.sent)],
                    recv_sem=self.recv.at[self.slot(name)],
                    device_id=to,
                    device_id_type=MESH,
                )
            )
            self.sent.append(waits[-1])
        first = len(self.sent) - len(copies)
        for piece in range(pieces):
            for i, (src, dst, to, name) in enumerate(copies):
                rows = src.shape[-2] // pieces
                at = (slice(None),) * (len(src.shape) - 2) + (pl.ds(rows * piece, rows),)
                pltpu.make_async_remote_copy(
                    src_ref=src.at[at],
                    dst_ref=dst.at[at],
                    send_sem=self.send.at[first + i],
                    recv_sem=self.recv.at[self.slot(name)],
                    device_id=to,
                    device_id_type=MESH,
                ).start()
        return waits

    def take(self, dst, name, to):
        pltpu.make_async_remote_copy(
            src_ref=dst,
            dst_ref=dst,
            send_sem=self.send.at[0],
            recv_sem=self.recv.at[self.slot(name)],
            device_id=to,
            device_id_type=MESH,
        ).wait_recv()

    def local(self, src, dst):
        assert len(self.kept) < self.near.shape[0]
        copy = pltpu.make_async_copy(src, dst, self.near.at[len(self.kept)])
        copy.start()
        self.kept.append(copy)
        return copy

    def drain(self, but=()):
        for copy in self.sent:
            if all(copy is not other for other in but):
                copy.wait_send()


def greet(peers, extra=0):
    barrier = pltpu.get_barrier_semaphore()
    for peer in peers:
        pl.semaphore_signal(barrier, inc=1, device_id=peer, device_id_type=MESH)
    return barrier


def add_into(out, terms):
    rows = out.shape[-2]
    lead = [()]
    for extent in out.shape[:-2]:
        lead = [one + (i,) for one in lead for i in range(extent)]
    for one in lead:

        def step(i, _):
            at = pl.ds(pl.multiple_of(i * 16, 16), 16)
            if len(terms) == 2:
                total = terms[0][one + (at, slice(None))] + terms[1][one + (at, slice(None))]
            else:
                total = terms[0][one + (at, slice(None))].astype(F32)
                for term in terms[1:]:
                    total = total + term[one + (at, slice(None))].astype(F32)
            out[one + (at, slice(None))] = total.astype(out.dtype)
            return 0

        lax.fori_loop(0, rows // 16, step, 0, unroll=2)


class GatherColumn:
    def __init__(self, net, me, g, tag):
        self.net, self.me, self.g, self.tag = net, me, g, tag
        self.sent = []

    def go(self, *what):
        self.sent.append(self.net.go(*what))

    def block(self, dy, k, c):
        return self.g.at[2 * turn(self.me.y, dy) + k, c]

    def start(self, src):
        me, net, tag = self.me, self.net, self.tag
        copies = []
        for k in range(2):
            copies.append((src.at[k], self.block(0, k, me.c), me.at(y=turn(me.y, 1)), (tag, "ring", -1, k)))
            copies.append((src.at[1 - k], self.block(0, 1 - k, me.c), me.at(y=turn(me.y, -1)), (tag, "ring", 1, 1 - k)))
            copies.append((src.at[k], self.block(0, k, me.c), me.sibling(), (tag, "sib", 0, k)))
        for group in (copies[:3], copies[3:]):
            self.sent += net.many(group, 1)
        self.own = net.local(src, self.g.at[pl.ds(2 * me.y, 2), me.c])

    def relay(self, halves=(0, 1)):
        me, net, tag = self.me, self.net, self.tag
        for first in halves:
            copies = []
            for dy in (-1, 1):
                k = first if dy == -1 else 1 - first
                here = self.block(dy, k, me.c)
                net.take(here, (tag, "ring", dy, k), me.sibling())
                if first == 0:
                    copies.append((here, here, me.at(y=turn(me.y, -dy)), (tag, "far", k)))
                copies.append((here, here, me.sibling(), (tag, "sib", dy, k)))
            self.sent += net.many(copies, 1)

    def last(self):
        me, net, tag = self.me, self.net, self.tag
        for k in range(2):
            here = self.block(2, k, me.c)
            net.take(here, (tag, "far", k), me.sibling())
            self.go(here, here, me.sibling(), (tag, "sib", 2, k))

    def whole(self, dy):
        me, net, tag = self.me, self.net, self.tag
        if dy == 0:
            self.own.wait()
        for k in range(2):
            net.take(self.block(dy, k, 1 - me.c), (tag, "sib", dy, k), me.sibling())

    def finish(self):
        for dy in (0, -1, 1, 2):
            self.whole(dy)


class ReduceColumn:
    def __init__(self, net, me, part, pair, far, side, tag):
        self.net, self.me, self.tag = net, me, tag
        self.part, self.pair, self.far, self.side = part, pair, far, side
        self.sent = []

    def go(self, *what):
        self.sent.append(self.net.go(*what))

    def drain(self):
        for copy in self.sent:
            copy.wait_send()

    def mine(self, dy):
        return self.part.at[pl.ds(2 * turn(self.me.y, dy), 2), self.me.c]

    def one(self, dy, k):
        return self.part.at[2 * turn(self.me.y, dy) + k, self.me.c]

    def send_pair(self, dy):
        me = self.me
        src = self.part.at[pl.ds(2 * turn(me.y, dy), 2), 1 - me.c]
        self.go(src, self.pair.at[dy % 4], me.sibling(), (self.tag, "pair", dy % 4))

    def take_pair(self, dy):
        me, net, tag = self.me, self.net, self.tag
        net.take(self.pair.at[dy % 4], (tag, "pair", dy % 4), me.sibling())
        add_into(self.mine(dy), (self.mine(dy), self.pair.at[dy % 4]))
        above, below = me.at(y=turn(me.y, 1)), me.at(y=turn(me.y, -1))
        if dy == 2:
            self.go(self.one(2, 0), self.far.at[0], above, (tag, "far", 0))
            self.go(self.one(2, 1), self.far.at[1], below, (tag, "far", 1))
        elif dy == 1:
            self.go(self.one(1, 1), self.side.at[0, 1], above, (tag, "side", 0, 1))
        elif dy == -1:
            self.go(self.one(-1, 0), self.side.at[1, 0], below, (tag, "side", 1, 0))

    def relay(self):
        me, net, tag = self.me, self.net, self.tag
        above, below = me.at(y=turn(me.y, 1)), me.at(y=turn(me.y, -1))
        net.take(self.far.at[0], (tag, "far", 0), below)
        add_into(self.one(1, 0), (self.one(1, 0), self.far.at[0]))
        self.go(self.one(1, 0), self.side.at[0, 0], above, (tag, "side", 0, 0))
        net.take(self.far.at[1], (tag, "far", 1), above)
        add_into(self.one(-1, 1), (self.one(-1, 1), self.far.at[1]))
        self.go(self.one(-1, 1), self.side.at[1, 1], below, (tag, "side", 1, 1))

    def arrive(self):
        for way in range(2):
            for k in range(2):
                self.net.take(self.side.at[way, k], (self.tag, "side", way, k), self.me.sibling())

    def total(self, k, at):
        return (
            self.one(0, k)[at, :].astype(F32)
            + self.side[0, k, at, :].astype(F32)
            + self.side[1, k, at, :].astype(F32)
        )


class GatherPlane:
    def __init__(self, net, me, g, tag, pieces):
        self.net, self.me, self.g, self.tag, self.pieces = net, me, g, tag, pieces
        self.sent = []

    def block(self, h, da, db):
        me = self.me
        if h == 0:
            return self.g.at[turn(me.x, db), turn(me.z, da), 0]
        return self.g.at[turn(me.x, da), turn(me.z, db), 1]

    def peer(self, h, da, db):
        me = self.me
        if h == 0:
            return me.at(x=turn(me.x, db), z=turn(me.z, da))
        return me.at(x=turn(me.x, da), z=turn(me.z, db))

    def copy(self, h, da, db, step_a, step_b, rows=None):
        here = self.block(h, da, db)
        name = (self.tag, h, (da - step_a) % 4, (db - step_b) % 4)
        if rows is not None:
            here = here.at[pl.ds(32 * rows, 32)]
            name += (rows,)
        return (here, here, self.peer(h, step_a, step_b), name)

    def send(self, copies):
        self.sent += self.net.many([self.copy(*one) for one in copies], self.pieces)

    def take(self, h, da, db, rows=None):
        here = self.block(h, da, db)
        name = (self.tag, h, da % 4, db % 4)
        if rows is not None:
            here = here.at[pl.ds(32 * rows, 32)]
            name += (rows,)
        self.net.take(here, name, self.me.sibling())

    def start(self):
        self.send([(h, 0, 0, step, 0) for h in range(2) for step in (1, -1)])
        self.send([(h, 0, 0, 0, step) for h in range(2) for step in (1, -1)])

    def second(self):
        for h in range(2):
            self.take(h, -1, 0)
            self.take(h, 1, 0)
        self.send(
            [(h, -step, 0, step, 0, 0 if step == 1 else 1) for h in range(2) for step in (1, -1)]
        )
        for da in (-1, 1):
            self.send([(h, da, 0, 0, step) for h in range(2) for step in (1, -1)])

    def third(self):
        for h in range(2):
            self.take(h, 0, -1)
            self.take(h, 0, 1)
        self.send([(h, 0, -1, 0, 1) for h in range(2)])
        for h in range(2):
            self.take(h, 2, 0, rows=0)
            self.take(h, 2, 0, rows=1)
        self.send([(h, 2, 0, 0, step) for h in range(2) for step in (1, -1)])

    def fourth(self):
        for h in range(2):
            self.take(h, -1, -1)
            self.take(h, -1, 1)
            self.take(h, 1, -1)
            self.take(h, 1, 1)
        self.send([(h, da, 1, 0, -1) for da in (-1, 1) for h in range(2)])

    def fifth(self):
        for h in range(2):
            self.take(h, 2, -1)
            self.take(h, 2, 1)
        self.send([(h, 2, -1, 0, 1) for h in range(2)])

    def finish(self):
        for h in range(2):
            for da in (0, -1, 1, 2):
                self.take(h, da, 2)


class ReducePlane:
    def __init__(self, net, me, g, far, side, far2, side2, tag):
        self.net, self.me, self.g, self.tag = net, me, g, tag
        self.far, self.side, self.far2, self.side2 = far, side, far2, side2

    def super(self, h, db, lo, g=None):
        me = self.me
        g = self.g if g is None else g
        if h == 0:
            return g.at[turn(me.x, db), pl.ds(lo, 2), 0]
        return g.at[pl.ds(lo, 2), turn(me.z, db), 1]

    def whole(self, h, a):
        me = self.me
        return self.g.at[me.x, a, 0] if h == 0 else self.g.at[a, me.z, 1]

    def along(self, h, db):
        me = self.me
        return me.at(x=turn(me.x, db)) if h == 0 else me.at(z=turn(me.z, db))

    def across(self, h, da):
        me = self.me
        return me.at(z=turn(me.z, da)) if h == 0 else me.at(x=turn(me.x, da))

    def start(self, g=None):
        net, tag = self.net, self.tag
        far, side = [], []
        for h in range(2):
            far.append((self.super(h, 2, 0, g), self.far.at[h, 0], self.along(h, 1), (tag, h, "far", 0)))
            far.append((self.super(h, 2, 2, g), self.far.at[h, 1], self.along(h, -1), (tag, h, "far", 1)))
            to = self.side.at[h, 0, pl.ds(2, 2)]
            side.append((self.super(h, 1, 2, g), to, self.along(h, 1), (tag, h, "side", 0, 1)))
            to = self.side.at[h, 1, pl.ds(0, 2)]
            side.append((self.super(h, -1, 0, g), to, self.along(h, -1), (tag, h, "side", 1, 0)))
        net.many(far, 1)
        net.many(side, 1)

    def second(self):
        net, tag = self.net, self.tag
        for h in range(2):
            for way in range(2):
                here = self.far.at[h, way]
                net.take(here, (tag, h, "far", way), self.me.sibling())
                step = 1 if way == 0 else -1
                add_into(here, (here, self.super(h, step, 2 * way)))
                net.go(
                    here, self.side.at[h, way, pl.ds(2 * way, 2)], self.along(h, step), (tag, h, "side", way, way)
                )

    def third(self):
        net, tag = self.net, self.tag
        for h in range(2):
            for way in range(2):
                for lo in range(2):
                    here = self.side.at[h, way, pl.ds(2 * lo, 2)]
                    net.take(here, (tag, h, "side", way, lo), self.me.sibling())
        me = self.me
        for h in range(2):
            mine = me.z if h == 0 else me.x
            for da in (2, 1, -1, 0):
                a = turn(mine, da)
                here = self.side.at[h, 0, a]
                add_into(here, (here, self.side.at[h, 1, a], self.whole(h, a)))
                if da == 2:
                    for way in range(2):
                        net.go(
                            here.at[pl.ds(32 * way, 32)],
                            self.far2.at[h, way],
                            self.across(h, 1 if way == 0 else -1),
                            (tag, h, "far2", way),
                        )
                elif da != 0:
                    way = 0 if da == 1 else 1
                    rows = pl.ds(32 * (1 - way), 32)
                    net.go(
                        here.at[rows], self.side2.at[h, way, rows], self.across(h, da), (tag, h, "side2", way, 1 - way)
                    )

    def fourth(self):
        net, tag, me = self.net, self.tag, self.me
        for h in range(2):
            mine = me.z if h == 0 else me.x
            for way in range(2):
                here = self.far2.at[h, way]
                net.take(here, (tag, h, "far2", way), me.sibling())
                da = 1 if way == 0 else -1
                rows = pl.ds(32 * way, 32)
                add_into(here, (here, self.side.at[h, 0, turn(mine, da), rows]))
                net.go(here, self.side2.at[h, way, rows], self.across(h, da), (tag, h, "side2", way, way))

    def finish(self):
        net, tag, me = self.net, self.tag, self.me
        for h in range(2):
            mine = me.z if h == 0 else me.x
            for way in range(2):
                for part in range(2):
                    here = self.side2.at[h, way, pl.ds(32 * part, 32)]
                    net.take(here, (tag, h, "side2", way, part), me.sibling())
            here = self.side2.at[h, 0]
            add_into(here, (here, self.side2.at[h, 1], self.side.at[h, 0, mine]))


def column_peers(me):
    peers = []
    for d in range(1, 8):
        y, c = me.column(d)
        peers.append(me.at(y=y, c=c))
    return peers


def one_less_exp(t, plain):
    series = 1.0 - t * (1.0 / 8.0)
    for k in range(7, 1, -1):
        series = 1.0 - t * (1.0 / k) * series
    return jnp.where(t < 0.5, t * series, plain)


def decay_parts(rate, log_scale, resets):
    log_decay = rate * log_scale
    a = jnp.exp(log_decay)
    margin = one_less_exp(-2.0 * log_decay, 1.0 - a * a)
    scale = jnp.where(resets > 0.5, 1.0, jnp.sqrt(jnp.maximum(margin, FLOOR_VALUE)))
    return a, a * (1.0 - resets), scale, margin


def log_scale_row(vec):
    return -8.0 * jax.nn.softplus(-vec[7:8, :])


STEP = 32


def blocks(first, count, body):
    def one(i, _):
        row, j = first + lax.div(i, 128 // STEP), lax.rem(i, 128 // STEP)
        at = pl.ds(pl.multiple_of(j * STEP, STEP), STEP)
        body(row, j, at)
        return 0

    lax.fori_loop(0, count * (128 // STEP), one, 0, unroll=2)


def mask_block(masks, row, j):
    inner = 64 // STEP
    at = pl.ds(pl.multiple_of(lax.rem(j, inner) * STEP, STEP), STEP)
    return masks[row, lax.div(j, inner), at, :].astype(F32)


def lanes_below(shape, limit):
    return lax.broadcasted_iota(jnp.int32, shape, len(shape) - 1) < limit


def forward_kernel(
    px, py, po, wg, wu, wd, tokens_in, cot_in, seg, rate_in, input_in, odds_in,
    p_out, one_out, mask_out, gain_out, vec_out, riw_out, ce_out,
    pre_out, co_out, rt_out, ig_out, st_out, carry_out, mix_out, gf_out, gd_out, gb_out, pout_out, res_out, gres_out, gain2_out,
    pxl, pyl, pol, wp, rate_l, input_l, odds, sm, x1, gt, gpart,
    pbuf, wf, xg, sg, small, riw, vec, gains, ce, pre, co, rt, ig, fa, st, mix, car, carry, pair, far, side, res, two, xo,
    s2, ct, cot, hid, gu, pout, gb, gres, gain2, flip, far_d, side_d, far2_d, side2_d,
    send, recv, local, ssend, srecv,
):
    me = Place()
    net = Net(send, recv, local)
    loads = [
        net.local(a, b)
        for a, b in (
            (px, pxl), (py, pyl), (po, pol), (odds_in, odds), (rate_in, rate_l), (input_in, input_l), (tokens_in, xo), (cot_in, cot)
        )
    ]
    to_y, to_c, index = me.x, lax.div(me.z, 2), lax.rem(me.z, 2) * 8 + me.c * 4 + me.y
    mine = jnp.logical_and(to_y == me.y, to_c == me.c)

    def small_from(j):
        return me.at(x=me.y, z=2 * me.c + j // 8, c=(j // 4) % 2, y=j % 4)

    def small_to(p):
        return me.at(x=p // 4, z=p % 4, c=to_c, y=to_y)

    barrier = greet(column_peers(me) + [me.flat(d) for d in range(1, 16)])
    for i in range(16):

        @pl.when(jnp.logical_not(jnp.logical_and(mine, me.plane == i)))
        def _():
            pl.semaphore_signal(barrier, inc=1, device_id=small_to(i), device_id_type=MESH)

        @pl.when(jnp.logical_not(jnp.logical_and(mine, index == i)))
        def _():
            pl.semaphore_signal(barrier, inc=1, device_id=small_from(i), device_id_type=MESH)

    spot = lax.broadcasted_iota(jnp.int32, (64, 128), 0) + (me.plane * 2 + me.c) * 64
    lane = lax.broadcasted_iota(jnp.int32, (64, 128), 1)
    for k in range(2):
        reset, crossed = jnp.zeros((64, 128), F32), jnp.zeros((64, 128), F32)
        for j in range(4):
            start = seg[k, j]
            reset = jnp.where(spot == start, 1.0, reset)
            crossed = jnp.where(jnp.logical_and(start <= spot, start > spot - lane), 1.0, crossed)
        usable = jnp.where(jnp.logical_and(lane <= 3, spot >= lane), 1.0 - crossed, 0.0)
        x1[k, :, 2048:TOK] = jnp.where(lane == 0, reset, usable).astype(BF)

    for copy in loads[:6]:
        copy.wait()
    zeros = jnp.zeros((16, 256), F32)
    for t in range(8):
        low, shift = 128 * (CH * t // 128), CH * t % 128

        def window(ref):
            wide = ref[:, low : low + WIDE].astype(F32)
            wide = pltpu.roll(wide, WIDE - shift, 1) if shift else wide
            return jnp.where(lanes_below((16, WIDE), CH), wide, 0.0)

        both = jnp.concatenate([window(pxl), zeros], axis=1)
        both = both + pltpu.roll(jnp.concatenate([window(pyl), zeros], axis=1), CH, 1)
        wp[t, :, 0:640] = both.astype(BF)
        wp[t, :, 640:PK] = window(pol).astype(BF)
    small[0:32, :] = jnp.zeros((32, WIDE), F32)
    small[0:20, 0:160] = rate_l[...].astype(F32)
    left = small[0:32, :]
    small[0:20, 0:160] = input_l[...].astype(F32)
    left = left + pltpu.roll(small[0:32, :], 160, 1)
    small[0:32, :] = left
    small[24:32, 0:128] = odds[0:8, :]
    sm[...] = small[0:32, :].astype(BF)
    gt[...] = pltpu.roll(odds[8:16, :], me.c * 64 + me.y * 16, 1)
    pl.semaphore_wait(barrier, 22 + 32 - 2 * mine.astype(jnp.int32))

    def p_block(y, c):
        return pbuf.at[me.x, me.z, c, pl.ds(pl.multiple_of(16 * y, 16), 16)]

    def f_block(y, c, k):
        rows = pl.ds(pl.multiple_of(16 * y, 16), 16)
        return wf.at[me.x, me.z, c, rows, pl.ds(HID * k, HID)]

    def features(p):
        return pl.ds(pl.multiple_of(128 * p, 128), 128)

    for d in range(1, 8):
        y, c = me.column(d)
        net.go(gt, gpart.at[d], me.at(y=y, c=c), ("gain8", d))
    for d in range(1, 8):
        y, c = me.column(d)
        net.go(wp.at[2 * y + c], p_block(me.y, me.c), me.at(y=y, c=c), ("wp", d))
    own_p = net.local(wp.at[me.part], p_block(me.y, me.c))
    total = gt[...]
    for d in range(1, 8):
        net.take(gpart.at[d], ("gain8", d), me.sibling())
        total = total + gpart[d]
    gpart[0] = total
    gains[:, features(me.plane)] = total
    for d in range(1, 16):
        net.go(gpart.at[0], gains.at[:, features(me.plane)], me.flat(d), ("gain", d))

    def source(d):
        return turn(me.y, -(d // 2)), me.c if d % 2 == 0 else 1 - me.c

    for d in range(1, 8):
        net.take(p_block(*source(d)), ("wp", d), me.sibling())
    own_p.wait()
    proj = GatherPlane(net, me, pbuf.at[:, :, :, :, pl.ds(0, 640)], "p", 1)
    outp = GatherPlane(net, me, pbuf.at[:, :, :, :, pl.ds(640, WIDE)], "o", 1)
    proj.start()
    loads[6].wait()
    for d in range(1, 16):
        net.take(gains.at[:, features(lax.rem(me.plane + 16 - d, 16))], ("gain", d), me.sibling())
    for k in range(2):

        def norm_step(i, _):
            at = pl.ds(pl.multiple_of(i * 16, 16), 16)
            x = xo[k, at, :].astype(F32)
            scale = lax.rsqrt(jnp.mean(x * x, axis=-1, keepdims=True) + EPSILON)
            x1[k, at, 0:2048] = (x * scale * gains[0:1, :]).astype(BF)
            return 0

        lax.fori_loop(0, 4, norm_step, 0, unroll=2)
    tokens = GatherColumn(net, me, xg, "x")
    tokens.start(x1)
    proj.second()
    outp.start()

    def small_copy(i):
        return pltpu.make_async_remote_copy(
            src_ref=sm,
            dst_ref=sg.at[index],
            send_sem=ssend.at[i],
            recv_sem=srecv.at[index],
            device_id=small_to(i),
            device_id_type=MESH,
        )

    for i in range(16):
        own = jnp.logical_and(mine, me.plane == i)

        @pl.when(jnp.logical_not(own))
        def _():
            small_copy(i).start()

        @pl.when(own)
        def _():
            pltpu.make_async_copy(sm, sg.at[index], srecv.at[index]).start()

    tokens.relay((0,))
    for d in range(1, 8):
        y, c = me.column(d)
        for k, w in enumerate((wg, wu, wd)):
            cols = pl.ds(pl.multiple_of(HID * (2 * y + c), HID), HID)
            net.go(w.at[:, cols], f_block(me.y, me.c, k), me.at(y=y, c=c), ("wf", d, k))
    own_f = []
    for k, w in enumerate((wg, wu, wd)):
        cols = pl.ds(pl.multiple_of(HID * me.part, HID), HID)
        own_f.append(net.local(w.at[:, cols], f_block(me.y, me.c, k)))
    proj.third()
    tokens.relay((1,))
    proj.fourth()
    outp.second()
    tokens.last()
    proj.fifth()
    for d in range(1, 8):
        for k in range(3):
            net.take(f_block(*source(d), k), ("wf", d, k), me.sibling())
    for copy in own_f:
        copy.wait()
    feed = GatherPlane(net, me, wf, "f", 1)
    feed.start()
    loads[7].wait()
    cots = GatherColumn(net, me, ct, "c")
    cots.start(cot)

    small[...] = jnp.zeros_like(small)
    for j in range(16):

        @pl.when(jnp.logical_not(jnp.logical_and(mine, index == j)))
        def _():
            pltpu.make_async_remote_copy(
                src_ref=sm,
                dst_ref=sg.at[j],
                send_sem=ssend.at[0],
                recv_sem=srecv.at[j],
                device_id=me.sibling(),
                device_id_type=MESH,
            ).wait_recv()

        @pl.when(jnp.logical_and(mine, index == j))
        def _():
            pltpu.make_async_copy(sm, sg.at[j], srecv.at[j]).wait()

    vectors = jnp.zeros((8, WIDE), F32)
    inside = lanes_below((8, WIDE), 20)
    for j in range(16):
        block = sg[j].astype(F32)
        small[20 * j : 20 * j + 20, :] = block[0:20, :]
        vectors = vectors + pltpu.roll(jnp.where(inside, block[24:32, :], 0.0), 20 * j, 1)
    vec[...] = vectors
    rows = lax.broadcasted_iota(jnp.int32, (WIDE, WIDE), 0)
    lanes = lax.broadcasted_iota(jnp.int32, (WIDE, WIDE), 1)
    held = small[...]
    first = jnp.logical_and(rows < 160, lanes < 160)
    second = jnp.logical_and(jnp.logical_and(rows >= 160, rows < CH), jnp.logical_and(lanes >= 160, lanes < CH))
    riw[:, 0:WIDE] = (jnp.where(first, held, 0.0) + jnp.where(second, pltpu.roll(held, 160, 1), 0.0)).astype(BF)
    riw[:, WIDE:] = (
        jnp.where(first, pltpu.roll(held, WIDE - 160, 1), 0.0) + jnp.where(second, held, 0.0)
    ).astype(BF)
    proj.finish()
    tokens.finish()
    masks = xg.at[:, :, :, pl.ds(2048, 128)]

    def project(i, _):
        at = pl.ds(2 * i, 2)
        left = xg[at, :, :, 0:2048].reshape(256, 2048)
        both = dot(left, pbuf[:, :, :, :, 0:640].reshape(2048, 640))
        low = jnp.where(lanes_below((256, WIDE), CH), both[:, 0:WIDE], 0.0).astype(BF)
        ce[at, 16:144, :] = low.reshape(2, 128, WIDE)
        right = jnp.where(lanes_below((256, WIDE), CH), pltpu.roll(both[:, 256:640], WIDE - 64, 1), 0.0)
        pre[at] = right.reshape(2, 128, WIDE)
        return 0

    lax.fori_loop(0, 4, project, 0)
    for copy in tokens.sent:
        copy.wait_send()
    wide = xg.at[:, :, :, pl.ds(0, 2048)]
    save_one = net.local(wide, one_out)
    net.go(ce.at[:, pl.ds(128, 16)], ce.at[:, pl.ds(0, 16)], me.flat(1), "halo")
    outp.third()
    cots.relay()
    net.take(ce.at[:, pl.ds(0, 16)], "halo", me.sibling())

    def convolve(row, j, at):
        wide = ce[row, pl.ds(pl.multiple_of(j * STEP, STEP), STEP + 16), :].astype(F32)
        valid = mask_block(masks, row, j)
        total = jnp.broadcast_to(vec[4:5, :], (STEP, WIDE))
        for k in range(4):
            piece = wide[16 - k : 16 - k + STEP, :]
            if k > 0:
                piece = piece * valid[:, k : k + 1]
            total = total + vec[k : k + 1, :] * piece
        co[row, at, :] = total

    blocks(0, 8, convolve)
    outp.fourth()
    feed.second()

    def gates(i, _):
        at = pl.ds(4 * i, 4)
        both = dot(co[at].reshape(512, WIDE).astype(BF), riw[...])
        rt[at] = both[:, 0:WIDE].reshape(4, 128, WIDE)
        ig[at] = both[:, WIDE:].reshape(4, 128, WIDE)
        return 0

    lax.fori_loop(0, 2, gates, 0)
    log_scale = log_scale_row(vec)

    def decays(row, j, at):
        rate = jax.nn.sigmoid(rt[row, at, :] + vec[5:6, :])
        gate = jax.nn.sigmoid(ig[row, at, :] + vec[6:7, :])
        _, factor, scale, _ = decay_parts(rate, log_scale, mask_block(masks, row, j)[:, 0:1])
        rt[row, at, :] = rate
        ig[row, at, :] = gate
        fa[row, at, :] = factor
        st[row, at, :] = scale * (gate * co[row, at, :])

    blocks(0, 8, decays)
    cots.last()
    outp.fifth()

    def scan(i, held):
        h, q = held
        at = pl.ds(pl.multiple_of(i * 8, 8), 8)
        f, d = jnp.swapaxes(fa[:, at, :], 0, 1), jnp.swapaxes(st[:, at, :], 0, 1)
        hs, qs = [], []
        for k in range(8):
            h, q = f[k] * h + d[k], q * f[k]
            hs.append(h)
            qs.append(q)
        st[:, at, :] = jnp.swapaxes(jnp.stack(hs), 0, 1)
        fa[:, at, :] = jnp.swapaxes(jnp.stack(qs), 0, 1)
        return h, q

    h, q = lax.fori_loop(0, 16, scan, (jnp.zeros((8, WIDE), F32), jnp.ones((8, WIDE), F32)), unroll=2)
    car[me.plane, 0] = q
    car[me.plane, 1] = h
    for d in range(1, 16):
        net.go(car.at[me.plane], car.at[me.plane], me.flat(d), ("carry", d))
    feed.third()
    for d in range(1, 16):
        net.take(car.at[lax.rem(me.plane + 16 - d, 16)], ("carry", d), me.sibling())
    h = jnp.zeros((8, WIDE), F32)
    for k in range(15):
        h = jnp.where(k < me.plane, car[k, 0] * h + car[k, 1], h)
    carry[...] = h
    branch = ReduceColumn(net, me, wide, pair, far, side, "branch")
    save_one.wait()
    outp.finish()

    def outward(dy):
        first = 2 * turn(me.y, dy)

        def mixing(row, j, at):
            states = st[row, at, :] + fa[row, at, :] * carry[pl.ds(row, 1), :]
            st[row, at, :] = states
            mix[row, at, :] = (states * gelu(pre[row, at, :])).astype(BF)

        blocks(first, 2, mixing)
        at = pl.ds(first, 2)

        def onto(n, _):
            low = dot_last(mix[at].reshape(256, WIDE), pbuf[n, :, :, :, 640:1024].reshape(512, WIDE)).astype(BF)
            xg[at, :, :, pl.ds(pl.multiple_of(512 * n, 512), 512)] = low.reshape(2, 2, 64, 512)
            return 0

        lax.fori_loop(0, 4, onto, 0)
        branch.send_pair(dy)

    outward(2)
    outward(1)
    branch.take_pair(2)
    feed.fourth()
    outward(-1)
    branch.take_pair(1)
    outward(0)
    branch.take_pair(-1)
    keep = [
        net.local(src, dst)
        for src, dst in (
            (rt, rt_out), (ig, ig_out), (co, co_out), (pbuf, p_out), (masks, mask_out), (gains, gain_out),
            (vec, vec_out), (riw, riw_out), (ce, ce_out), (pre, pre_out), (st, st_out), (carry, carry_out),
            (mix, mix_out),
        )
    ]
    branch.relay()
    branch.take_pair(0)
    feed.fifth()
    branch.arrive()
    for k in range(2):

        def close_branch(i, _):
            at = pl.ds(pl.multiple_of(i * 16, 16), 16)
            value = xo[k, at, :].astype(F32) + branch.total(k, at)
            res[k, at, :] = value
            scale = lax.rsqrt(jnp.mean(value * value, axis=-1, keepdims=True) + EPSILON)
            two[k, at, :] = (value * scale * gains[1:2, :]).astype(BF)
            return 0

        lax.fori_loop(0, 4, close_branch, 0, unroll=2)
    branch.drain()
    scaled = GatherColumn(net, me, s2, "two")
    scaled.start(two)
    cots.finish()
    for copy in keep[:3]:
        copy.wait()
    feed.finish()

    def ahead(dy):
        yy = turn(me.y, dy)
        at = pl.ds(2 * yy, 2)
        for ref, left, k in ((rt, s2, 0), (ig, s2, 1), (co, ct, 2)):
            product = dot(left[at].reshape(256, 2048), wf[:, :, :, :, HID * k : HID * (k + 1)].reshape(2048, HID))
            ref[0:2] = product[:, 0:WIDE].reshape(2, 128, WIDE)
            ref[2:4] = product[:, WIDE:].reshape(2, 128, WIDE)

        def bend(j, _):
            row = lax.div(j, 8)
            here = pl.ds(pl.multiple_of(16 * lax.rem(j, 8), 16), 16)
            rows = pl.ds(pl.multiple_of(256 * yy + 16 * j, 16), 16)
            for half in range(2):
                lanes = slice(WIDE * half, WIDE * (half + 1))
                up, grad = ig[2 * half + row, here, :], co[2 * half + row, here, :]
                act, slant = gelu_and_slope(rt[2 * half + row, here, :])
                hid[rows, lanes] = (act * up).astype(BF)
                gu[rows, lanes] = (grad * (up * slant)).astype(BF)
                gu[rows, HID + WIDE * half : HID + WIDE * (half + 1)] = (grad * act).astype(BF)
            return 0

        lax.fori_loop(0, 16, bend, 0)

    scaled.whole(0)
    ahead(0)
    scaled.relay()
    scaled.whole(1)
    ahead(1)
    scaled.last()
    scaled.whole(-1)
    ahead(-1)
    scaled.whole(2)
    ahead(2)
    slope = ReduceColumn(net, me, wide, pair, far, side, "slope")

    def inner(dy):
        yy = turn(me.y, dy)
        rows = pl.ds(pl.multiple_of(256 * yy, 256), 256)

        def out(n, _):
            low = dot_last(gu[rows, :], wf[n, :, :, :, 0:FG].reshape(512, FG))
            at = pl.ds(pl.multiple_of(512 * n, 512), 512)
            xg[pl.ds(2 * yy, 2), :, :, at] = low.astype(BF).reshape(2, 2, 64, 512)
            return 0

        lax.fori_loop(0, 4, out, 0)
        slope.send_pair(dy)

    def down(dy):
        yy = turn(me.y, dy)
        rows = pl.ds(pl.multiple_of(256 * yy, 256), 256)

        def out(n, _):
            low = dot_last(hid[rows, :], wf[n, :, :, :, 2 * HID :].reshape(512, HID)).astype(BF)
            pout[pl.ds(2 * yy, 2), :, :, pl.ds(pl.multiple_of(512 * n, 512), 512)] = low.reshape(2, 2, 64, 512)
            return 0

        lax.fori_loop(0, 4, out, 0)

    inner(2)
    inner(1)
    slope.take_pair(2)
    inner(-1)
    slope.take_pair(1)
    inner(0)
    slope.take_pair(-1)
    down(2)
    slope.take_pair(0)
    slope.relay()

    def store(i):
        lanes = pl.ds(0, FG)
        return pltpu.make_async_copy(wf.at[i, :, :, :, lanes], gf_out.at[i], ssend.at[i])

    def columns(i):
        return pl.ds(pl.multiple_of(512 * i, 512), 512)

    def weights_down(i, _):
        flip[...] = jnp.transpose(ct[:, :, :, columns(i)].reshape(1024, 512))
        wf[i, :, :, :, FG:] = dot(flip[...], hid[...]).astype(BF).reshape(4, 2, 64, HID)
        return 0

    def weights(i, _):
        flip[...] = jnp.transpose(s2[:, :, :, columns(i)].reshape(1024, 512))
        for k in range(2):
            lanes = slice(HID * k, HID * (k + 1))
            wf[i, :, :, :, lanes] = dot(flip[...], gu[:, lanes]).astype(BF).reshape(4, 2, 64, HID)
        store(i).start()
        return 0

    under = ReducePlane(net, me, wf.at[:, :, :, :, pl.ds(FG, HID)], far_d, side_d, far2_d, side2_d, "d")

    down(1)
    down(-1)
    down(0)
    for i in range(16):

        @pl.when(jnp.logical_not(jnp.logical_and(mine, me.plane == i)))
        def _():
            small_copy(i).wait_send()

    gain2[...] = jnp.zeros_like(gain2)
    for copy in feed.sent:
        copy.wait_send()
    lax.fori_loop(0, 4, weights_down, 0)
    under.start()
    slope.arrive()
    for k in range(2):

        def close(i, _):
            at = pl.ds(pl.multiple_of(i * 16, 16), 16)
            value = res[k, at, :]
            scale = lax.rsqrt(jnp.mean(value * value, axis=-1, keepdims=True) + EPSILON)
            normed = value * scale
            got = slope.total(k, at)
            gain2[0:8, :] = gain2[0:8, :] + (got * normed).reshape(2, 8, 2048).sum(axis=0)
            v = got * gains[1:2, :]
            back = (v - normed * jnp.mean(v * normed, axis=-1, keepdims=True)) * scale
            total = cot[k, at, :].astype(F32) + back
            gres[k, at, :] = total
            gb[k, at, :] = total.astype(BF)
            return 0

        lax.fori_loop(0, 4, close, 0, unroll=2)
    back = GatherColumn(net, me, gb_out, "gb")
    back.start(gb)
    keep += [net.local(gres, gres_out), net.local(gain2, gain2_out), net.local(pout, pout_out), net.local(res, res_out)]
    under.second()
    lax.fori_loop(0, 2, weights, 0)
    back.relay((0,))
    under.third()
    lax.fori_loop(2, 3, weights, 0)
    back.relay((1,))
    lax.fori_loop(3, 4, weights, 0)
    back.last()
    under.fourth()
    under.finish()
    keep.append(net.local(side2_d.at[:, 0], gd_out))
    for i in range(4):
        store(i).wait()
    back.finish()
    for copy in keep[3:]:
        copy.wait()
    net.drain(tokens.sent + branch.sent + feed.sent)


def backward_kernel(
    gb_in, p_in, gf_in, one_in, mask_in, gain_in, vec_in, riw_in, ce_in, pre_in, co_in, rt_in, ig_in, st_in, mix_in,
    carry_in, gres_in, gain2_in, x_in, pout_in, res_in, gd_in,
    ff_out, fd_out, fo_out, fi_out, small_out, gains_out, gx_out, out_out,
    gb, w, gf, masks, gains, vec, riw, ce, pre, co, rt, ig, st, mix, carry, gres, gain2, xo,
    gm, fa, car, edge, z, sgr, srec, ssum, part, pair, far, side, pair2, far2, side2, res, out, far_f, side_f, far2_f, side2_f,
    far_o, side_o, far2_o, side2_o, far_i, side_i, far2_i, side2_i, ff, fd, fo, fi, grow, gsum, gtot, gall, gx, wacc, halo,
    send, recv, local, ssend, srecv,
):
    me = Place()
    net = Net(send, recv, local)
    loads = {
        name: net.local(a, b)
        for name, a, b in (
            ("part", pout_in, part), ("gb", gb_in, gb), ("w", p_in, w), ("pre", pre_in, pre), ("st", st_in, st), ("mix", mix_in, mix),
            ("rt", rt_in, rt), ("masks", mask_in, masks), ("vec", vec_in, vec), ("gf", gf_in, gf), ("co", co_in, co),
            ("ig", ig_in, ig), ("carry", carry_in, carry), ("riw", riw_in, riw), ("ce", ce_in, ce),
            ("gains", gain_in, gains), ("gres", gres_in, gres), ("gain2", gain2_in, gain2), ("x", x_in, xo), ("res", res_in, res),
        )
    }

    def need(*names):
        for name in names:
            loads[name].wait()

    to_y, to_c, index = me.x, lax.div(me.z, 2), lax.rem(me.z, 2) * 8 + me.c * 4 + me.y
    mine = jnp.logical_and(to_y == me.y, to_c == me.c)

    def small_to(j):
        return me.at(x=me.y, z=2 * me.c + j // 8, c=(j // 4) % 2, y=j % 4)

    def small_from(p):
        return me.at(x=p // 4, z=p % 4, c=to_c, y=to_y)

    barrier = greet(column_peers(me) + [me.flat(d) for d in range(1, 16)])
    for i in range(16):

        @pl.when(jnp.logical_not(jnp.logical_and(mine, me.plane == i)))
        def _():
            pl.semaphore_signal(barrier, inc=1, device_id=small_from(i), device_id_type=MESH)

        @pl.when(jnp.logical_not(jnp.logical_and(mine, index == i)))
        def _():
            pl.semaphore_signal(barrier, inc=1, device_id=small_to(i), device_id_type=MESH)

    pl.semaphore_wait(barrier, 22 + 32 - 2 * mine.astype(jnp.int32))
    feed = ReducePlane(net, me, gf, far_f, side_f, far2_f, side2_f, "f")
    result = ReduceColumn(net, me, part, pair2, far2, side2, "result")
    gpo, gpi = w.at[:, :, :, :, pl.ds(640, WIDE)], w.at[:, :, :, :, pl.ds(0, 640)]
    outer = ReducePlane(net, me, gpo, far_o, side_o, far2_o, side2_o, "o")
    inner = ReducePlane(net, me, gpi, far_i, side_i, far2_i, side2_i, "i")
    feed.start(gf_in)
    need("part")
    for dy in (2, 1, -1, 0):
        result.send_pair(dy)

    def share(source, dst, tag):
        for d in range(1, 8):
            y, c = me.column(d)
            src = source.at[c, pl.ds(pl.multiple_of(16 * y, 16), 16)]
            net.go(src, dst.at[me.part], me.at(y=y, c=c), (tag, d))
        src = source.at[me.c, pl.ds(pl.multiple_of(16 * me.y, 16), 16)]
        return net.local(src, dst.at[me.part])

    def collect(dst, tag):
        for d in range(1, 8):
            y = turn(me.y, -(d // 2))
            c = me.c if d % 2 == 0 else 1 - me.c
            net.take(dst.at[2 * y + c], (tag, d), me.sibling())

    own_d = share(gd_in, fd, "fd")
    need("gb", "w")

    def mix_back(i, _):
        at = pl.ds(4 * i, 4)
        grad = dot(gb[at].reshape(512, 2048), w[:, :, :, :, 640:1024].reshape(2048, WIDE))
        gm[at] = grad.reshape(4, 128, WIDE)
        return 0

    lax.fori_loop(0, 2, mix_back, 0)
    need("pre", "st", "rt", "masks", "vec")
    log_scale = log_scale_row(vec)

    def bend_back(row, j, at):
        act, slant = gelu_and_slope(pre[row, at, :])
        grad = jnp.where(lanes_below((STEP, WIDE), CH), gm[row, at, :], 0.0)
        low = grad * st[row, at, :] * slant
        z[row, at, 256:640] = pltpu.roll(low, 64, 1).astype(BF)
        gm[row, at, :] = grad * act
        _, factor, _, _ = decay_parts(rt[row, at, :], log_scale, mask_block(masks, row, j)[:, 0:1])
        fa[row, at, :] = factor

    blocks(0, 8, bend_back)

    def scan(step, held):
        g, m = held
        at = pl.ds(pl.multiple_of((15 - step) * 8, 8), 8)
        f, d = jnp.swapaxes(fa[:, at, :], 0, 1), jnp.swapaxes(gm[:, at, :], 0, 1)
        las, lps = [None] * 8, [None] * 8
        for k in range(7, -1, -1):
            la = d[k] + g
            las[k], lps[k] = la, m
            g, m = f[k] * la, f[k] * m
        gm[:, at, :] = jnp.swapaxes(jnp.stack(las), 0, 1)
        fa[:, at, :] = jnp.swapaxes(jnp.stack(lps), 0, 1)
        return g, m

    g, m = lax.fori_loop(0, 16, scan, (jnp.zeros((8, WIDE), F32), jnp.ones((8, WIDE), F32)), unroll=2)
    car[me.plane, 0] = m
    car[me.plane, 1] = g
    for d in range(1, 16):
        net.go(car.at[me.plane], car.at[me.plane], me.flat(d), ("carry", d))
    need("mix", "gf")

    def weight_out(i, _):
        left = gb[:, :, :, pl.ds(pl.multiple_of(512 * i, 512), 512)].reshape(1024, 512)
        w[i, :, :, :, 640:1024] = dot_first(left, mix[...].reshape(1024, WIDE)).astype(BF).reshape(4, 2, 64, WIDE)
        return 0

    lax.fori_loop(0, 4, weight_out, 0)
    load_one = net.local(one_in, gb)
    feed.second()
    outer.start()
    for dy in (2, 1, -1, 0):
        result.take_pair(dy)
    for d in range(1, 16):
        net.take(car.at[lax.rem(me.plane + 16 - d, 16)], ("carry", d), me.sibling())
    g = jnp.zeros((8, WIDE), F32)
    for k in range(15, 0, -1):
        g = jnp.where(k > me.plane, car[k, 1] + car[k, 0] * g, g)
    edge[...] = g
    wacc[...] = jnp.zeros_like(wacc)
    need("co", "ig", "carry", "riw", "ce")

    def fold(value):
        return value.reshape(STEP // 8, 8, WIDE).sum(axis=0)

    def gate_back(row, j, at):
        resets = mask_block(masks, row, j)[:, 0:1]
        adjoint = gm[row, at, :] + fa[row, at, :] * edge[pl.ds(row, 1), :]
        rate, gate, conv = rt[row, at, :], ig[row, at, :], co[row, at, :]
        a, factor, scale, margin = decay_parts(rate, log_scale, resets)
        before = st[row, pl.ds(pl.multiple_of(jnp.maximum(j * STEP - 8, 0), 8), 8), :]
        edge_row = jnp.where(j == 0, carry[pl.ds(row, 1), :], before[7:8, :])
        top = lax.broadcasted_iota(jnp.int32, (STEP, WIDE), 0) == 0
        previous = jnp.where(top, edge_row, pltpu.roll(st[row, at, :], 1, 0))
        grad_scale = adjoint * gate * conv
        free = jnp.logical_and(margin > FLOOR_VALUE, resets < 0.5)
        grad_log = adjoint * previous * factor - jnp.where(free, grad_scale * (a * a) / scale, 0.0)
        rate_pre = grad_log * log_scale * rate * (1.0 - rate)
        through = adjoint * scale
        gate_pre = through * conv * gate * (1.0 - gate)
        wacc[5] = wacc[5] + fold(rate_pre)
        wacc[6] = wacc[6] + fold(gate_pre)
        wacc[7] = wacc[7] + fold(grad_log * rate)
        gm[row, at, :] = through * gate
        rt[row, at, :] = rate_pre
        ig[row, at, :] = gate_pre

    blocks(0, 8, gate_back)
    result.relay()

    def through_gates(i, _):
        at = pl.ds(4 * i, 4)
        total = gm[at].reshape(512, WIDE)
        total = total + dot_last(rt[at].reshape(512, WIDE).astype(BF), riw[:, 0:WIDE])
        total = total + dot_last(ig[at].reshape(512, WIDE).astype(BF), riw[:, WIDE:])
        gm[at] = total.reshape(4, 128, WIDE)
        return 0

    lax.fori_loop(0, 2, through_gates, 0)

    def conv_back(row, j, at):
        wide = ce[row, pl.ds(pl.multiple_of(j * STEP, STEP), STEP + 16), :].astype(F32)
        valid = mask_block(masks, row, j)
        grad = gm[row, at, :]
        wacc[4] = wacc[4] + fold(grad)
        total = jnp.zeros((STEP + 8, WIDE), F32)
        for k in range(4):
            kept = grad if k == 0 else grad * valid[:, k : k + 1]
            wacc[k] = wacc[k] + fold(kept * wide[16 - k : 16 - k + STEP, :])
            scaled = kept * vec[k : k + 1, :]
            total = total + jnp.concatenate(
                [jnp.zeros((8 - k, WIDE), F32), scaled] + ([jnp.zeros((k, WIDE), F32)] if k else []), axis=0
            )
        fa[row, at, :] = total[8:, :]
        early = total[0:8, :]

        @pl.when(j == 0)
        def _():
            halo[0, row] = early

        @pl.when(j > 0)
        def _():
            last = pl.ds(pl.multiple_of(j * STEP - 8, 8), 8)
            fa[row, last, :] = fa[row, last, :] + early

    blocks(0, 8, conv_back)
    net.go(halo.at[0], halo.at[1], me.flat(-1), "halo")
    feed.third()
    outer.second()

    net.take(halo.at[1], "halo", me.sibling())

    def conv_in_back(row, j, at):
        grad = fa[row, at, :]
        tail = jnp.where(j == 128 // STEP - 1, halo[1, row], 0.0)
        grad = grad + jnp.concatenate([jnp.zeros((STEP - 8, WIDE), F32), tail], axis=0)
        z[row, at, 0:256] = grad[:, 0:256].astype(BF)
        late = jnp.where(lanes_below((STEP, 128), 64), grad[:, 256:384], z[row, at, 256:384].astype(F32))
        z[row, at, 256:384] = late.astype(BF)

    blocks(0, 8, conv_in_back)
    result.arrive()
    result.drain()
    need("res")
    for k in range(2):

        def close_result(i, _):
            at = pl.ds(pl.multiple_of(i * 16, 16), 16)
            out[k, at, :] = (res[k, at, :] + result.total(k, at)).astype(BF)
            return 0

        lax.fori_loop(0, 4, close_result, 0, unroll=2)
    save_out = net.local(out, out_out)
    entry = ReduceColumn(net, me, part, pair, far, side, "entry")

    def inward(dy):
        at = pl.ds(2 * turn(me.y, dy), 2)

        def out(n, _):
            low = dot_last(z[at].reshape(256, 640), w[n, :, :, :, 0:640].reshape(512, 640)).astype(BF)
            part[at, :, :, pl.ds(pl.multiple_of(512 * n, 512), 512)] = low.reshape(2, 2, 64, 512)
            return 0

        lax.fori_loop(0, 4, out, 0)
        entry.send_pair(dy)

    def weight_in(i, _):
        left = gb[:, :, :, pl.ds(pl.multiple_of(512 * i, 512), 512)].reshape(1024, 512)
        w[i, :, :, :, 0:640] = dot_first(left, z[...].reshape(1024, 640)).astype(BF).reshape(4, 2, 64, 640)
        return 0

    inward(2)
    inward(1)
    entry.take_pair(2)
    inward(-1)
    entry.take_pair(1)
    inward(0)
    entry.take_pair(-1)
    load_one.wait()
    lax.fori_loop(0, 4, weight_in, 0)
    inner.start()
    entry.relay()
    entry.take_pair(0)
    feed.fourth()
    outer.third()
    need("gains", "gres", "gain2", "x")
    grow[...] = jnp.zeros_like(grow)
    inner.second()
    entry.arrive()
    for k in range(2):

        def close(i, _):
            at = pl.ds(pl.multiple_of(i * 16, 16), 16)
            value = xo[k, at, :].astype(F32)
            scale = lax.rsqrt(jnp.mean(value * value, axis=-1, keepdims=True) + EPSILON)
            normed = value * scale
            got = entry.total(k, at)
            grow[...] = grow[...] + (got * normed).reshape(2, 8, 2048).sum(axis=0)
            v = got * gains[0:1, :]
            back = (v - normed * jnp.mean(v * normed, axis=-1, keepdims=True)) * scale
            gx[k, at, :] = (gres[k, at, :] + back).astype(BF)
            return 0

        lax.fori_loop(0, 4, close, 0, unroll=2)
    keep = [net.local(gx, gx_out), save_out]
    line = lax.broadcasted_iota(jnp.int32, (8, 2048), 0)
    one = jnp.broadcast_to(jnp.sum(grow[...], axis=0, keepdims=True), (8, 2048))
    two = jnp.broadcast_to(jnp.sum(gain2[...], axis=0, keepdims=True), (8, 2048))
    grow[...] = jnp.where(line == 0, one, jnp.where(line == 1, two, 0.0))

    def features(p):
        return pl.ds(pl.multiple_of(128 * p, 128), 128)

    for d in range(1, 16):
        p = lax.rem(me.plane + d, 16)
        net.go(grow.at[:, features(p)], gsum.at[me.plane], me.flat(d), ("gain", d))
    gsum[me.plane] = grow[:, features(me.plane)]

    inner.third()
    feed.finish()
    own_f = share(side2_f.at[:, 0], ff, "ff")
    low = co[...].reshape(1024, WIDE).astype(BF)
    grad_rate = dot_first(low, rt[...].reshape(1024, WIDE).astype(BF))
    grad_gate = dot_first(low, ig[...].reshape(1024, WIDE).astype(BF))
    rows = lax.broadcasted_iota(jnp.int32, (WIDE, WIDE), 0)
    lanes = lax.broadcasted_iota(jnp.int32, (WIDE, WIDE), 1)
    upper = rows < 160
    held = jnp.where(
        lanes < 160,
        jnp.where(upper, grad_rate, pltpu.roll(grad_rate, WIDE - 160, 1)),
        jnp.where(upper, pltpu.roll(grad_gate, 160, 1), grad_gate),
    )
    vectors = jnp.concatenate([jnp.sum(wacc[k], axis=0, keepdims=True) for k in range(8)], axis=0)
    slope = -8.0 * -jax.nn.sigmoid(-vec[7:8, :])
    line = lax.broadcasted_iota(jnp.int32, (8, WIDE), 0)
    vectors = jnp.where(line == 7, vectors * slope, vectors)
    tall = jnp.transpose(jnp.concatenate([vectors, jnp.zeros((120, WIDE), F32)], axis=0))
    gm[0:3] = held.reshape(3, 128, WIDE)
    late = jnp.where(lanes_below((WIDE, 128), 64), held[:, 256:384], pltpu.roll(tall, 64, 1))
    gm[0:3, :, 256:384] = late.reshape(3, 128, 128)
    flat = gm[0:3].reshape(WIDE, WIDE)
    for j in range(16):
        piece = jnp.concatenate([flat[20 * j : 20 * j + 20, :], jnp.zeros((12, WIDE), F32)], axis=0)
        sgr[j] = piece.astype(BF)

    def small_copy(j):
        return pltpu.make_async_remote_copy(
            src_ref=sgr.at[j],
            dst_ref=srec.at[me.plane],
            send_sem=ssend.at[j],
            recv_sem=srecv.at[me.plane],
            device_id=small_to(j),
            device_id_type=MESH,
        )

    for j in range(16):
        own = jnp.logical_and(mine, index == j)

        @pl.when(jnp.logical_not(own))
        def _():
            small_copy(j).start()

        @pl.when(own)
        def _():
            pltpu.make_async_copy(sgr.at[j], srec.at[me.plane], srecv.at[me.plane]).start()

    outer.fourth()
    inner.fourth()
    for d in range(1, 16):
        net.take(gsum.at[lax.rem(me.plane + 16 - d, 16)], ("gain", d), me.sibling())
    total = gsum[0]
    for k in range(1, 16):
        total = total + gsum[k]
    gall[me.part] = total
    for d in range(1, 8):
        y, c = me.column(d)
        net.go(gall.at[me.part], gall.at[me.part], me.at(y=y, c=c), ("gain8", d))
    outer.finish()
    own_o = share(side2_o.at[:, 0], fo, "fo")
    inner.finish()
    own_i = share(side2_i.at[:, 0], fi, "fi")
    for p in range(16):

        @pl.when(jnp.logical_not(jnp.logical_and(mine, me.plane == p)))
        def _():
            pltpu.make_async_remote_copy(
                src_ref=sgr.at[0],
                dst_ref=srec.at[p],
                send_sem=ssend.at[0],
                recv_sem=srecv.at[p],
                device_id=me.sibling(),
                device_id_type=MESH,
            ).wait_recv()

        @pl.when(jnp.logical_and(mine, me.plane == p))
        def _():
            pltpu.make_async_copy(sgr.at[0], srec.at[p], srecv.at[p]).wait()

    total = srec[0].astype(F32)
    for k in range(1, 16):
        total = total + srec[k].astype(F32)
    ssum[...] = total
    keep.append(net.local(ssum, small_out))
    own_f.wait()
    collect(ff, "ff")
    keep.append(net.local(ff, ff_out))
    own_d.wait()
    collect(fd, "fd")
    keep.append(net.local(fd, fd_out))
    collect(gall, "gain8")
    total = gall[0]
    for k in range(1, 8):
        total = total + gall[k]
    gtot[...] = total
    keep.append(net.local(gtot, gains_out))
    own_o.wait()
    collect(fo, "fo")
    keep.append(net.local(fo, fo_out))
    own_i.wait()
    collect(fi, "fi")
    keep.append(net.local(fi, fi_out))
    for copy in keep:
        copy.wait()
    net.drain(result.sent)
    for j in range(16):

        @pl.when(jnp.logical_not(jnp.logical_and(mine, index == j)))
        def _():
            small_copy(j).wait_send()


def shaped(shape, kind):
    return jax.ShapeDtypeStruct(shape, kind)


def vmem(shape, kind):
    return pltpu.VMEM(shape, kind)


def call(kernel, args, outs, scratch, name, number, sends, recvs, extra=(), places={}):
    anywhere = pl.BlockSpec(memory_space=pl.ANY)
    return pl.pallas_call(
        kernel,
        out_shape=[shaped(*out) for out in outs],
        in_specs=[places.get(i, anywhere) for i in range(len(args))],
        out_specs=[anywhere] * len(outs),
        scratch_shapes=[vmem(*one) for one in scratch]
        + [pltpu.SemaphoreType.DMA((sends,)), pltpu.SemaphoreType.DMA((recvs,)), pltpu.SemaphoreType.DMA((48,))]
        + list(extra),
        compiler_params=pltpu.CompilerParams(
            collective_id=number, has_side_effects=True, vmem_limit_bytes=62 * 1024 * 1024
        ),
        name=name,
    )(*args)


ROWS = (8, 128, WIDE)
BLOCK = (2, 64, 2048)
ALL = (8, 2, 64, 2048)
SIXTEEN = (pltpu.SemaphoreType.DMA((16,)), pltpu.SemaphoreType.DMA((16,)))


def plane(width):
    return [((2, 2, 2, 64, width), BF), ((2, 2, 4, 64, width), BF), ((2, 2, 32, width), BF), ((2, 2, 64, width), BF)]


def forward(args):
    weights = (4, 4, 2, 64)
    flat = pl.BlockSpec(memory_space=pltpu.SMEM)
    sums = [((4,) + BLOCK, BF), (BLOCK, BF), ((2,) + BLOCK, BF)]
    return call(
        forward_kernel,
        args,
        [
            (weights + (PK,), BF), (ALL, BF), ((8, 2, 64, 128), BF), ((8, 2048), F32), ((8, WIDE), F32),
            ((WIDE, 2 * WIDE), BF), ((8, 144, WIDE), BF),
            (ROWS, F32), (ROWS, F32), (ROWS, F32), (ROWS, F32), (ROWS, F32), ((8, WIDE), F32), (ROWS, BF),
            (weights + (FG,), BF), ((2, 64, HID), BF), (ALL, BF), (ALL, BF), (BLOCK, F32), (BLOCK, F32),
            ((8, 2048), F32),
        ],
        [
            ((16, 2560), BF), ((16, 2560), BF), ((16, 2560), BF), ((8, 16, PK), BF), ((20, 160), BF), ((20, 160), BF),
            ((16, 128), F32), ((SMALL, WIDE), BF), ((2, 64, TOK), BF), ((8, 128), F32), ((8, 8, 128), F32),
            (weights + (PK,), BF), (weights + (FK,), BF), ((8, 2, 64, TOK), BF), ((16, SMALL, WIDE), BF),
            ((WIDE, WIDE), F32), ((WIDE, 2 * WIDE), BF), ((8, WIDE), F32), ((8, 2048), F32), ((8, 144, WIDE), BF),
            (ROWS, F32), (ROWS, F32), (ROWS, F32), (ROWS, F32), (ROWS, F32), (ROWS, F32), (ROWS, BF),
            ((16, 2, 8, WIDE), F32), ((8, WIDE), F32), *sums, (BLOCK, F32), (BLOCK, BF), (BLOCK, BF),
            (ALL, BF), (ALL, BF), (BLOCK, BF), ((1024, HID), BF), ((1024, FG), BF),
            (ALL, BF), (BLOCK, BF), (BLOCK, F32), ((8, 2048), F32), ((512, 1024), BF), *plane(HID),
        ],
        "forward", 1, 320, 320, SIXTEEN, {8: flat},
    )


def backward(args):
    return call(
        backward_kernel,
        args,
        [
            ((8, 16, FG), BF), ((8, 16, HID), BF), ((8, 16, WIDE), BF), ((8, 16, 640), BF), ((SMALL, WIDE), F32), ((8, 128), F32),
            (BLOCK, BF), (BLOCK, BF),
        ],
        [
            (ALL, BF), ((4, 4, 2, 64, PK), BF), ((4, 4, 2, 64, FG), BF), ((8, 2, 64, 128), BF), ((8, 2048), F32),
            ((8, WIDE), F32), ((WIDE, 2 * WIDE), BF), ((8, 144, WIDE), BF), (ROWS, F32), (ROWS, F32), (ROWS, F32),
            (ROWS, F32), (ROWS, F32), (ROWS, BF), ((8, WIDE), F32), (BLOCK, F32), ((8, 2048), F32), (BLOCK, BF),
            (ROWS, F32), (ROWS, F32), ((16, 2, 8, WIDE), F32), ((8, WIDE), F32), ((8, 128, 640), BF),
            ((16, SMALL, WIDE), BF), ((16, SMALL, WIDE), BF), ((SMALL, WIDE), F32),
            (ALL, BF), ((4,) + BLOCK, BF), (BLOCK, BF), ((2,) + BLOCK, BF),
            ((4,) + BLOCK, BF), (BLOCK, BF), ((2,) + BLOCK, BF), (BLOCK, F32), (BLOCK, BF),
            *plane(FG), *plane(WIDE), *plane(640),
            ((8, 16, FG), BF), ((8, 16, HID), BF), ((8, 16, WIDE), BF), ((8, 16, 640), BF),
            ((8, 2048), F32), ((16, 8, 128), F32), ((8, 128), F32),
            ((8, 8, 128), F32), (BLOCK, BF), ((8, 8, WIDE), F32), ((2, 8, 8, WIDE), F32),
        ],
        "recurrent_backward", 3, 256, 256, SIXTEEN,
    )


def finish_kernel(
    ff_in, fd_in, fo_in, fi_in, small_in, sums_in, gx_in, result_in,
    output, grad_tokens, gain_a, gain_b, conv_w, conv_b, rate_w, input_w, rate_b, input_b, decay,
    out_w, x_w, y_w, gate_w, up_w, down_w,
    ff, fd, fo, fi, small, sums, sems,
):
    me = Place()
    moves = (
        (ff_in, ff), (fd_in, fd), (fo_in, fo), (fi_in, fi), (small_in, small), (sums_in, sums), (gx_in, grad_tokens),
        (result_in, output),
    )
    loads = [pltpu.make_async_copy(a, b, sems.at[i]) for i, (a, b) in enumerate(moves)]
    for copy in loads:
        copy.start()
    for copy in loads:
        copy.wait()
    own = pltpu.roll(sums[...], 128 - (me.c * 64 + me.y * 16), 1)
    gain_a[...] = own[0:1, 0:16]
    gain_b[...] = own[1:2, 0:16]
    rate_w[...] = small[0:20, 0:160]
    input_w[...] = pltpu.roll(small[0:20, :], WIDE - 160, 1)[:, 0:160]
    tall = jnp.concatenate([small[:, 256:384], jnp.zeros((128 - SMALL, 128), F32)], axis=0)
    vectors = jnp.transpose(tall)[64:72, 0:20]
    conv_w[...] = vectors[0:4, :]
    conv_b[...] = vectors[4:5, :]
    rate_b[...] = vectors[5:6, :]
    input_b[...] = vectors[6:7, :]
    decay[...] = vectors[7:8, :]
    for t in range(8):
        at = slice(HID * t, HID * (t + 1))
        gate_w[:, at] = ff[t, :, 0:HID].astype(F32)
        up_w[:, at] = ff[t, :, HID:].astype(F32)
        down_w[:, at] = fd[t].astype(F32)
    zeros = jnp.zeros((16, 256), F32)

    def pair(first, second):
        keep = lanes_below((16, WIDE), CH)
        left = jnp.concatenate([jnp.where(keep, first, 0.0), zeros], axis=1)
        right = jnp.concatenate([jnp.where(keep, second, 0.0), zeros], axis=1)
        return left + pltpu.roll(right, CH, 1)

    for t in range(0, 8, 2):
        at = slice(CH * t, CH * (t + 2))
        out_w[:, at] = pair(fo[t].astype(F32), fo[t + 1].astype(F32))
        x_w[:, at] = pair(fi[t, :, 0:WIDE].astype(F32), fi[t + 1, :, 0:WIDE].astype(F32))
        late = [pltpu.roll(fi[t + i, :, 256:640].astype(F32), WIDE - 64, 1) for i in range(2)]
        y_w[:, at] = pair(*late)


def finish(args):
    held = pl.BlockSpec(memory_space=pltpu.VMEM)
    outs = [
        (BLOCK, BF), (BLOCK, BF), ((1, 16), F32), ((1, 16), F32), ((4, 20), F32), ((1, 20), F32), ((20, 160), F32),
        ((20, 160), F32), ((1, 20), F32), ((1, 20), F32), ((1, 20), F32), ((16, 2560), F32), ((16, 2560), F32),
        ((16, 2560), F32), ((16, 6144), F32), ((16, 6144), F32), ((16, 6144), F32),
    ]
    return pl.pallas_call(
        finish_kernel,
        out_shape=[shaped(*out) for out in outs],
        in_specs=[pl.BlockSpec(memory_space=pl.ANY)] * len(args),
        out_specs=[held] * len(outs),
        scratch_shapes=[
            vmem((8, 16, FG), BF), vmem((8, 16, HID), BF), vmem((8, 16, WIDE), BF), vmem((8, 16, 640), BF),
            vmem((SMALL, WIDE), F32), vmem((8, 128), F32), pltpu.SemaphoreType.DMA((8,)),
        ],
        compiler_params=pltpu.CompilerParams(vmem_limit_bytes=62 * 1024 * 1024),
        name="results",
    )(*args)


def local(
    tokens,
    seg_starts,
    gain_one,
    gain_two,
    conv_weight,
    conv_bias,
    rate_weight,
    input_weight,
    rate_bias,
    input_bias,
    decay_param,
    proj_out,
    proj_x,
    proj_y,
    ffn_gate,
    ffn_up,
    ffn_down,
    cotangent,
):
    vectors = jnp.concatenate([conv_weight, jnp.stack([conv_bias, rate_bias, input_bias, decay_param])], axis=0)
    odds = jnp.concatenate(
        [
            jnp.pad(vectors, ((0, 0), (0, 108))),
            jnp.pad(jnp.stack([gain_one, gain_two]), ((0, 6), (0, 112))),
        ],
        axis=0,
    ).astype(F32)
    (
        p_all, one, mask_all, gains, vec, riw, ce, pre, co, rt, ig, st, carry, mix, gf, gd, gb, pout, res, gres, gain2
    ) = forward((
        proj_x, proj_y, proj_out, ffn_gate, ffn_up, ffn_down, tokens, cotangent, seg_starts, rate_weight, input_weight,
        odds,
    ))
    ff, fd, fo, fi, small, gain_sums, grad_tokens, output = backward((
        gb, p_all, gf, one, mask_all, gains, vec, riw, ce, pre, co, rt, ig, st, mix, carry, gres, gain2, tokens, pout, res,
        gd,
    ))
    results = finish((ff, fd, fo, fi, small, gain_sums, grad_tokens, output))
    return tuple(one.reshape(one.shape[1:]) if i in (2, 3, 5, 8, 9, 10) else one for i, one in enumerate(results))


def solution(mesh):
    both = ("seq", "rows")
    wide, flat = P(both, None), P(both)
    rows = P("rows", "seq", None)
    return jax.shard_map(
        local,
        mesh=mesh,
        in_specs=(
            rows, P("rows", None), flat, flat, P(None, both), flat, wide, wide, flat, flat, flat,
            wide, wide, wide, wide, wide, wide, rows,
        ),
        out_specs=(
            rows, rows, flat, flat, P(None, both), flat, wide, wide, flat, flat, flat,
            wide, wide, wide, wide, wide, wide,
        ),
        check_vma=False,
    )
```

```python
import jax
import jax.numpy as jnp
from jax import lax
from jax.experimental import pallas as pl
from jax.experimental.pallas import tpu as pltpu
from jax.sharding import PartitionSpec as P

BF, F32 = jnp.bfloat16, jnp.float32
MESH = pl.DeviceIdType.MESH
EPSILON = 1e-06
FLOOR_VALUE = 0.001
HID = 768
CH = 320
WIDE = 384
PK = 1024
FK = 2304
FG = 1536
TOK = 2176
SMALL = 32


def dot(left, right):
    return jnp.dot(left, right, preferred_element_type=F32)


def dot_last(left, right):
    return lax.dot_general(left, right, (((1,), (1,)), ((), ())), preferred_element_type=F32)


def dot_first(left, right):
    return lax.dot_general(left, right, (((0,), (0,)), ((), ())), preferred_element_type=F32)


def gelu(v):
    return 0.5 * v * (1.0 + jnp.tanh(0.7978845608028654 * (v + 0.044715 * (v * v * v))))


def gelu_and_slope(v):
    square = v * v
    t = jnp.tanh(0.7978845608028654 * v * (1.0 + 0.044715 * square))
    half = 0.5 * (1.0 + t)
    slope = half + 0.5 * v * (1.0 - t * t) * (0.7978845608028654 * (1.0 + 0.134145 * square))
    return v * half, slope


def turn(v, d):
    return lax.rem(v + (d % 4), 4)


class Place:
    def __init__(self):
        s, self.y = lax.axis_index("seq"), lax.axis_index("rows")
        self.x, self.z, self.c = lax.div(s, 8), lax.rem(lax.div(s, 2), 4), lax.rem(s, 2)
        self.plane = self.x * 4 + self.z
        self.part = self.y * 2 + self.c

    def at(self, x=None, z=None, c=None, y=None):
        x = self.x if x is None else x
        z = self.z if z is None else z
        c = self.c if c is None else c
        return (x * 8 + z * 2 + c, self.y if y is None else y)

    def sibling(self):
        return self.at(c=1 - self.c)

    def column(self, d):
        return turn(self.y, d // 2), (self.c + d % 2) % 2 if d % 2 == 0 else 1 - self.c

    def flat(self, d):
        p = lax.rem(self.plane + (d % 16), 16)
        return self.at(x=lax.div(p, 4), z=lax.rem(p, 4))


class Net:
    def __init__(self, send, recv, local):
        self.send, self.recv, self.near = send, recv, local
        self.names, self.sent, self.kept = {}, [], []

    def slot(self, name):
        assert len(self.names) < self.recv.shape[0] and len(self.sent) <= self.send.shape[0]
        return self.names.setdefault(name, len(self.names))

    def go(self, src, dst, to, name):
        copy = pltpu.make_async_remote_copy(
            src_ref=src,
            dst_ref=dst,
            send_sem=self.send.at[len(self.sent)],
            recv_sem=self.recv.at[self.slot(name)],
            device_id=to,
            device_id_type=MESH,
        )
        copy.start()
        self.sent.append(copy)
        return copy

    def many(self, copies, pieces):
        waits = []
        for src, dst, to, name in copies:
            waits.append(
                pltpu.make_async_remote_copy(
                    src_ref=src,
                    dst_ref=dst,
                    send_sem=self.send.at[len(self.sent)],
                    recv_sem=self.recv.at[self.slot(name)],
                    device_id=to,
                    device_id_type=MESH,
                )
            )
            self.sent.append(waits[-1])
        first = len(self.sent) - len(copies)
        for piece in range(pieces):
            for i, (src, dst, to, name) in enumerate(copies):
                rows = src.shape[-2] // pieces
                at = (slice(None),) * (len(src.shape) - 2) + (pl.ds(rows * piece, rows),)
                pltpu.make_async_remote_copy(
                    src_ref=src.at[at],
                    dst_ref=dst.at[at],
                    send_sem=self.send.at[first + i],
                    recv_sem=self.recv.at[self.slot(name)],
                    device_id=to,
                    device_id_type=MESH,
                ).start()
        return waits

    def take(self, dst, name, to):
        pltpu.make_async_remote_copy(
            src_ref=dst,
            dst_ref=dst,
            send_sem=self.send.at[0],
            recv_sem=self.recv.at[self.slot(name)],
            device_id=to,
            device_id_type=MESH,
        ).wait_recv()

    def local(self, src, dst):
        assert len(self.kept) < self.near.shape[0]
        copy = pltpu.make_async_copy(src, dst, self.near.at[len(self.kept)])
        copy.start()
        self.kept.append(copy)
        return copy

    def drain(self, but=()):
        for copy in self.sent:
            if all(copy is not other for other in but):
                copy.wait_send()


def greet(peers, extra=0):
    barrier = pltpu.get_barrier_semaphore()
    for peer in peers:
        pl.semaphore_signal(barrier, inc=1, device_id=peer, device_id_type=MESH)
    return barrier


def add_into(out, terms):
    rows = out.shape[-2]
    lead = [()]
    for extent in out.shape[:-2]:
        lead = [one + (i,) for one in lead for i in range(extent)]
    for one in lead:

        def step(i, _):
            at = pl.ds(pl.multiple_of(i * 16, 16), 16)
            if len(terms) == 2:
                total = terms[0][one + (at, slice(None))] + terms[1][one + (at, slice(None))]
            else:
                total = terms[0][one + (at, slice(None))].astype(F32)
                for term in terms[1:]:
                    total = total + term[one + (at, slice(None))].astype(F32)
            out[one + (at, slice(None))] = total.astype(out.dtype)
            return 0

        lax.fori_loop(0, rows // 16, step, 0, unroll=2)


class GatherColumn:
    def __init__(self, net, me, g, tag):
        self.net, self.me, self.g, self.tag = net, me, g, tag
        self.sent = []

    def go(self, *what):
        self.sent.append(self.net.go(*what))

    def block(self, dy, k, c):
        return self.g.at[2 * turn(self.me.y, dy) + k, c]

    def start(self, src):
        me, net, tag = self.me, self.net, self.tag
        copies = []
        for k in range(2):
            copies.append((src.at[k], self.block(0, k, me.c), me.at(y=turn(me.y, 1)), (tag, "ring", -1, k)))
            copies.append((src.at[1 - k], self.block(0, 1 - k, me.c), me.at(y=turn(me.y, -1)), (tag, "ring", 1, 1 - k)))
            copies.append((src.at[k], self.block(0, k, me.c), me.sibling(), (tag, "sib", 0, k)))
        for group in (copies[:3], copies[3:]):
            self.sent += net.many(group, 1)
        self.own = net.local(src, self.g.at[pl.ds(2 * me.y, 2), me.c])

    def relay(self, halves=(0, 1)):
        me, net, tag = self.me, self.net, self.tag
        for first in halves:
            copies = []
            for dy in (-1, 1):
                k = first if dy == -1 else 1 - first
                here = self.block(dy, k, me.c)
                net.take(here, (tag, "ring", dy, k), me.sibling())
                if first == 0:
                    copies.append((here, here, me.at(y=turn(me.y, -dy)), (tag, "far", k)))
                copies.append((here, here, me.sibling(), (tag, "sib", dy, k)))
            self.sent += net.many(copies, 1)

    def last(self):
        me, net, tag = self.me, self.net, self.tag
        for k in range(2):
            here = self.block(2, k, me.c)
            net.take(here, (tag, "far", k), me.sibling())
            self.go(here, here, me.sibling(), (tag, "sib", 2, k))

    def whole(self, dy):
        me, net, tag = self.me, self.net, self.tag
        if dy == 0:
            self.own.wait()
        for k in range(2):
            net.take(self.block(dy, k, 1 - me.c), (tag, "sib", dy, k), me.sibling())

    def finish(self):
        for dy in (0, -1, 1, 2):
            self.whole(dy)


class ReduceColumn:
    def __init__(self, net, me, part, pair, far, side, tag):
        self.net, self.me, self.tag = net, me, tag
        self.part, self.pair, self.far, self.side = part, pair, far, side
        self.sent = []

    def go(self, *what):
        self.sent.append(self.net.go(*what))

    def drain(self):
        for copy in self.sent:
            copy.wait_send()

    def mine(self, dy):
        return self.part.at[pl.ds(2 * turn(self.me.y, dy), 2), self.me.c]

    def one(self, dy, k):
        return self.part.at[2 * turn(self.me.y, dy) + k, self.me.c]

    def send_pair(self, dy):
        me = self.me
        src = self.part.at[pl.ds(2 * turn(me.y, dy), 2), 1 - me.c]
        self.go(src, self.pair.at[dy % 4], me.sibling(), (self.tag, "pair", dy % 4))

    def take_pair(self, dy):
        me, net, tag = self.me, self.net, self.tag
        net.take(self.pair.at[dy % 4], (tag, "pair", dy % 4), me.sibling())
        add_into(self.mine(dy), (self.mine(dy), self.pair.at[dy % 4]))
        above, below = me.at(y=turn(me.y, 1)), me.at(y=turn(me.y, -1))
        if dy == 2:
            self.go(self.one(2, 0), self.far.at[0], above, (tag, "far", 0))
            self.go(self.one(2, 1), self.far.at[1], below, (tag, "far", 1))
        elif dy == 1:
            self.go(self.one(1, 1), self.side.at[0, 1], above, (tag, "side", 0, 1))
        elif dy == -1:
            self.go(self.one(-1, 0), self.side.at[1, 0], below, (tag, "side", 1, 0))

    def relay(self):
        me, net, tag = self.me, self.net, self.tag
        above, below = me.at(y=turn(me.y, 1)), me.at(y=turn(me.y, -1))
        net.take(self.far.at[0], (tag, "far", 0), below)
        add_into(self.one(1, 0), (self.one(1, 0), self.far.at[0]))
        self.go(self.one(1, 0), self.side.at[0, 0], above, (tag, "side", 0, 0))
        net.take(self.far.at[1], (tag, "far", 1), above)
        add_into(self.one(-1, 1), (self.one(-1, 1), self.far.at[1]))
        self.go(self.one(-1, 1), self.side.at[1, 1], below, (tag, "side", 1, 1))

    def arrive(self):
        for way in range(2):
            for k in range(2):
                self.net.take(self.side.at[way, k], (self.tag, "side", way, k), self.me.sibling())

    def total(self, k, at):
        return (
            self.one(0, k)[at, :].astype(F32)
            + self.side[0, k, at, :].astype(F32)
            + self.side[1, k, at, :].astype(F32)
        )


class GatherPlane:
    def __init__(self, net, me, g, tag, pieces):
        self.net, self.me, self.g, self.tag, self.pieces = net, me, g, tag, pieces
        self.sent = []

    def block(self, h, da, db):
        me = self.me
        if h == 0:
            return self.g.at[turn(me.x, db), turn(me.z, da), 0]
        return self.g.at[turn(me.x, da), turn(me.z, db), 1]

    def peer(self, h, da, db):
        me = self.me
        if h == 0:
            return me.at(x=turn(me.x, db), z=turn(me.z, da))
        return me.at(x=turn(me.x, da), z=turn(me.z, db))

    def copy(self, h, da, db, step_a, step_b, rows=None):
        here = self.block(h, da, db)
        name = (self.tag, h, (da - step_a) % 4, (db - step_b) % 4)
        if rows is not None:
            here = here.at[pl.ds(32 * rows, 32)]
            name += (rows,)
        return (here, here, self.peer(h, step_a, step_b), name)

    def send(self, copies):
        self.sent += self.net.many([self.copy(*one) for one in copies], self.pieces)

    def take(self, h, da, db, rows=None):
        here = self.block(h, da, db)
        name = (self.tag, h, da % 4, db % 4)
        if rows is not None:
            here = here.at[pl.ds(32 * rows, 32)]
            name += (rows,)
        self.net.take(here, name, self.me.sibling())

    def start(self):
        self.send([(h, 0, 0, step, 0) for h in range(2) for step in (1, -1)])
        self.send([(h, 0, 0, 0, step) for h in range(2) for step in (1, -1)])

    def second(self):
        for h in range(2):
            self.take(h, -1, 0)
            self.take(h, 1, 0)
        self.send(
            [(h, -step, 0, step, 0, 0 if step == 1 else 1) for h in range(2) for step in (1, -1)]
        )
        for da in (-1, 1):
            self.send([(h, da, 0, 0, step) for h in range(2) for step in (1, -1)])

    def third(self):
        for h in range(2):
            self.take(h, 0, -1)
            self.take(h, 0, 1)
        self.send([(h, 0, -1, 0, 1) for h in range(2)])
        for h in range(2):
            self.take(h, 2, 0, rows=0)
            self.take(h, 2, 0, rows=1)
        self.send([(h, 2, 0, 0, step) for h in range(2) for step in (1, -1)])

    def fourth(self):
        for h in range(2):
            self.take(h, -1, -1)
            self.take(h, -1, 1)
            self.take(h, 1, -1)
            self.take(h, 1, 1)
        self.send([(h, da, 1, 0, -1) for da in (-1, 1) for h in range(2)])

    def fifth(self):
        for h in range(2):
            self.take(h, 2, -1)
            self.take(h, 2, 1)
        self.send([(h, 2, -1, 0, 1) for h in range(2)])

    def finish(self):
        for h in range(2):
            for da in (0, -1, 1, 2):
                self.take(h, da, 2)


class ReducePlane:
    def __init__(self, net, me, g, far, side, far2, side2, tag):
        self.net, self.me, self.g, self.tag = net, me, g, tag
        self.far, self.side, self.far2, self.side2 = far, side, far2, side2

    def super(self, h, db, lo, g=None):
        me = self.me
        g = self.g if g is None else g
        if h == 0:
            return g.at[turn(me.x, db), pl.ds(lo, 2), 0]
        return g.at[pl.ds(lo, 2), turn(me.z, db), 1]

    def whole(self, h, a):
        me = self.me
        return self.g.at[me.x, a, 0] if h == 0 else self.g.at[a, me.z, 1]

    def along(self, h, db):
        me = self.me
        return me.at(x=turn(me.x, db)) if h == 0 else me.at(z=turn(me.z, db))

    def across(self, h, da):
        me = self.me
        return me.at(z=turn(me.z, da)) if h == 0 else me.at(x=turn(me.x, da))

    def start(self, g=None):
        net, tag = self.net, self.tag
        far, side = [], []
        for h in range(2):
            far.append((self.super(h, 2, 0, g), self.far.at[h, 0], self.along(h, 1), (tag, h, "far", 0)))
            far.append((self.super(h, 2, 2, g), self.far.at[h, 1], self.along(h, -1), (tag, h, "far", 1)))
            to = self.side.at[h, 0, pl.ds(2, 2)]
            side.append((self.super(h, 1, 2, g), to, self.along(h, 1), (tag, h, "side", 0, 1)))
            to = self.side.at[h, 1, pl.ds(0, 2)]
            side.append((self.super(h, -1, 0, g), to, self.along(h, -1), (tag, h, "side", 1, 0)))
        net.many(far, 1)
        net.many(side, 1)

    def second(self):
        net, tag = self.net, self.tag
        for h in range(2):
            for way in range(2):
                here = self.far.at[h, way]
                net.take(here, (tag, h, "far", way), self.me.sibling())
                step = 1 if way == 0 else -1
                add_into(here, (here, self.super(h, step, 2 * way)))
                net.go(
                    here, self.side.at[h, way, pl.ds(2 * way, 2)], self.along(h, step), (tag, h, "side", way, way)
                )

    def third(self):
        net, tag = self.net, self.tag
        for h in range(2):
            for way in range(2):
                for lo in range(2):
                    here = self.side.at[h, way, pl.ds(2 * lo, 2)]
                    net.take(here, (tag, h, "side", way, lo), self.me.sibling())
        me = self.me
        for h in range(2):
            mine = me.z if h == 0 else me.x
            for da in (2, 1, -1, 0):
                a = turn(mine, da)
                here = self.side.at[h, 0, a]
                add_into(here, (here, self.side.at[h, 1, a], self.whole(h, a)))
                if da == 2:
                    for way in range(2):
                        net.go(
                            here.at[pl.ds(32 * way, 32)],
                            self.far2.at[h, way],
                            self.across(h, 1 if way == 0 else -1),
                            (tag, h, "far2", way),
                        )
                elif da != 0:
                    way = 0 if da == 1 else 1
                    rows = pl.ds(32 * (1 - way), 32)
                    net.go(
                        here.at[rows], self.side2.at[h, way, rows], self.across(h, da), (tag, h, "side2", way, 1 - way)
                    )

    def fourth(self):
        net, tag, me = self.net, self.tag, self.me
        for h in range(2):
            mine = me.z if h == 0 else me.x
            for way in range(2):
                here = self.far2.at[h, way]
                net.take(here, (tag, h, "far2", way), me.sibling())
                da = 1 if way == 0 else -1
                rows = pl.ds(32 * way, 32)
                add_into(here, (here, self.side.at[h, 0, turn(mine, da), rows]))
                net.go(here, self.side2.at[h, way, rows], self.across(h, da), (tag, h, "side2", way, way))

    def finish(self):
        net, tag, me = self.net, self.tag, self.me
        for h in range(2):
            mine = me.z if h == 0 else me.x
            for way in range(2):
                for part in range(2):
                    here = self.side2.at[h, way, pl.ds(32 * part, 32)]
                    net.take(here, (tag, h, "side2", way, part), me.sibling())
            here = self.side2.at[h, 0]
            add_into(here, (here, self.side2.at[h, 1], self.side.at[h, 0, mine]))


def column_peers(me):
    peers = []
    for d in range(1, 8):
        y, c = me.column(d)
        peers.append(me.at(y=y, c=c))
    return peers


def one_less_exp(t, plain):
    series = 1.0 - t * (1.0 / 8.0)
    for k in range(7, 1, -1):
        series = 1.0 - t * (1.0 / k) * series
    return jnp.where(t < 0.5, t * series, plain)


def decay_parts(rate, log_scale, resets):
    log_decay = rate * log_scale
    a = jnp.exp(log_decay)
    margin = one_less_exp(-2.0 * log_decay, 1.0 - a * a)
    scale = jnp.where(resets > 0.5, 1.0, jnp.sqrt(jnp.maximum(margin, FLOOR_VALUE)))
    return a, a * (1.0 - resets), scale, margin


def log_scale_row(vec):
    return -8.0 * jax.nn.softplus(-vec[7:8, :])


STEP = 32


def blocks(first, count, body):
    def one(i, _):
        row, j = first + lax.div(i, 128 // STEP), lax.rem(i, 128 // STEP)
        at = pl.ds(pl.multiple_of(j * STEP, STEP), STEP)
        body(row, j, at)
        return 0

    lax.fori_loop(0, count * (128 // STEP), one, 0, unroll=2)


def mask_block(masks, row, j):
    inner = 64 // STEP
    at = pl.ds(pl.multiple_of(lax.rem(j, inner) * STEP, STEP), STEP)
    return masks[row, lax.div(j, inner), at, :].astype(F32)


def lanes_below(shape, limit):
    return lax.broadcasted_iota(jnp.int32, shape, len(shape) - 1) < limit


def forward_kernel(
    px, py, po, wg, wu, wd, tokens_in, cot_in, seg, rate_in, input_in, odds_in,
    p_out, one_out, mask_out, gain_out, vec_out, riw_out, ce_out,
    pre_out, co_out, rt_out, ig_out, st_out, carry_out, mix_out, gf_out, gd_out, gb_out, pout_out, res_out, gres_out, gain2_out,
    pxl, pyl, pol, wp, rate_l, input_l, odds, sm, x1, gt, gpart,
    pbuf, wf, xg, sg, small, riw, vec, gains, ce, pre, co, rt, ig, fa, st, mix, car, carry, pair, far, side, res, two, xo,
    s2, ct, cot, hid, gu, pout, gb, gres, gain2, flip, far_d, side_d, far2_d, side2_d,
    send, recv, local, ssend, srecv,
):
    me = Place()
    net = Net(send, recv, local)
    loads = [
        net.local(a, b)
        for a, b in (
            (px, pxl), (py, pyl), (po, pol), (odds_in, odds), (rate_in, rate_l), (input_in, input_l), (tokens_in, xo), (cot_in, cot)
        )
    ]
    to_y, to_c, index = me.x, lax.div(me.z, 2), lax.rem(me.z, 2) * 8 + me.c * 4 + me.y
    mine = jnp.logical_and(to_y == me.y, to_c == me.c)

    def small_from(j):
        return me.at(x=me.y, z=2 * me.c + j // 8, c=(j // 4) % 2, y=j % 4)

    def small_to(p):
        return me.at(x=p // 4, z=p % 4, c=to_c, y=to_y)

    barrier = greet(column_peers(me) + [me.flat(d) for d in range(1, 16)])
    for i in range(16):

        @pl.when(jnp.logical_not(jnp.logical_and(mine, me.plane == i)))
        def _():
            pl.semaphore_signal(barrier, inc=1, device_id=small_to(i), device_id_type=MESH)

        @pl.when(jnp.logical_not(jnp.logical_and(mine, index == i)))
        def _():
            pl.semaphore_signal(barrier, inc=1, device_id=small_from(i), device_id_type=MESH)

    spot = lax.broadcasted_iota(jnp.int32, (64, 128), 0) + (me.plane * 2 + me.c) * 64
    lane = lax.broadcasted_iota(jnp.int32, (64, 128), 1)
    for k in range(2):
        reset, crossed = jnp.zeros((64, 128), F32), jnp.zeros((64, 128), F32)
        for j in range(4):
            start = seg[k, j]
            reset = jnp.where(spot == start, 1.0, reset)
            crossed = jnp.where(jnp.logical_and(start <= spot, start > spot - lane), 1.0, crossed)
        usable = jnp.where(jnp.logical_and(lane <= 3, spot >= lane), 1.0 - crossed, 0.0)
        x1[k, :, 2048:TOK] = jnp.where(lane == 0, reset, usable).astype(BF)

    for copy in loads[:6]:
        copy.wait()
    zeros = jnp.zeros((16, 256), F32)
    for t in range(8):
        low, shift = 128 * (CH * t // 128), CH * t % 128

        def window(ref):
            wide = ref[:, low : low + WIDE].astype(F32)
            wide = pltpu.roll(wide, WIDE - shift, 1) if shift else wide
            return jnp.where(lanes_below((16, WIDE), CH), wide, 0.0)

        both = jnp.concatenate([window(pxl), zeros], axis=1)
        both = both + pltpu.roll(jnp.concatenate([window(pyl), zeros], axis=1), CH, 1)
        wp[t, :, 0:640] = both.astype(BF)
        wp[t, :, 640:PK] = window(pol).astype(BF)
    small[0:32, :] = jnp.zeros((32, WIDE), F32)
    small[0:20, 0:160] = rate_l[...].astype(F32)
    left = small[0:32, :]
    small[0:20, 0:160] = input_l[...].astype(F32)
    left = left + pltpu.roll(small[0:32, :], 160, 1)
    small[0:32, :] = left
    small[24:32, 0:128] = odds[0:8, :]
    sm[...] = small[0:32, :].astype(BF)
    gt[...] = pltpu.roll(odds[8:16, :], me.c * 64 + me.y * 16, 1)
    pl.semaphore_wait(barrier, 22 + 32 - 2 * mine.astype(jnp.int32))

    def p_block(y, c):
        return pbuf.at[me.x, me.z, c, pl.ds(pl.multiple_of(16 * y, 16), 16)]

    def f_block(y, c, k):
        rows = pl.ds(pl.multiple_of(16 * y, 16), 16)
        return wf.at[me.x, me.z, c, rows, pl.ds(HID * k, HID)]

    def features(p):
        return pl.ds(pl.multiple_of(128 * p, 128), 128)

    for d in range(1, 8):
        y, c = me.column(d)
        net.go(gt, gpart.at[d], me.at(y=y, c=c), ("gain8", d))
    for d in range(1, 8):
        y, c = me.column(d)
        net.go(wp.at[2 * y + c], p_block(me.y, me.c), me.at(y=y, c=c), ("wp", d))
    own_p = net.local(wp.at[me.part], p_block(me.y, me.c))
    total = gt[...]
    for d in range(1, 8):
        net.take(gpart.at[d], ("gain8", d), me.sibling())
        total = total + gpart[d]
    gpart[0] = total
    gains[:, features(me.plane)] = total
    for d in range(1, 16):
        net.go(gpart.at[0], gains.at[:, features(me.plane)], me.flat(d), ("gain", d))
    for d in range(1, 8):
        y, c = me.column(d)
        for k, w in enumerate((wg, wu, wd)):
            cols = pl.ds(pl.multiple_of(HID * (2 * y + c), HID), HID)
            net.go(w.at[:, cols], f_block(me.y, me.c, k), me.at(y=y, c=c), ("wf", d, k))
    own_f = []
    for k, w in enumerate((wg, wu, wd)):
        cols = pl.ds(pl.multiple_of(HID * me.part, HID), HID)
        own_f.append(net.local(w.at[:, cols], f_block(me.y, me.c, k)))

    def source(d):
        return turn(me.y, -(d // 2)), me.c if d % 2 == 0 else 1 - me.c

    for d in range(1, 8):
        net.take(p_block(*source(d)), ("wp", d), me.sibling())
    own_p.wait()
    proj = GatherPlane(net, me, pbuf.at[:, :, :, :, pl.ds(0, 640)], "p", 1)
    outp = GatherPlane(net, me, pbuf.at[:, :, :, :, pl.ds(640, WIDE)], "o", 1)
    proj.start()
    loads[6].wait()
    for d in range(1, 16):
        net.take(gains.at[:, features(lax.rem(me.plane + 16 - d, 16))], ("gain", d), me.sibling())
    for k in range(2):

        def norm_step(i, _):
            at = pl.ds(pl.multiple_of(i * 16, 16), 16)
            x = xo[k, at, :].astype(F32)
            scale = lax.rsqrt(jnp.mean(x * x, axis=-1, keepdims=True) + EPSILON)
            x1[k, at, 0:2048] = (x * scale * gains[0:1, :]).astype(BF)
            return 0

        lax.fori_loop(0, 4, norm_step, 0, unroll=2)
    tokens = GatherColumn(net, me, xg, "x")
    tokens.start(x1)
    proj.second()
    outp.start()

    def small_copy(i):
        return pltpu.make_async_remote_copy(
            src_ref=sm,
            dst_ref=sg.at[index],
            send_sem=ssend.at[i],
            recv_sem=srecv.at[index],
            device_id=small_to(i),
            device_id_type=MESH,
        )

    for i in range(16):
        own = jnp.logical_and(mine, me.plane == i)

        @pl.when(jnp.logical_not(own))
        def _():
            small_copy(i).start()

        @pl.when(own)
        def _():
            pltpu.make_async_copy(sm, sg.at[index], srecv.at[index]).start()

    tokens.relay((0,))
    proj.third()
    for d in range(1, 8):
        for k in range(3):
            net.take(f_block(*source(d), k), ("wf", d, k), me.sibling())
    for copy in own_f:
        copy.wait()
    feed = GatherPlane(net, me, wf, "f", 1)
    feed.start()
    tokens.relay((1,))
    proj.fourth()
    outp.second()
    tokens.last()
    proj.fifth()
    loads[7].wait()
    cots = GatherColumn(net, me, ct, "c")
    cots.start(cot)

    small[...] = jnp.zeros_like(small)
    for j in range(16):

        @pl.when(jnp.logical_not(jnp.logical_and(mine, index == j)))
        def _():
            pltpu.make_async_remote_copy(
                src_ref=sm,
                dst_ref=sg.at[j],
                send_sem=ssend.at[0],
                recv_sem=srecv.at[j],
                device_id=me.sibling(),
                device_id_type=MESH,
            ).wait_recv()

        @pl.when(jnp.logical_and(mine, index == j))
        def _():
            pltpu.make_async_copy(sm, sg.at[j], srecv.at[j]).wait()

    vectors = jnp.zeros((8, WIDE), F32)
    inside = lanes_below((8, WIDE), 20)
    for j in range(16):
        block = sg[j].astype(F32)
        small[20 * j : 20 * j + 20, :] = block[0:20, :]
        vectors = vectors + pltpu.roll(jnp.where(inside, block[24:32, :], 0.0), 20 * j, 1)
    vec[...] = vectors
    rows = lax.broadcasted_iota(jnp.int32, (WIDE, WIDE), 0)
    lanes = lax.broadcasted_iota(jnp.int32, (WIDE, WIDE), 1)
    held = small[...]
    first = jnp.logical_and(rows < 160, lanes < 160)
    second = jnp.logical_and(jnp.logical_and(rows >= 160, rows < CH), jnp.logical_and(lanes >= 160, lanes < CH))
    riw[:, 0:WIDE] = (jnp.where(first, held, 0.0) + jnp.where(second, pltpu.roll(held, 160, 1), 0.0)).astype(BF)
    riw[:, WIDE:] = (
        jnp.where(first, pltpu.roll(held, WIDE - 160, 1), 0.0) + jnp.where(second, held, 0.0)
    ).astype(BF)
    proj.finish()
    tokens.finish()
    masks = xg.at[:, :, :, pl.ds(2048, 128)]

    def project(i, _):
        at = pl.ds(4 * i, 4)
        left = xg[at, :, :, 0:2048].reshape(512, 2048)
        both = dot(left, pbuf[:, :, :, :, 0:640].reshape(2048, 640))
        low = jnp.where(lanes_below((512, WIDE), CH), both[:, 0:WIDE], 0.0).astype(BF)
        ce[at, 16:144, :] = low.reshape(4, 128, WIDE)
        right = jnp.where(lanes_below((512, WIDE), CH), pltpu.roll(both[:, 256:640], WIDE - 64, 1), 0.0)
        pre[at] = right.reshape(4, 128, WIDE)
        return 0

    lax.fori_loop(0, 2, project, 0)
    for copy in tokens.sent:
        copy.wait_send()
    wide = xg.at[:, :, :, pl.ds(0, 2048)]
    save_one = net.local(wide, one_out)
    net.go(ce.at[:, pl.ds(128, 16)], ce.at[:, pl.ds(0, 16)], me.flat(1), "halo")
    outp.third()
    cots.relay()
    net.take(ce.at[:, pl.ds(0, 16)], "halo", me.sibling())

    def convolve(row, j, at):
        wide = ce[row, pl.ds(pl.multiple_of(j * STEP, STEP), STEP + 16), :].astype(F32)
        valid = mask_block(masks, row, j)
        total = jnp.broadcast_to(vec[4:5, :], (STEP, WIDE))
        for k in range(4):
            piece = wide[16 - k : 16 - k + STEP, :]
            if k > 0:
                piece = piece * valid[:, k : k + 1]
            total = total + vec[k : k + 1, :] * piece
        co[row, at, :] = total

    blocks(0, 8, convolve)
    outp.fourth()
    feed.second()

    def gates(i, _):
        at = pl.ds(4 * i, 4)
        both = dot(co[at].reshape(512, WIDE).astype(BF), riw[...])
        rt[at] = both[:, 0:WIDE].reshape(4, 128, WIDE)
        ig[at] = both[:, WIDE:].reshape(4, 128, WIDE)
        return 0

    lax.fori_loop(0, 2, gates, 0)
    log_scale = log_scale_row(vec)

    def decays(row, j, at):
        rate = jax.nn.sigmoid(rt[row, at, :] + vec[5:6, :])
        gate = jax.nn.sigmoid(ig[row, at, :] + vec[6:7, :])
        _, factor, scale, _ = decay_parts(rate, log_scale, mask_block(masks, row, j)[:, 0:1])
        rt[row, at, :] = rate
        ig[row, at, :] = gate
        fa[row, at, :] = factor
        st[row, at, :] = scale * (gate * co[row, at, :])

    blocks(0, 8, decays)
    cots.last()
    outp.fifth()

    def scan(i, held):
        h, q = held
        at = pl.ds(pl.multiple_of(i * 8, 8), 8)
        f, d = jnp.swapaxes(fa[:, at, :], 0, 1), jnp.swapaxes(st[:, at, :], 0, 1)
        hs, qs = [], []
        for k in range(8):
            h, q = f[k] * h + d[k], q * f[k]
            hs.append(h)
            qs.append(q)
        st[:, at, :] = jnp.swapaxes(jnp.stack(hs), 0, 1)
        fa[:, at, :] = jnp.swapaxes(jnp.stack(qs), 0, 1)
        return h, q

    h, q = lax.fori_loop(0, 16, scan, (jnp.zeros((8, WIDE), F32), jnp.ones((8, WIDE), F32)), unroll=2)
    car[me.plane, 0] = q
    car[me.plane, 1] = h
    for d in range(1, 16):
        net.go(car.at[me.plane], car.at[me.plane], me.flat(d), ("carry", d))
    feed.third()
    for d in range(1, 16):
        net.take(car.at[lax.rem(me.plane + 16 - d, 16)], ("carry", d), me.sibling())
    h = jnp.zeros((8, WIDE), F32)
    for k in range(15):
        h = jnp.where(k < me.plane, car[k, 0] * h + car[k, 1], h)
    carry[...] = h
    branch = ReduceColumn(net, me, wide, pair, far, side, "branch")
    save_one.wait()
    outp.finish()

    def outward(dy):
        first = 2 * turn(me.y, dy)

        def mixing(row, j, at):
            states = st[row, at, :] + fa[row, at, :] * carry[pl.ds(row, 1), :]
            st[row, at, :] = states
            mix[row, at, :] = (states * gelu(pre[row, at, :])).astype(BF)

        blocks(first, 2, mixing)
        at = pl.ds(first, 2)

        def onto(n, _):
            low = dot_last(mix[at].reshape(256, WIDE), pbuf[n, :, :, :, 640:1024].reshape(512, WIDE)).astype(BF)
            xg[at, :, :, pl.ds(pl.multiple_of(512 * n, 512), 512)] = low.reshape(2, 2, 64, 512)
            return 0

        lax.fori_loop(0, 4, onto, 0)
        branch.send_pair(dy)

    outward(2)
    outward(1)
    branch.take_pair(2)
    feed.fourth()
    outward(-1)
    branch.take_pair(1)
    outward(0)
    branch.take_pair(-1)
    keep = [
        net.local(src, dst)
        for src, dst in (
            (rt, rt_out), (ig, ig_out), (co, co_out), (pbuf, p_out), (masks, mask_out), (gains, gain_out),
            (vec, vec_out), (riw, riw_out), (ce, ce_out), (pre, pre_out), (st, st_out), (carry, carry_out),
            (mix, mix_out),
        )
    ]
    branch.relay()
    branch.take_pair(0)
    feed.fifth()
    branch.arrive()
    for k in range(2):

        def close_branch(i, _):
            at = pl.ds(pl.multiple_of(i * 16, 16), 16)
            value = xo[k, at, :].astype(F32) + branch.total(k, at)
            res[k, at, :] = value
            scale = lax.rsqrt(jnp.mean(value * value, axis=-1, keepdims=True) + EPSILON)
            two[k, at, :] = (value * scale * gains[1:2, :]).astype(BF)
            return 0

        lax.fori_loop(0, 4, close_branch, 0, unroll=2)
    branch.drain()
    scaled = GatherColumn(net, me, s2, "two")
    scaled.start(two)
    cots.finish()
    for copy in keep[:3]:
        copy.wait()
    feed.finish()

    def ahead(*dys):
        count = 2 * len(dys)
        first = [turn(me.y, dy) for dy in dys]
        for ref, source, k in ((rt, s2, 0), (ig, s2, 1), (co, ct, 2)):
            left = jnp.concatenate([source[pl.ds(2 * yy, 2)].reshape(256, 2048) for yy in first], axis=0)
            product = dot(left, wf[:, :, :, :, HID * k : HID * (k + 1)].reshape(2048, HID))
            ref[0:count] = product[:, 0:WIDE].reshape(count, 128, WIDE)
            ref[count : 2 * count] = product[:, WIDE:].reshape(count, 128, WIDE)
        for number, yy in enumerate(first):

            def bend(j, _):
                row = lax.div(j, 8)
                here = pl.ds(pl.multiple_of(16 * lax.rem(j, 8), 16), 16)
                rows = pl.ds(pl.multiple_of(256 * yy + 16 * j, 16), 16)
                for half in range(2):
                    lanes = slice(WIDE * half, WIDE * (half + 1))
                    at = count * half + 2 * number + row
                    up, grad = ig[at, here, :], co[at, here, :]
                    act, slant = gelu_and_slope(rt[at, here, :])
                    hid[rows, lanes] = (act * up).astype(BF)
                    gu[rows, lanes] = (grad * (up * slant)).astype(BF)
                    gu[rows, HID + WIDE * half : HID + WIDE * (half + 1)] = (grad * act).astype(BF)
                return 0

            lax.fori_loop(0, 16, bend, 0, unroll=2)

    scaled.whole(0)
    ahead(0)
    scaled.relay()
    scaled.whole(1)
    scaled.whole(-1)
    ahead(1, -1)
    scaled.last()
    scaled.whole(2)
    ahead(2)
    slope = ReduceColumn(net, me, wide, pair, far, side, "slope")

    def inner(*dys):
        first = [turn(me.y, dy) for dy in dys]

        def out(n, _):
            left = [gu[pl.ds(pl.multiple_of(256 * yy, 256), 256), :] for yy in first]
            low = dot_last(jnp.concatenate(left, axis=0), wf[n, :, :, :, 0:FG].reshape(512, FG)).astype(BF)
            at = pl.ds(pl.multiple_of(512 * n, 512), 512)
            for number, yy in enumerate(first):
                xg[pl.ds(2 * yy, 2), :, :, at] = low[256 * number : 256 * (number + 1)].reshape(2, 2, 64, 512)
            return 0

        lax.fori_loop(0, 4, out, 0)
        for dy in dys:
            slope.send_pair(dy)

    def down(n, _):
        low = dot_last(hid[...], wf[n, :, :, :, FG:].reshape(512, HID)).astype(BF)
        pout[:, :, :, pl.ds(pl.multiple_of(512 * n, 512), 512)] = low.reshape(8, 2, 64, 512)
        return 0

    inner(2, 1)
    slope.take_pair(2)
    slope.take_pair(1)
    inner(-1, 0)
    slope.take_pair(-1)
    slope.relay()
    slope.take_pair(0)
    lax.fori_loop(0, 4, down, 0)

    def store(i):
        lanes = pl.ds(0, FG)
        return pltpu.make_async_copy(wf.at[i, :, :, :, lanes], gf_out.at[i], ssend.at[i])

    def columns(i):
        return pl.ds(pl.multiple_of(512 * i, 512), 512)

    def weights_down(i, _):
        flip[...] = jnp.transpose(ct[:, :, :, columns(i)].reshape(1024, 512))
        wf[i, :, :, :, FG:] = dot(flip[...], hid[...]).astype(BF).reshape(4, 2, 64, HID)
        return 0

    def weights(i, _):
        flip[...] = jnp.transpose(s2[:, :, :, columns(i)].reshape(1024, 512))
        for k in range(2):
            lanes = slice(HID * k, HID * (k + 1))
            wf[i, :, :, :, lanes] = dot(flip[...], gu[:, lanes]).astype(BF).reshape(4, 2, 64, HID)
        store(i).start()
        return 0

    under = ReducePlane(net, me, wf.at[:, :, :, :, pl.ds(FG, HID)], far_d, side_d, far2_d, side2_d, "d")

    for i in range(16):

        @pl.when(jnp.logical_not(jnp.logical_and(mine, me.plane == i)))
        def _():
            small_copy(i).wait_send()

    gain2[...] = jnp.zeros_like(gain2)
    for copy in feed.sent:
        copy.wait_send()
    lax.fori_loop(0, 4, weights_down, 0)
    under.start()
    slope.arrive()
    for k in range(2):

        def close(i, _):
            at = pl.ds(pl.multiple_of(i * 16, 16), 16)
            value = res[k, at, :]
            scale = lax.rsqrt(jnp.mean(value * value, axis=-1, keepdims=True) + EPSILON)
            normed = value * scale
            got = slope.total(k, at)
            gain2[0:8, :] = gain2[0:8, :] + (got * normed).reshape(2, 8, 2048).sum(axis=0)
            v = got * gains[1:2, :]
            back = (v - normed * jnp.mean(v * normed, axis=-1, keepdims=True)) * scale
            total = cot[k, at, :].astype(F32) + back
            gres[k, at, :] = total
            gb[k, at, :] = total.astype(BF)
            return 0

        lax.fori_loop(0, 4, close, 0, unroll=2)
    back = GatherColumn(net, me, gb_out, "gb")
    back.start(gb)
    keep += [net.local(gres, gres_out), net.local(gain2, gain2_out), net.local(pout, pout_out), net.local(res, res_out)]
    under.second()
    lax.fori_loop(0, 2, weights, 0)
    back.relay((0,))
    under.third()
    lax.fori_loop(2, 3, weights, 0)
    back.relay((1,))
    lax.fori_loop(3, 4, weights, 0)
    back.last()
    under.fourth()
    under.finish()
    keep.append(net.local(side2_d.at[:, 0], gd_out))
    for i in range(4):
        store(i).wait()
    back.finish()
    for copy in keep[3:]:
        copy.wait()
    net.drain(tokens.sent + branch.sent + feed.sent)


def backward_kernel(
    gb_in, p_in, gf_in, one_in, mask_in, gain_in, vec_in, riw_in, ce_in, pre_in, co_in, rt_in, ig_in, st_in, mix_in,
    carry_in, gres_in, gain2_in, x_in, pout_in, res_in, gd_in,
    ff_out, fd_out, fo_out, fi_out, small_out, gains_out, gx_out, out_out,
    gb, w, gf, masks, gains, vec, riw, ce, pre, co, rt, ig, st, mix, carry, gres, gain2, xo,
    gm, fa, car, edge, z, sgr, srec, ssum, part, pair, far, side, pair2, far2, side2, res, out, gpi, g16, far_f, side_f, far2_f, side2_f,
    far_o, side_o, far2_o, side2_o, far_i, side_i, far2_i, side2_i, ff, fd, fo, fi, grow, gsum, gtot, gall, gx, wacc, halo,
    send, recv, local, ssend, srecv,
):
    me = Place()
    net = Net(send, recv, local)
    loads = {
        name: net.local(a, b)
        for name, a, b in (
            ("gb", gb_in, gb), ("w", p_in, w), ("pre", pre_in, pre), ("st", st_in, st), ("part", pout_in, part), ("mix", mix_in, mix),
            ("rt", rt_in, rt), ("masks", mask_in, masks), ("vec", vec_in, vec), ("gf", gf_in, gf), ("co", co_in, co),
            ("ig", ig_in, ig), ("carry", carry_in, carry), ("riw", riw_in, riw), ("ce", ce_in, ce),
            ("gains", gain_in, gains), ("gres", gres_in, gres), ("gain2", gain2_in, gain2), ("x", x_in, xo), ("res", res_in, res),
        )
    }

    def need(*names):
        for name in names:
            loads[name].wait()

    to_y, to_c, index = me.x, lax.div(me.z, 2), lax.rem(me.z, 2) * 8 + me.c * 4 + me.y
    mine = jnp.logical_and(to_y == me.y, to_c == me.c)

    def small_to(j):
        return me.at(x=me.y, z=2 * me.c + j // 8, c=(j // 4) % 2, y=j % 4)

    def small_from(p):
        return me.at(x=p // 4, z=p % 4, c=to_c, y=to_y)

    barrier = greet(column_peers(me) + [me.flat(d) for d in range(1, 16)])
    for i in range(16):

        @pl.when(jnp.logical_not(jnp.logical_and(mine, me.plane == i)))
        def _():
            pl.semaphore_signal(barrier, inc=1, device_id=small_from(i), device_id_type=MESH)

        @pl.when(jnp.logical_not(jnp.logical_and(mine, index == i)))
        def _():
            pl.semaphore_signal(barrier, inc=1, device_id=small_to(i), device_id_type=MESH)

    pl.semaphore_wait(barrier, 22 + 32 - 2 * mine.astype(jnp.int32))
    feed = ReducePlane(net, me, gf, far_f, side_f, far2_f, side2_f, "f")
    result = ReduceColumn(net, me, part, pair2, far2, side2, "result")
    gpo = w.at[:, :, :, :, pl.ds(640, WIDE)]
    outer = ReducePlane(net, me, gpo, far_o, side_o, far2_o, side2_o, "o")
    inner = ReducePlane(net, me, gpi, far_i, side_i, far2_i, side2_i, "i")
    feed.start(gf_in)

    def share(source, dst, tag):
        for d in range(1, 8):
            y, c = me.column(d)
            src = source.at[c, pl.ds(pl.multiple_of(16 * y, 16), 16)]
            net.go(src, dst.at[me.part], me.at(y=y, c=c), (tag, d))
        src = source.at[me.c, pl.ds(pl.multiple_of(16 * me.y, 16), 16)]
        return net.local(src, dst.at[me.part])

    def collect(dst, tag):
        for d in range(1, 8):
            y = turn(me.y, -(d // 2))
            c = me.c if d % 2 == 0 else 1 - me.c
            net.take(dst.at[2 * y + c], (tag, d), me.sibling())

    own_d = share(gd_in, fd, "fd")
    need("gb", "w")

    def mix_back(i, _):
        at = pl.ds(4 * i, 4)
        grad = dot(gb[at].reshape(512, 2048), w[:, :, :, :, 640:1024].reshape(2048, WIDE))
        gm[at] = grad.reshape(4, 128, WIDE)
        return 0

    lax.fori_loop(0, 2, mix_back, 0)
    need("part")
    for dy in (2, 1, -1, 0):
        result.send_pair(dy)
    need("pre", "st", "rt", "masks", "vec")
    log_scale = log_scale_row(vec)

    def bend_back(row, j, at):
        act, slant = gelu_and_slope(pre[row, at, :])
        grad = jnp.where(lanes_below((STEP, WIDE), CH), gm[row, at, :], 0.0)
        low = grad * st[row, at, :] * slant
        z[row, at, 256:640] = pltpu.roll(low, 64, 1).astype(BF)
        gm[row, at, :] = grad * act
        _, factor, _, _ = decay_parts(rt[row, at, :], log_scale, mask_block(masks, row, j)[:, 0:1])
        fa[row, at, :] = factor

    blocks(0, 8, bend_back)

    def scan(step, held):
        g, m = held
        at = pl.ds(pl.multiple_of((15 - step) * 8, 8), 8)
        f, d = jnp.swapaxes(fa[:, at, :], 0, 1), jnp.swapaxes(gm[:, at, :], 0, 1)
        las, lps = [None] * 8, [None] * 8
        for k in range(7, -1, -1):
            la = d[k] + g
            las[k], lps[k] = la, m
            g, m = f[k] * la, f[k] * m
        gm[:, at, :] = jnp.swapaxes(jnp.stack(las), 0, 1)
        fa[:, at, :] = jnp.swapaxes(jnp.stack(lps), 0, 1)
        return g, m

    g, m = lax.fori_loop(0, 16, scan, (jnp.zeros((8, WIDE), F32), jnp.ones((8, WIDE), F32)), unroll=2)
    car[me.plane, 0] = m
    car[me.plane, 1] = g
    for d in range(1, 16):
        net.go(car.at[me.plane], car.at[me.plane], me.flat(d), ("carry", d))
    need("mix", "gf")

    def weight_out(i, _):
        left = gb[:, :, :, pl.ds(pl.multiple_of(512 * i, 512), 512)].reshape(1024, 512)
        w[i, :, :, :, 640:1024] = dot_first(left, mix[...].reshape(1024, WIDE)).astype(BF).reshape(4, 2, 64, WIDE)
        return 0

    lax.fori_loop(0, 4, weight_out, 0)
    load_one = net.local(one_in, gb)
    feed.second()
    outer.start()
    for dy in (2, 1, -1, 0):
        result.take_pair(dy)
    for d in range(1, 16):
        net.take(car.at[lax.rem(me.plane + 16 - d, 16)], ("carry", d), me.sibling())
    g = jnp.zeros((8, WIDE), F32)
    for k in range(15, 0, -1):
        g = jnp.where(k > me.plane, car[k, 1] + car[k, 0] * g, g)
    edge[...] = g
    wacc[...] = jnp.zeros_like(wacc)
    need("co", "ig", "carry", "riw", "ce")

    def fold(value):
        return value.reshape(STEP // 8, 8, WIDE).sum(axis=0)

    def gate_back(row, j, at):
        resets = mask_block(masks, row, j)[:, 0:1]
        adjoint = gm[row, at, :] + fa[row, at, :] * edge[pl.ds(row, 1), :]
        rate, gate, conv = rt[row, at, :], ig[row, at, :], co[row, at, :]
        a, factor, scale, margin = decay_parts(rate, log_scale, resets)
        before = st[row, pl.ds(pl.multiple_of(jnp.maximum(j * STEP - 8, 0), 8), 8), :]
        edge_row = jnp.where(j == 0, carry[pl.ds(row, 1), :], before[7:8, :])
        top = lax.broadcasted_iota(jnp.int32, (STEP, WIDE), 0) == 0
        previous = jnp.where(top, edge_row, pltpu.roll(st[row, at, :], 1, 0))
        grad_scale = adjoint * gate * conv
        free = jnp.logical_and(margin > FLOOR_VALUE, resets < 0.5)
        grad_log = adjoint * previous * factor - jnp.where(free, grad_scale * (a * a) / scale, 0.0)
        rate_pre = grad_log * log_scale * rate * (1.0 - rate)
        through = adjoint * scale
        gate_pre = through * conv * gate * (1.0 - gate)
        wacc[5] = wacc[5] + fold(rate_pre)
        wacc[6] = wacc[6] + fold(gate_pre)
        wacc[7] = wacc[7] + fold(grad_log * rate)
        gm[row, at, :] = through * gate
        g16[row, at, 0:WIDE] = rate_pre.astype(BF)
        g16[row, at, WIDE:] = gate_pre.astype(BF)

    blocks(0, 8, gate_back)
    result.relay()

    def through_gates(i, _):
        at = pl.ds(4 * i, 4)
        total = gm[at].reshape(512, WIDE)
        total = total + dot_last(g16[at].reshape(512, 2 * WIDE), riw[...])
        gm[at] = total.reshape(4, 128, WIDE)
        return 0

    lax.fori_loop(0, 2, through_gates, 0)

    def conv_back(row, j, at):
        wide = ce[row, pl.ds(pl.multiple_of(j * STEP, STEP), STEP + 16), :].astype(F32)
        valid = mask_block(masks, row, j)
        grad = gm[row, at, :]
        wacc[4] = wacc[4] + fold(grad)
        total = jnp.zeros((STEP + 8, WIDE), F32)
        for k in range(4):
            kept = grad if k == 0 else grad * valid[:, k : k + 1]
            wacc[k] = wacc[k] + fold(kept * wide[16 - k : 16 - k + STEP, :])
            scaled = kept * vec[k : k + 1, :]
            total = total + jnp.concatenate(
                [jnp.zeros((8 - k, WIDE), F32), scaled] + ([jnp.zeros((k, WIDE), F32)] if k else []), axis=0
            )
        fa[row, at, :] = total[8:, :]
        early = total[0:8, :]

        @pl.when(j == 0)
        def _():
            halo[0, row] = early

        @pl.when(j > 0)
        def _():
            last = pl.ds(pl.multiple_of(j * STEP - 8, 8), 8)
            fa[row, last, :] = fa[row, last, :] + early

    blocks(0, 8, conv_back)
    net.go(halo.at[0], halo.at[1], me.flat(-1), "halo")
    feed.third()
    outer.second()

    low = co[...].reshape(1024, WIDE).astype(BF)
    both = dot_first(low, g16[...].reshape(1024, 2 * WIDE))
    grad_rate, grad_gate = both[:, 0:WIDE], both[:, WIDE:]
    rows = lax.broadcasted_iota(jnp.int32, (WIDE, WIDE), 0)
    lanes = lax.broadcasted_iota(jnp.int32, (WIDE, WIDE), 1)
    upper = rows < 160
    held = jnp.where(
        lanes < 160,
        jnp.where(upper, grad_rate, pltpu.roll(grad_rate, WIDE - 160, 1)),
        jnp.where(upper, pltpu.roll(grad_gate, 160, 1), grad_gate),
    )
    vectors = jnp.concatenate([jnp.sum(wacc[k], axis=0, keepdims=True) for k in range(8)], axis=0)
    slope = -8.0 * -jax.nn.sigmoid(-vec[7:8, :])
    line = lax.broadcasted_iota(jnp.int32, (8, WIDE), 0)
    vectors = jnp.where(line == 7, vectors * slope, vectors)
    tall = jnp.transpose(jnp.concatenate([vectors, jnp.zeros((120, WIDE), F32)], axis=0))
    gm[0:3] = held.reshape(3, 128, WIDE)
    late = jnp.where(lanes_below((WIDE, 128), 64), held[:, 256:384], pltpu.roll(tall, 64, 1))
    gm[0:3, :, 256:384] = late.reshape(3, 128, 128)
    flat = gm[0:3].reshape(WIDE, WIDE)
    for j in range(16):
        piece = jnp.concatenate([flat[20 * j : 20 * j + 20, :], jnp.zeros((12, WIDE), F32)], axis=0)
        sgr[j] = piece.astype(BF)

    def small_copy(j):
        return pltpu.make_async_remote_copy(
            src_ref=sgr.at[j],
            dst_ref=srec.at[me.plane],
            send_sem=ssend.at[j],
            recv_sem=srecv.at[me.plane],
            device_id=small_to(j),
            device_id_type=MESH,
        )

    for j in range(16):
        own = jnp.logical_and(mine, index == j)

        @pl.when(jnp.logical_not(own))
        def _():
            small_copy(j).start()

        @pl.when(own)
        def _():
            pltpu.make_async_copy(sgr.at[j], srec.at[me.plane], srecv.at[me.plane]).start()

    net.take(halo.at[1], "halo", me.sibling())

    def conv_in_back(row, j, at):
        grad = fa[row, at, :]
        tail = jnp.where(j == 128 // STEP - 1, halo[1, row], 0.0)
        grad = grad + jnp.concatenate([jnp.zeros((STEP - 8, WIDE), F32), tail], axis=0)
        z[row, at, 0:256] = grad[:, 0:256].astype(BF)
        late = jnp.where(lanes_below((STEP, 128), 64), grad[:, 256:384], z[row, at, 256:384].astype(F32))
        z[row, at, 256:384] = late.astype(BF)

    blocks(0, 8, conv_in_back)
    result.arrive()
    result.drain()
    need("res")
    for k in range(2):

        def close_result(i, _):
            at = pl.ds(pl.multiple_of(i * 16, 16), 16)
            out[k, at, :] = (res[k, at, :] + result.total(k, at)).astype(BF)
            return 0

        lax.fori_loop(0, 4, close_result, 0, unroll=2)
    save_out = net.local(out, out_out)
    entry = ReduceColumn(net, me, part, pair, far, side, "entry")

    def inward(dy):
        at = pl.ds(2 * turn(me.y, dy), 2)

        def out(n, _):
            low = dot_last(z[at].reshape(256, 640), w[n, :, :, :, 0:640].reshape(512, 640)).astype(BF)
            part[at, :, :, pl.ds(pl.multiple_of(512 * n, 512), 512)] = low.reshape(2, 2, 64, 512)
            return 0

        lax.fori_loop(0, 4, out, 0)
        entry.send_pair(dy)

    def weight_in(i, _):
        left = gb[:, :, :, pl.ds(pl.multiple_of(512 * i, 512), 512)].reshape(1024, 512)
        gpi[i] = dot_first(left, z[...].reshape(1024, 640)).astype(BF).reshape(4, 2, 64, 640)
        return 0

    inward(2)
    inward(1)
    entry.take_pair(2)
    inward(-1)
    entry.take_pair(1)
    inward(0)
    entry.take_pair(-1)
    entry.relay()
    entry.take_pair(0)
    load_one.wait()
    lax.fori_loop(0, 4, weight_in, 0)
    inner.start()
    need("gains", "gres", "gain2", "x")
    grow[...] = jnp.zeros_like(grow)
    entry.arrive()
    for k in range(2):

        def close(i, _):
            at = pl.ds(pl.multiple_of(i * 16, 16), 16)
            value = xo[k, at, :].astype(F32)
            scale = lax.rsqrt(jnp.mean(value * value, axis=-1, keepdims=True) + EPSILON)
            normed = value * scale
            got = entry.total(k, at)
            grow[...] = grow[...] + (got * normed).reshape(2, 8, 2048).sum(axis=0)
            v = got * gains[0:1, :]
            back = (v - normed * jnp.mean(v * normed, axis=-1, keepdims=True)) * scale
            gx[k, at, :] = (gres[k, at, :] + back).astype(BF)
            return 0

        lax.fori_loop(0, 4, close, 0, unroll=2)
    keep = [net.local(gx, gx_out), save_out]
    line = lax.broadcasted_iota(jnp.int32, (8, 2048), 0)
    one = jnp.broadcast_to(jnp.sum(grow[...], axis=0, keepdims=True), (8, 2048))
    two = jnp.broadcast_to(jnp.sum(gain2[...], axis=0, keepdims=True), (8, 2048))
    grow[...] = jnp.where(line == 0, one, jnp.where(line == 1, two, 0.0))

    def features(p):
        return pl.ds(pl.multiple_of(128 * p, 128), 128)

    for d in range(1, 16):
        p = lax.rem(me.plane + d, 16)
        net.go(grow.at[:, features(p)], gsum.at[me.plane], me.flat(d), ("gain", d))
    gsum[me.plane] = grow[:, features(me.plane)]

    feed.fourth()
    inner.second()
    outer.third()
    for d in range(1, 16):
        net.take(gsum.at[lax.rem(me.plane + 16 - d, 16)], ("gain", d), me.sibling())
    total = gsum[0]
    for k in range(1, 16):
        total = total + gsum[k]
    gall[me.part] = total
    for d in range(1, 8):
        y, c = me.column(d)
        net.go(gall.at[me.part], gall.at[me.part], me.at(y=y, c=c), ("gain8", d))
    feed.finish()
    own_f = share(side2_f.at[:, 0], ff, "ff")
    inner.third()
    outer.fourth()
    for p in range(16):

        @pl.when(jnp.logical_not(jnp.logical_and(mine, me.plane == p)))
        def _():
            pltpu.make_async_remote_copy(
                src_ref=sgr.at[0],
                dst_ref=srec.at[p],
                send_sem=ssend.at[0],
                recv_sem=srecv.at[p],
                device_id=me.sibling(),
                device_id_type=MESH,
            ).wait_recv()

        @pl.when(jnp.logical_and(mine, me.plane == p))
        def _():
            pltpu.make_async_copy(sgr.at[0], srec.at[p], srecv.at[p]).wait()

    total = srec[0].astype(F32)
    for k in range(1, 16):
        total = total + srec[k].astype(F32)
    ssum[...] = total
    keep.append(net.local(ssum, small_out))
    inner.fourth()
    outer.finish()
    own_o = share(side2_o.at[:, 0], fo, "fo")
    inner.finish()
    own_i = share(side2_i.at[:, 0], fi, "fi")
    own_f.wait()
    collect(ff, "ff")
    keep.append(net.local(ff, ff_out))
    own_d.wait()
    collect(fd, "fd")
    keep.append(net.local(fd, fd_out))
    collect(gall, "gain8")
    total = gall[0]
    for k in range(1, 8):
        total = total + gall[k]
    gtot[...] = total
    keep.append(net.local(gtot, gains_out))
    own_o.wait()
    collect(fo, "fo")
    keep.append(net.local(fo, fo_out))
    own_i.wait()
    collect(fi, "fi")
    keep.append(net.local(fi, fi_out))
    for copy in keep:
        copy.wait()
    net.drain(result.sent)
    for j in range(16):

        @pl.when(jnp.logical_not(jnp.logical_and(mine, index == j)))
        def _():
            small_copy(j).wait_send()


def shaped(shape, kind):
    return jax.ShapeDtypeStruct(shape, kind)


def vmem(shape, kind):
    return pltpu.VMEM(shape, kind)


def call(kernel, args, outs, scratch, name, number, sends, recvs, extra=(), places={}):
    anywhere = pl.BlockSpec(memory_space=pl.ANY)
    return pl.pallas_call(
        kernel,
        out_shape=[shaped(*out) for out in outs],
        in_specs=[places.get(i, anywhere) for i in range(len(args))],
        out_specs=[anywhere] * len(outs),
        scratch_shapes=[vmem(*one) for one in scratch]
        + [pltpu.SemaphoreType.DMA((sends,)), pltpu.SemaphoreType.DMA((recvs,)), pltpu.SemaphoreType.DMA((48,))]
        + list(extra),
        compiler_params=pltpu.CompilerParams(
            collective_id=number, has_side_effects=True, vmem_limit_bytes=62 * 1024 * 1024
        ),
        name=name,
    )(*args)


ROWS = (8, 128, WIDE)
BLOCK = (2, 64, 2048)
ALL = (8, 2, 64, 2048)
SIXTEEN = (pltpu.SemaphoreType.DMA((16,)), pltpu.SemaphoreType.DMA((16,)))


def plane(width):
    return [((2, 2, 2, 64, width), BF), ((2, 2, 4, 64, width), BF), ((2, 2, 32, width), BF), ((2, 2, 64, width), BF)]


def forward(args):
    weights = (4, 4, 2, 64)
    flat = pl.BlockSpec(memory_space=pltpu.SMEM)
    sums = [((4,) + BLOCK, BF), (BLOCK, BF), ((2,) + BLOCK, BF)]
    return call(
        forward_kernel,
        args,
        [
            (weights + (PK,), BF), (ALL, BF), ((8, 2, 64, 128), BF), ((8, 2048), F32), ((8, WIDE), F32),
            ((WIDE, 2 * WIDE), BF), ((8, 144, WIDE), BF),
            (ROWS, F32), (ROWS, F32), (ROWS, F32), (ROWS, F32), (ROWS, F32), ((8, WIDE), F32), (ROWS, BF),
            (weights + (FG,), BF), ((2, 64, HID), BF), (ALL, BF), (ALL, BF), (BLOCK, F32), (BLOCK, F32),
            ((8, 2048), F32),
        ],
        [
            ((16, 2560), BF), ((16, 2560), BF), ((16, 2560), BF), ((8, 16, PK), BF), ((20, 160), BF), ((20, 160), BF),
            ((16, 128), F32), ((SMALL, WIDE), BF), ((2, 64, TOK), BF), ((8, 128), F32), ((8, 8, 128), F32),
            (weights + (PK,), BF), (weights + (FK,), BF), ((8, 2, 64, TOK), BF), ((16, SMALL, WIDE), BF),
            ((WIDE, WIDE), F32), ((WIDE, 2 * WIDE), BF), ((8, WIDE), F32), ((8, 2048), F32), ((8, 144, WIDE), BF),
            (ROWS, F32), (ROWS, F32), (ROWS, F32), (ROWS, F32), (ROWS, F32), (ROWS, F32), (ROWS, BF),
            ((16, 2, 8, WIDE), F32), ((8, WIDE), F32), *sums, (BLOCK, F32), (BLOCK, BF), (BLOCK, BF),
            (ALL, BF), (ALL, BF), (BLOCK, BF), ((1024, HID), BF), ((1024, FG), BF),
            (ALL, BF), (BLOCK, BF), (BLOCK, F32), ((8, 2048), F32), ((512, 1024), BF), *plane(HID),
        ],
        "forward", 1, 320, 320, SIXTEEN, {8: flat},
    )


def backward(args):
    return call(
        backward_kernel,
        args,
        [
            ((8, 16, FG), BF), ((8, 16, HID), BF), ((8, 16, WIDE), BF), ((8, 16, 640), BF), ((SMALL, WIDE), F32), ((8, 128), F32),
            (BLOCK, BF), (BLOCK, BF),
        ],
        [
            (ALL, BF), ((4, 4, 2, 64, PK), BF), ((4, 4, 2, 64, FG), BF), ((8, 2, 64, 128), BF), ((8, 2048), F32),
            ((8, WIDE), F32), ((WIDE, 2 * WIDE), BF), ((8, 144, WIDE), BF), (ROWS, F32), (ROWS, F32), (ROWS, F32),
            (ROWS, F32), (ROWS, F32), (ROWS, BF), ((8, WIDE), F32), (BLOCK, F32), ((8, 2048), F32), (BLOCK, BF),
            (ROWS, F32), (ROWS, F32), ((16, 2, 8, WIDE), F32), ((8, WIDE), F32), ((8, 128, 640), BF),
            ((16, SMALL, WIDE), BF), ((16, SMALL, WIDE), BF), ((SMALL, WIDE), F32),
            (ALL, BF), ((4,) + BLOCK, BF), (BLOCK, BF), ((2,) + BLOCK, BF),
            ((4,) + BLOCK, BF), (BLOCK, BF), ((2,) + BLOCK, BF), (BLOCK, F32), (BLOCK, BF), ((4, 4, 2, 64, 640), BF),
            ((8, 128, 2 * WIDE), BF),
            *plane(FG), *plane(WIDE), *plane(640),
            ((8, 16, FG), BF), ((8, 16, HID), BF), ((8, 16, WIDE), BF), ((8, 16, 640), BF),
            ((8, 2048), F32), ((16, 8, 128), F32), ((8, 128), F32),
            ((8, 8, 128), F32), (BLOCK, BF), ((8, 8, WIDE), F32), ((2, 8, 8, WIDE), F32),
        ],
        "recurrent_backward", 3, 256, 256, SIXTEEN,
    )


def finish_kernel(
    ff_in, fd_in, fo_in, fi_in, small_in, sums_in, gx_in, result_in,
    output, grad_tokens, gain_a, gain_b, conv_w, conv_b, rate_w, input_w, rate_b, input_b, decay,
    out_w, x_w, y_w, gate_w, up_w, down_w,
    ff, fd, fo, fi, small, sums, sems,
):
    me = Place()
    moves = (
        (ff_in, ff), (fd_in, fd), (fo_in, fo), (fi_in, fi), (small_in, small), (sums_in, sums), (gx_in, grad_tokens),
        (result_in, output),
    )
    loads = [pltpu.make_async_copy(a, b, sems.at[i]) for i, (a, b) in enumerate(moves)]
    for copy in loads:
        copy.start()
    for copy in loads:
        copy.wait()
    own = pltpu.roll(sums[...], 128 - (me.c * 64 + me.y * 16), 1)
    gain_a[...] = own[0:1, 0:16]
    gain_b[...] = own[1:2, 0:16]
    rate_w[...] = small[0:20, 0:160]
    input_w[...] = pltpu.roll(small[0:20, :], WIDE - 160, 1)[:, 0:160]
    tall = jnp.concatenate([small[:, 256:384], jnp.zeros((128 - SMALL, 128), F32)], axis=0)
    vectors = jnp.transpose(tall)[64:72, 0:20]
    conv_w[...] = vectors[0:4, :]
    conv_b[...] = vectors[4:5, :]
    rate_b[...] = vectors[5:6, :]
    input_b[...] = vectors[6:7, :]
    decay[...] = vectors[7:8, :]
    for t in range(8):
        at = slice(HID * t, HID * (t + 1))
        gate_w[:, at] = ff[t, :, 0:HID].astype(F32)
        up_w[:, at] = ff[t, :, HID:].astype(F32)
        down_w[:, at] = fd[t].astype(F32)
    zeros = jnp.zeros((16, 256), F32)

    def pair(first, second):
        keep = lanes_below((16, WIDE), CH)
        left = jnp.concatenate([jnp.where(keep, first, 0.0), zeros], axis=1)
        right = jnp.concatenate([jnp.where(keep, second, 0.0), zeros], axis=1)
        return left + pltpu.roll(right, CH, 1)

    for t in range(0, 8, 2):
        at = slice(CH * t, CH * (t + 2))
        out_w[:, at] = pair(fo[t].astype(F32), fo[t + 1].astype(F32))
        x_w[:, at] = pair(fi[t, :, 0:WIDE].astype(F32), fi[t + 1, :, 0:WIDE].astype(F32))
        late = [pltpu.roll(fi[t + i, :, 256:640].astype(F32), WIDE - 64, 1) for i in range(2)]
        y_w[:, at] = pair(*late)


def finish(args):
    held = pl.BlockSpec(memory_space=pltpu.VMEM)
    outs = [
        (BLOCK, BF), (BLOCK, BF), ((1, 16), F32), ((1, 16), F32), ((4, 20), F32), ((1, 20), F32), ((20, 160), F32),
        ((20, 160), F32), ((1, 20), F32), ((1, 20), F32), ((1, 20), F32), ((16, 2560), F32), ((16, 2560), F32),
        ((16, 2560), F32), ((16, 6144), F32), ((16, 6144), F32), ((16, 6144), F32),
    ]
    return pl.pallas_call(
        finish_kernel,
        out_shape=[shaped(*out) for out in outs],
        in_specs=[pl.BlockSpec(memory_space=pl.ANY)] * len(args),
        out_specs=[held] * len(outs),
        scratch_shapes=[
            vmem((8, 16, FG), BF), vmem((8, 16, HID), BF), vmem((8, 16, WIDE), BF), vmem((8, 16, 640), BF),
            vmem((SMALL, WIDE), F32), vmem((8, 128), F32), pltpu.SemaphoreType.DMA((8,)),
        ],
        compiler_params=pltpu.CompilerParams(vmem_limit_bytes=62 * 1024 * 1024),
        name="results",
    )(*args)


def local(
    tokens,
    seg_starts,
    gain_one,
    gain_two,
    conv_weight,
    conv_bias,
    rate_weight,
    input_weight,
    rate_bias,
    input_bias,
    decay_param,
    proj_out,
    proj_x,
    proj_y,
    ffn_gate,
    ffn_up,
    ffn_down,
    cotangent,
):
    vectors = jnp.concatenate([conv_weight, jnp.stack([conv_bias, rate_bias, input_bias, decay_param])], axis=0)
    odds = jnp.concatenate(
        [
            jnp.pad(vectors, ((0, 0), (0, 108))),
            jnp.pad(jnp.stack([gain_one, gain_two]), ((0, 6), (0, 112))),
        ],
        axis=0,
    ).astype(F32)
    (
        p_all, one, mask_all, gains, vec, riw, ce, pre, co, rt, ig, st, carry, mix, gf, gd, gb, pout, res, gres, gain2
    ) = forward((
        proj_x, proj_y, proj_out, ffn_gate, ffn_up, ffn_down, tokens, cotangent, seg_starts, rate_weight, input_weight,
        odds,
    ))
    ff, fd, fo, fi, small, gain_sums, grad_tokens, output = backward((
        gb, p_all, gf, one, mask_all, gains, vec, riw, ce, pre, co, rt, ig, st, mix, carry, gres, gain2, tokens, pout, res,
        gd,
    ))
    results = finish((ff, fd, fo, fi, small, gain_sums, grad_tokens, output))
    return tuple(one.reshape(one.shape[1:]) if i in (2, 3, 5, 8, 9, 10) else one for i, one in enumerate(results))


def solution(mesh):
    both = ("seq", "rows")
    wide, flat = P(both, None), P(both)
    rows = P("rows", "seq", None)
    return jax.shard_map(
        local,
        mesh=mesh,
        in_specs=(
            rows, P("rows", None), flat, flat, P(None, both), flat, wide, wide, flat, flat, flat,
            wide, wide, wide, wide, wide, wide, rows,
        ),
        out_specs=(
            rows, rows, flat, flat, P(None, both), flat, wide, wide, flat, flat, flat,
            wide, wide, wide, wide, wide, wide,
        ),
        check_vma=False,
    )
```
